32 devices in a mesh: groups: 2 (over y), loop: 4 (over z), enc: 2 (over x), rep: 2 (over core).
Axes of the slice: x: 2, y: 2, z: 4, core: 2. Of those that a mesh axis runs over, the one named last changes fastest.
Arguments:
- embeddings: bfloat16 [4096, 768], P(('groups', 'loop', 'rep'), 'enc'), parts along dimension 0, may hold values from -24 to 24
- head_weight: bfloat16 [768, 768], P('enc'), may hold values from -0.21875 to 0.21875
- gp_weights: float32 [4096], P('groups'), parts along dimension 0, may hold values from -24 to 24
- counts: int32 [8], P('groups'), parts along dimension 0, may hold values from 64 to 512, as said below
Outputs:
- embed_grad: bfloat16 [4096, 768], P(('groups', 'loop', 'rep'), 'enc'), parts along dimension 0
- head_grad: float32 [1536, 768], P(('groups', 'enc')), parts along dimension 0
The draws below stay inside these ranges and needn't reach their ends.
There are 2 independent parts, one for each index of `groups`. The reference program is written for one: setup_inputs(seed, part) draws one part's arguments, and reference() takes and returns one part's arrays. A program takes and returns all parts, laid end to end along the dimension named above; an argument that names none is the same for every part. Nothing has to cross between parts.
Inputs may be any that keep to these rules, and one draw needn't show every extreme that they name: `counts`: some block is full and some block holds exactly 64 valid molecules.
All inputs are finite; a program needn't handle non-finite values.
Results may differ from the reference program's by a relative error of at most 0.019.
Values may be sent and summed in bfloat16 or wider, within the bound.
A program may use at most 64 MiB of HBM per device.

```python
import math
import jax
import jax.numpy as jnp
from jax import lax

E = 768
F = 768
BLOCK = 512
BLOCKS = 4
MOLS = 2048


def draw_embeddings(key, part):
    key = jax.random.fold_in(key, 11)
    key_base = jax.random.fold_in(key, 0)
    key_rows = jax.random.fold_in(key, 1)
    key_cols = jax.random.fold_in(key, 3)
    row_scale = jnp.exp(jax.random.uniform(key_rows, (MOLS, 1), jnp.float32, math.log(0.3), math.log(3.0)))
    col_scale = jnp.exp(jax.random.uniform(key_cols, (1, E), jnp.float32, math.log(0.5), math.log(2.0)))
    base = jax.random.normal(key_base, (MOLS, E), jnp.float32)
    base = jnp.clip(base, -4.0, 4.0)
    return (base * row_scale * col_scale).astype(jnp.bfloat16)


def draw_counts(key, part):
    key = jax.random.fold_in(key, 7)
    key_draw, key_full, key_low = jax.random.split(key, 3)
    values = jax.random.randint(key_draw, (BLOCKS,), BLOCK // 8, BLOCK + 1)
    full_at = jax.random.randint(key_full, (), 0, BLOCKS)
    low_at = (full_at + 1 + jax.random.randint(key_low, (), 0, BLOCKS - 1)) % BLOCKS
    values = values.at[full_at].set(BLOCK).at[low_at].set(BLOCK // 8)
    return values.astype(jnp.int32)


def level_of(stream_key, dims, pieces, low, top_value):
    factor_of = 1.0
    for dim, shards_of in pieces:
        steps = jax.random.uniform(jax.random.fold_in(jax.random.fold_in(stream_key, 6), dim), (shards_of,), jnp.float32, low / len(pieces), top_value / len(pieces))
        factor_of = factor_of * jnp.repeat(jnp.exp(steps), dims[dim] // shards_of).reshape((-1,) + (1,) * (len(dims) - 1 - dim))
    return factor_of


def centred(key, shape, width, reach, pieces=(), kind=jnp.bfloat16):
    loudness = level_of(key, shape, pieces, -0.22, 0.18) if pieces else 1.0
    drawn = jax.random.normal(key, shape, jnp.float32) * width * loudness
    return jnp.minimum(jnp.maximum(drawn, -reach), reach).astype(kind)


def setup_inputs(seed: int = 0, part: int = 0) -> dict:
    streams_of = jax.random.split(jax.random.key(seed), 5)
    part_keys = jax.random.split(jax.random.fold_in(streams_of[4], part), 5)
    embeddings = draw_embeddings(jax.random.fold_in(jax.random.fold_in(streams_of[4], part), 71), part)
    head_weight = centred(streams_of[1], (E, F), E ** -0.5, 0.21875, ((0, 2),))
    gp_weights = centred(part_keys[2], (MOLS,), 4.0, 24.0, (), jnp.float32)
    counts = draw_counts(jax.random.fold_in(jax.random.fold_in(streams_of[4], part), 71), part)
    return {"embeddings": embeddings, "head_weight": head_weight, "gp_weights": gp_weights, "counts": counts}


EPSILON = 1e-6


def reference(embeddings, head_weight, gp_weights, counts):
    features = jnp.dot(embeddings, head_weight, preferred_element_type=jnp.float32).astype(jnp.bfloat16)
    wide = features.astype(jnp.float32)
    norms = jnp.sum(wide * wide, axis=1)
    total = embeddings.shape[0]
    rows_all = jnp.arange(total, dtype=jnp.int32)
    block_of = rows_all // BLOCK
    inside = rows_all % BLOCK
    limit = counts[block_of]
    weights = jnp.where(inside < limit, gp_weights, jnp.zeros_like(gp_weights))

    def one_block(block_index):
        start = (block_index * BLOCK).astype(jnp.int32)
        left = lax.dynamic_slice_in_dim(features, start, BLOCK, 0)
        left_norms = lax.dynamic_slice_in_dim(norms, start, BLOCK, 0)
        left_weights = lax.dynamic_slice_in_dim(weights, start, BLOCK, 0)
        scores = jnp.dot(left, features.T, preferred_element_type=jnp.float32)
        denom = left_norms[:, None] + norms[None, :] - scores + EPSILON
        inverse = 1.0 / (denom * denom)
        pair_coef = left_weights[:, None] * weights[None, :]
        pair_weight = (pair_coef * (left_norms[:, None] + norms[None, :]) * inverse).astype(jnp.bfloat16)
        quotient = jnp.sum(pair_coef * 2.0 * scores * inverse, axis=1)
        carried = jnp.dot(pair_weight, features, preferred_element_type=jnp.float32)
        return carried - left.astype(jnp.float32) * quotient[:, None]

    grads = lax.map(one_block, jnp.arange(total // BLOCK, dtype=jnp.int32))
    grad_features = grads.reshape(total, features.shape[1])
    feature_grad = grad_features.astype(jnp.bfloat16)
    embed_grad = jnp.dot(feature_grad, head_weight.T, preferred_element_type=jnp.float32).astype(jnp.bfloat16)
    head_grad = jnp.dot(embeddings.T, feature_grad, preferred_element_type=jnp.float32)
    return embed_grad, head_grad
```

```python
import functools

import jax
import jax.numpy as jnp
from jax import lax
from jax.experimental import pallas as pl
from jax.experimental.pallas import tpu as pltpu
from jax.sharding import PartitionSpec as P

EPSILON = 1e-06
PARTS = 6
CHUNKS = 2
VMEM_BYTES = 60 * 1024 * 1024
MESH_ID = pl.DeviceIdType.MESH


def kernel(
    sizes,
    emb_ref,
    head_ref,
    gp_hbm,
    counts_hbm,
    embed_out,
    head_out,
    gp_ref,
    counts_ref,
    e_all,
    w_all,
    f_own,
    n_own,
    accum,
    quot,
    h_own,
    h_core,
    h_recv,
    h_send,
    h_side,
    h_full,
    e_recv,
    z_send,
    x_send,
    c_send,
    w_send,
    w_recv,
    wy_send,
    wc_send,
    wc_recv,
    in_sem,
    hc_send,
    hc_recv,
    hi_send,
    hi_recv,
    ho_send,
    hf_send,
    hf_recv,
):
    nz, nx, nc, ng = sizes
    z = lax.axis_index("loop")
    x = lax.axis_index("enc")
    c = lax.axis_index("rep")
    g = lax.axis_index("groups")
    other = 1 - c
    rows, cols = e_all.shape[3:]
    piece = rows // CHUNKS
    quarter, feats = w_all.shape[3:]
    half = quarter * ng
    width = feats // PARTS
    has_left = z > 0
    has_right = z < nz - 1

    def x_peer(j):
        return lax.rem(x + 1 + j, nx)

    def remote(src, dst, send, recv, device):
        return pltpu.make_async_remote_copy(
            src_ref=src, dst_ref=dst, send_sem=send, recv_sem=recv,
            device_id=device, device_id_type=MESH_ID,
        )

    def g_peer(i):
        return lax.rem(g + 1 + i, ng)

    def e_copy(b, cc, xx, h, send, device):
        start = h * piece if isinstance(h, int) else pl.multiple_of(h * piece, piece)
        slot = e_all.at[b, cc, xx, pl.ds(start, piece)]
        return remote(slot, slot, send, e_recv.at[b, cc, xx, h], device)

    def z_copy(b, d, h):
        return e_copy(b, c, x, h, z_send.at[d, b, h], {"loop": z + (1 if d == 0 else -1)})

    def x_copy(b, j, h):
        return e_copy(b, c, x, h, x_send.at[j, b, h], {"enc": x_peer(j)})

    def c_copy(b, xx, h):
        return e_copy(b, c, xx, h, c_send.at[b, xx, h], {"rep": other})

    def e_wait(b, cc, xx, h):
        e_copy(b, cc, xx, h, c_send.at[b, xx, h], {"rep": other}).wait_recv()

    def w_copy(xx, gg, send, device):
        slot = w_all.at[xx, c, gg]
        return remote(slot, slot, send, w_recv.at[xx, gg], device)

    def wx_copy(j):
        return w_copy(x, g, w_send.at[j], {"enc": x_peer(j)})

    def wy_copy(j, i):
        return w_copy(x_peer(j), g, wy_send.at[j, i], {"groups": g_peer(i)})

    def w_wait(xx, gg):
        w_copy(xx, gg, w_send.at[0], {"rep": other}).wait_recv()

    def wc_copy(xx, cc, gg):
        slot = w_all.at[xx, cc, gg]
        return remote(slot, slot, wc_send.at[xx, gg], wc_recv.at[xx, gg], {"rep": other})

    own_emb = pltpu.make_async_copy(emb_ref, e_all.at[z, c, x], in_sem.at[0])
    own_emb.start()
    own_head = [
        pltpu.make_async_copy(gp_hbm, gp_ref, in_sem.at[1]),
        pltpu.make_async_copy(counts_hbm, counts_ref, in_sem.at[2]),
    ]
    for copy in own_head:
        copy.start()
    for cc in range(nc):
        for gg in range(ng):
            start = (cc * ng + gg) * quarter
            own_head.append(
                pltpu.make_async_copy(
                    head_ref.at[pl.ds(start, quarter)],
                    w_all.at[x, cc, gg],
                    in_sem.at[3 + cc * ng + gg],
                )
            )
            own_head[-1].start()

    barrier = pltpu.get_barrier_semaphore()

    @pl.when(has_left)
    def _():
        pl.semaphore_signal(barrier, 1, device_id={"loop": z - 1}, device_id_type=MESH_ID)

    @pl.when(has_right)
    def _():
        pl.semaphore_signal(barrier, 1, device_id={"loop": z + 1}, device_id_type=MESH_ID)

    for j in range(nx - 1):
        pl.semaphore_signal(barrier, 1, device_id={"enc": x_peer(j)}, device_id_type=MESH_ID)
    pl.semaphore_signal(barrier, 1, device_id={"rep": other}, device_id_type=MESH_ID)

    for i in range(ng - 1):
        pl.semaphore_signal(barrier, 1, device_id={"groups": g_peer(i)}, device_id_type=MESH_ID)
    accum[...] = jnp.zeros_like(accum)
    quot[...] = jnp.zeros_like(quot)

    pl.semaphore_wait(
        barrier, nx + ng - 1 + has_left.astype(jnp.int32) + has_right.astype(jnp.int32)
    )
    own_emb.wait()
    for copy in own_head:
        copy.wait()
    for j in range(nx - 1):
        wx_copy(j).start()

    def features(b, cc):
        total = jnp.dot(
            e_all[b, cc, 0], w_all[0].reshape(cols, feats),
            preferred_element_type=jnp.float32,
        )
        for xx in range(1, nx):
            total = total + jnp.dot(
                e_all[b, cc, xx], w_all[xx].reshape(cols, feats),
                preferred_element_type=jnp.float32,
            )
        total = total.astype(jnp.bfloat16)
        wide = total.astype(jnp.float32)
        return total, jnp.sum(wide * wide, axis=1, keepdims=True)

    def eye():
        return lax.broadcasted_iota(jnp.int32, (rows, rows), 0) == lax.broadcasted_iota(
            jnp.int32, (rows, rows), 1
        )

    def weight_row(b, cc):
        place = cc * rows + lax.broadcasted_iota(jnp.int32, (1, rows), 1)
        lanes = gp_ref.shape[1]
        split = rows // lanes
        first = (b * nc + cc) * split
        held = [gp_ref[pl.ds(first + i, 1), :] for i in range(split)]
        return jnp.where(place < counts_ref[b], jnp.concatenate(held, axis=1), 0.0)

    def tile(b, cc, feat, norm):
        norm_row = jnp.sum(jnp.where(eye(), norm, 0.0), axis=0, keepdims=True)
        scores = lax.dot_general(
            f_own[...], feat, (((1,), (1,)), ((), ())), preferred_element_type=jnp.float32
        )
        both = n_own[...] + norm_row
        denom = both - scores + EPSILON
        scaled = weight_row(b, cc) * (1.0 / (denom * denom))
        quot[...] += jnp.sum(scaled * scores, axis=1, keepdims=True)
        accum[...] += jnp.dot(
            (both * scaled).astype(jnp.bfloat16), feat, preferred_element_type=jnp.float32
        )

    def at_step(s, d):
        b = z - s if d == 0 else z + s
        return b, jnp.logical_and(jnp.logical_and(b >= 0, b < nz), s >= (1 if d else 0))

    def stage_z(u, d):
        s, h = u // CHUNKS, lax.rem(u, CHUNKS)
        b, valid = at_step(s, d)

        @pl.when(valid)
        def _():
            @pl.when(s > 0)
            def _():
                e_wait(b, c, x, h)

            @pl.when(has_right if d == 0 else has_left)
            def _():
                z_copy(b, d, h).start()

            if d == 0:
                @pl.when(jnp.logical_and(s == 0, has_left))
                def _():
                    z_copy(b, 1, h).start()

            for j in range(nx - 1):
                x_copy(b, j, h).start()
            c_copy(b, x, h).start()

    def stage_x(u, d):
        s, h = u // CHUNKS, lax.rem(u, CHUNKS)
        b, valid = at_step(s, d)

        @pl.when(valid)
        def _():
            for j in range(nx - 1):
                e_wait(b, c, x_peer(j), h)
                c_copy(b, x_peer(j), h).start()

    def stage_w():
        for j in range(nx - 1):
            w_wait(x_peer(j), g)
            for i in range(ng - 1):
                wy_copy(j, i).start()
            wc_copy(x_peer(j), c, g).start()

    def stage_first():
        for j in range(nx - 1):
            for i in range(ng - 1):
                w_wait(x_peer(j), g_peer(i))
                wc_copy(x_peer(j), c, g_peer(i)).start()
        for j in range(nx - 1):
            for gg in range(ng):
                wc_copy(x_peer(j), other, gg).wait_recv()
        feat, norm = features(z, c)
        f_own[...] = feat
        n_own[...] = norm

    def stage_c(s, d):
        b, valid = at_step(s, d)

        @pl.when(valid)
        def _():
            for h in range(CHUNKS):
                for xx in range(nx):
                    e_wait(b, other, xx, h)

            @pl.loop(0, nc)
            def _(cc):
                feat, norm = features(b, cc)
                tile(b, cc, feat, norm)

    steps = nz * CHUNKS
    x_lag = 3
    c_lag = 3 + CHUNKS

    @pl.loop(0, steps + c_lag - 1)
    def _(t):
        @pl.when(t < steps)
        def _():
            stage_z(t, 0)
            stage_z(t, 1)

        @pl.when(t == 2)
        def _():
            stage_w()

        @pl.when(t == c_lag)
        def _():
            stage_first()

        @pl.when(jnp.logical_and(t >= c_lag, lax.rem(t - c_lag + CHUNKS, CHUNKS) == 0))
        def _():
            stage_c((t - c_lag) // CHUNKS, 0)
            stage_c((t - c_lag) // CHUNKS, 1)

        @pl.when(jnp.logical_and(t >= x_lag, t < steps + x_lag))
        def _():
            stage_x(t - x_lag, 0)
            stage_x(t - x_lag, 1)

    own_weight = jnp.sum(jnp.where(eye(), weight_row(z, c), 0.0), axis=1, keepdims=True)
    grad = (
        own_weight * (accum[...] - f_own[...].astype(jnp.float32) * (2.0 * quot[...]))
    ).astype(jnp.bfloat16)
    f_own[...] = grad

    middle = nz // 2
    left_side = z < middle
    inward = jnp.where(left_side, z + 1, z - 1)
    outward = jnp.where(left_side, z - 1, z + 1)
    is_middle = jnp.logical_or(z == middle - 1, z == middle)
    is_outer = jnp.logical_or(z == 0, z == nz - 1)
    spot = is_middle.astype(jnp.int32)

    def hc_copy(k):
        return remote(
            h_core.at[k], h_recv.at[k], hc_send.at[k], hc_recv.at[k], {"rep": other}
        )

    def hi_copy(k):
        return remote(
            h_send.at[k], h_side.at[spot, k], hi_send.at[k], hi_recv.at[spot, k],
            {"loop": inward},
        )

    def hi_wait(place, k):
        remote(
            h_send.at[k], h_side.at[place, k], hi_send.at[k], hi_recv.at[place, k],
            {"loop": inward},
        ).wait_recv()

    def ho_copy(k):
        slot = h_full.at[c, k]
        return remote(slot, slot, ho_send.at[k], hf_recv.at[c, k], {"loop": outward})

    def hf_copy(k):
        slot = h_full.at[c, k]
        return remote(slot, slot, hf_send.at[k], hf_recv.at[c, k], {"rep": other})

    for k in range(PARTS):
        part = lax.dot_general(
            e_all[z, c, x], f_own[:, k * width : (k + 1) * width], (((0,), (0,)), ((), ())),
            preferred_element_type=jnp.float32,
        )
        h_full_part = part.reshape(nc, half, width)

        @pl.when(c == 0)
        def _():
            h_own[k] = h_full_part[0]
            h_core[k] = h_full_part[1].astype(jnp.bfloat16)

        @pl.when(c == 1)
        def _():
            h_own[k] = h_full_part[1]
            h_core[k] = h_full_part[0].astype(jnp.bfloat16)

        hc_copy(k).start()

    for k in range(PARTS):
        hc_copy(k).wait_recv()
        h_own[k] = h_own[k] + h_recv[k].astype(jnp.float32)

        @pl.when(is_outer)
        def _():
            h_send[k] = h_own[k].astype(jnp.bfloat16)
            hi_copy(k).start()

    for k in range(PARTS):
        @pl.when(jnp.logical_not(is_outer))
        def _():
            hi_wait(0, k)
            h_send[k] = (h_own[k] + h_side[0, k].astype(jnp.float32)).astype(jnp.bfloat16)
            hi_copy(k).start()

    embed_out[...] = lax.dot_general(
        f_own[...], w_all[x].reshape(cols, feats), (((1,), (1,)), ((), ())), preferred_element_type=jnp.float32
    ).astype(jnp.bfloat16)

    for k in range(PARTS):
        @pl.when(is_middle)
        def _():
            hi_wait(1, k)
            h_full[c, k] = (
                h_send[k].astype(jnp.float32) + h_side[1, k].astype(jnp.float32)
            ).astype(jnp.bfloat16)

        @pl.when(jnp.logical_not(is_middle))
        def _():
            ho_copy(k).wait_recv()

        @pl.when(jnp.logical_not(is_outer))
        def _():
            ho_copy(k).start()

        hf_copy(k).start()

    for k in range(PARTS):
        slot = h_full.at[other, k]
        remote(slot, slot, hf_send.at[k], hf_recv.at[other, k], {"rep": other}).wait_recv()
    head_out[...] = h_full[...]

    @pl.loop(0, nz)
    def _(b):
        for h in range(CHUNKS):
            @pl.when(jnp.logical_and(b <= z, has_right))
            def _():
                z_copy(b, 0, h).wait_send()

            @pl.when(jnp.logical_and(b >= z, has_left))
            def _():
                z_copy(b, 1, h).wait_send()

            for j in range(nx - 1):
                x_copy(b, j, h).wait_send()
            for xx in range(nx):
                c_copy(b, xx, h).wait_send()

    for j in range(nx - 1):
        wx_copy(j).wait_send()
        for i in range(ng - 1):
            wy_copy(j, i).wait_send()
        for gg in range(ng):
            wc_copy(x_peer(j), c, gg).wait_send()
    for k in range(PARTS):
        hc_copy(k).wait_send()
        hi_copy(k).wait_send()
        hf_copy(k).wait_send()

        @pl.when(jnp.logical_not(is_outer))
        def _():
            ho_copy(k).wait_send()


def finish(embed_ref, head_ref, embed_out, head_out):
    cores, parts, half, width = head_ref.shape
    embed_out[...] = embed_ref[...]
    for cc in range(cores):
        for k in range(parts):
            head_out[cc * half : (cc + 1) * half, k * width : (k + 1) * width] = head_ref[
                cc, k
            ].astype(jnp.float32)


def ring_body(embeddings, head_weight, gp_weights, counts):
    nz, nx, nc, ng = (lax.axis_size(name) for name in ("loop", "enc", "rep", "groups"))
    rows, cols = embeddings.shape
    feats = head_weight.shape[1]
    half, width = cols // nc, feats // PARTS
    if half % (16 * ng):
        raise ValueError("head rows")
    gp_rows = gp_weights.reshape(-1, 128)
    vmem = pl.BlockSpec(memory_space=pltpu.VMEM)
    hbm = pl.BlockSpec(memory_space=pltpu.HBM)
    dma = pltpu.SemaphoreType.DMA
    embed_grad, head_sum = pl.pallas_call(
        functools.partial(kernel, (nz, nx, nc, ng)),
        out_shape=(
            jax.ShapeDtypeStruct((rows, cols), jnp.bfloat16),
            jax.ShapeDtypeStruct((nc, PARTS, half, width), jnp.bfloat16),
        ),
        in_specs=[hbm, hbm, hbm, hbm],
        out_specs=(vmem, vmem),
        scratch_shapes=[
            pltpu.VMEM(gp_rows.shape, jnp.float32),
            pltpu.SMEM(counts.shape, jnp.int32),
            pltpu.VMEM((nz, nc, nx, rows, cols), jnp.bfloat16),
            pltpu.VMEM((nx, nc, ng, half // ng, feats), jnp.bfloat16),
            pltpu.VMEM((rows, feats), jnp.bfloat16),
            pltpu.VMEM((rows, 1), jnp.float32),
            pltpu.VMEM((rows, feats), jnp.float32),
            pltpu.VMEM((rows, 1), jnp.float32),
            pltpu.VMEM((PARTS, half, width), jnp.float32),
            pltpu.VMEM((PARTS, half, width), jnp.bfloat16),
            pltpu.VMEM((PARTS, half, width), jnp.bfloat16),
            pltpu.VMEM((PARTS, half, width), jnp.bfloat16),
            pltpu.VMEM((2, PARTS, half, width), jnp.bfloat16),
            pltpu.VMEM((nc, PARTS, half, width), jnp.bfloat16),
            dma((nz, nc, nx, CHUNKS)),
            dma((2, nz, CHUNKS)),
            dma((nx - 1, nz, CHUNKS)),
            dma((nz, nx, CHUNKS)),
            dma((nx - 1,)),
            dma((nx, ng)),
            dma((nx - 1, max(ng - 1, 1))),
            dma((nx, ng)),
            dma((nx, ng)),
            dma((3 + nc * ng,)),
            dma((PARTS,)),
            dma((PARTS,)),
            dma((PARTS,)),
            dma((2, PARTS)),
            dma((PARTS,)),
            dma((PARTS,)),
            dma((nc, PARTS)),
        ],
        compiler_params=pltpu.CompilerParams(
            collective_id=0, has_side_effects=True, vmem_limit_bytes=VMEM_BYTES
        ),
    )(embeddings, head_weight, gp_rows, counts)
    return pl.pallas_call(
        finish,
        out_shape=(
            jax.ShapeDtypeStruct((rows, cols), jnp.bfloat16),
            jax.ShapeDtypeStruct((cols, feats), jnp.float32),
        ),
        in_specs=[vmem, vmem],
        out_specs=(vmem, vmem),
        compiler_params=pltpu.CompilerParams(vmem_limit_bytes=VMEM_BYTES),
    )(embed_grad, head_sum)


LINE = 4
PIECES = 2
COLUMNS = 3


def line_kernel(
    emb_ref,
    head_ref,
    gp_hbm,
    counts_hbm,
    embed_out,
    own_out,
    peer_out,
    gp_ref,
    counts_ref,
    e_all,
    w_all,
    f_all,
    n_row,
    n_col,
    w_row,
    accum,
    quot,
    grads,
    in_sem,
    e_send,
    e_recv,
    w_send,
    w_recv,
    f_send,
    f_recv,
    n_send,
    n_recv,
    h_send,
    h_recv,
):
    nz, nc = LINE, 2
    z = lax.axis_index("loop")
    x = lax.axis_index("enc")
    c = lax.axis_index("rep")
    g = lax.axis_index("groups")
    rows, cols = e_all.shape[2:]
    piece = rows // PIECES
    quarter, feats = w_all.shape[3:]
    block = nc * rows
    lanes = gp_ref.shape[1]
    inward = jnp.where(z < nz // 2, 1, -1)
    is_end = jnp.logical_or(z == 0, z == nz - 1)
    is_mid = jnp.logical_not(is_end)
    near = z + inward
    outer = z - inward
    second = z + 2 * inward
    third = z + 3 * inward
    x_dev, c_dev, g_dev = {"enc": 1 - x}, {"rep": 1 - c}, {"groups": 1 - g}

    def remote(src, dst, send, recv, device):
        return pltpu.make_async_remote_copy(
            src_ref=src, dst_ref=dst, send_sem=send, recv_sem=recv,
            device_id=device, device_id_type=MESH_ID,
        )

    def e_copy(side, b, h, kind, device):
        slot = e_all.at[side, b, pl.ds(h * piece, piece)]
        return remote(slot, slot, e_send.at[kind, h], e_recv.at[side, b, h], device)

    def e_wait(side, b, h):
        e_copy(side, b, h, 0, x_dev).wait_recv()

    def w_copy(cc, gg, kind, device):
        slot = w_all.at[1 - x, cc, gg]
        return remote(slot, slot, w_send.at[kind], w_recv.at[cc, gg], device)

    def w_first():
        slot = w_all.at[x, c, g]
        return remote(slot, slot, w_send.at[0], w_recv.at[c, g], x_dev)

    def f_copy(b, cc):
        slot = f_all.at[b, cc]
        return remote(slot, slot, f_send.at[b], f_recv.at[b], c_dev)

    def n_copy(b, cc):
        slot = n_row.at[b, cc]
        return remote(slot, slot, n_send.at[b], n_recv.at[b], c_dev)

    own_emb = pltpu.make_async_copy(emb_ref, e_all.at[x, z], in_sem.at[0])
    own_emb.start()
    loads = []
    for cc in range(nc):
        for gg in range(2):
            loads.append(
                pltpu.make_async_copy(
                    head_ref.at[pl.ds((cc * 2 + gg) * quarter, quarter)],
                    w_all.at[x, cc, gg],
                    in_sem.at[3 + cc * 2 + gg],
                )
            )
    loads.append(pltpu.make_async_copy(gp_hbm, gp_ref, in_sem.at[1]))
    loads.append(pltpu.make_async_copy(counts_hbm, counts_ref, in_sem.at[2]))
    for copy in loads:
        copy.start()

    barrier = pltpu.get_barrier_semaphore()

    def greet(device):
        pl.semaphore_signal(barrier, 1, device_id=device, device_id_type=MESH_ID)

    greet(x_dev)
    greet(c_dev)
    greet(g_dev)
    greet({"loop": near})
    greet({"loop": second})

    @pl.when(is_mid)
    def _():
        greet({"loop": outer})

    own_emb.wait()
    for copy in loads:
        copy.wait()
    pl.semaphore_wait(barrier, 5 + is_mid.astype(jnp.int32))

    w_first().start()
    for h in range(PIECES):
        e_copy(x, z, h, 0, x_dev).start()
        e_copy(x, z, h, 1, {"loop": second}).start()
        e_copy(x, z, h, 2, {"loop": near}).start()

        @pl.when(is_mid)
        def _():
            e_copy(x, z, h, 3, {"loop": outer}).start()

    accum[...] = jnp.zeros_like(accum)
    quot[...] = jnp.zeros_like(quot)
    inside = lax.broadcasted_iota(jnp.int32, (1, lanes), 1)
    for b in range(nz):
        for k in range(block // lanes):
            held = gp_ref[pl.ds(b * (block // lanes) + k, 1), :]
            w_row[b, :, k * lanes : (k + 1) * lanes] = jnp.where(
                inside + k * lanes < counts_ref[b], held, 0.0
            )

    w_copy(c, g, 0, x_dev).wait_recv()
    w_copy(c, g, 1, g_dev).start()
    w_copy(c, g, 2, c_dev).start()
    for h in range(PIECES):
        @pl.when(is_mid)
        def _():
            e_wait(x, second, h)
            e_copy(x, second, h, 4, {"loop": outer}).start()
            e_copy(x, second, h, 5, x_dev).start()

        e_wait(1 - x, z, h)
        e_copy(1 - x, z, h, 6, {"loop": near}).start()

        @pl.when(is_mid)
        def _():
            e_copy(1 - x, z, h, 7, {"loop": outer}).start()

        @pl.when(is_end)
        def _():
            e_wait(x, second, h)
            e_copy(x, second, h, 5, x_dev).start()

    w_copy(c, 1 - g, 1, g_dev).wait_recv()
    w_copy(c, 1 - g, 3, c_dev).start()
    w_copy(1 - c, g, 2, c_dev).wait_recv()
    w_copy(1 - c, 1 - g, 3, c_dev).wait_recv()

    def features(b):
        total = jnp.dot(
            e_all[0, b], w_all[0].reshape(cols, feats), preferred_element_type=jnp.float32
        ) + jnp.dot(
            e_all[1, b], w_all[1].reshape(cols, feats), preferred_element_type=jnp.float32
        )
        held = total.astype(jnp.bfloat16)
        f_all[b, c] = held
        f_copy(b, c).start()
        wide = held.astype(jnp.float32)
        norm = jnp.sum(wide * wide, axis=1, keepdims=True)
        n_col[b] = jnp.broadcast_to(norm, (rows, lanes))
        eye = lax.broadcasted_iota(jnp.int32, (rows, rows), 0) == lax.broadcasted_iota(
            jnp.int32, (rows, rows), 1
        )
        n_row[b, c] = jnp.sum(jnp.where(eye, norm, 0.0), axis=0, keepdims=True)
        n_copy(b, c).start()

    def scores_of(i, j):
        return lax.dot_general(
            f_all[i, c], f_all[j].reshape(block, feats), (((1,), (1,)), ((), ())),
            preferred_element_type=jnp.float32,
        )

    def pairs(i, j, scores):
        spread = block // lanes
        left = jnp.concatenate([n_col[i]] * spread, axis=1)
        right = jnp.concatenate([n_row[j, cc] for cc in range(nc)], axis=1)
        both = left + right
        denom = (both - scores) + EPSILON
        scaled = w_row[j] * (1.0 / (denom * denom))
        part = scaled * scores
        total = part[:, :lanes]
        for k in range(1, spread):
            total = total + part[:, k * lanes : (k + 1) * lanes]
        quot[i, j // 2] += total
        return (both * scaled).astype(jnp.bfloat16)

    def tiles(todo):
        scores = scores_of(*todo[0])
        for k, (i, j) in enumerate(todo):
            following = scores_of(*todo[k + 1]) if k + 1 < len(todo) else None
            weight = pairs(i, j, scores)
            accum[i, j // 2] += jnp.dot(
                weight, f_all[j].reshape(block, feats), preferred_element_type=jnp.float32
            )
            scores = following

    order = [
        z,
        jnp.where(is_end, second, outer),
        near,
        jnp.where(is_end, third, second),
    ]
    for s in range(nz):
        b = order[s]
        if s > 0:
            for h in range(PIECES):
                for side in range(2):
                    seen_end = jnp.logical_and(side == x, jnp.logical_or(b == second, b == third))
                    seen_mid = jnp.logical_and(side == x, b == second)
                    seen = jnp.where(is_end, seen_end, seen_mid)

                    @pl.when(jnp.logical_not(seen))
                    def _():
                        e_wait(side, b, h)

        features(b)
        if s > 0:
            tiles([(b, order[j]) for j in range(s)])
        f_copy(b, 1 - c).wait_recv()
        n_copy(b, 1 - c).wait_recv()
        tiles([(order[i], b) for i in range(s + 1)])
        if s == 0:
            @pl.when(is_end)
            def _():
                for h in range(PIECES):
                    e_wait(x, third, h)
                    e_copy(x, third, h, 4, x_dev).start()

    for b in range(nz):
        quotient = 2.0 * jnp.sum(quot[b, 0] + quot[b, 1], axis=1, keepdims=True)
        spread = block // nc // lanes
        row = jnp.concatenate(
            [
                jnp.where(c == 0, w_row[b, :, k * lanes : (k + 1) * lanes],
                          w_row[b, :, rows + k * lanes : rows + (k + 1) * lanes])
                for k in range(spread)
            ],
            axis=1,
        )
        eye = lax.broadcasted_iota(jnp.int32, (rows, rows), 0) == lax.broadcasted_iota(
            jnp.int32, (rows, rows), 1
        )
        own_weight = jnp.sum(jnp.where(eye, row, 0.0), axis=1, keepdims=True)
        carried = accum[b, 0] + accum[b, 1]
        grads[b] = (
            own_weight * (carried - f_all[b, c].astype(jnp.float32) * quotient)
        ).astype(jnp.bfloat16)

    width = feats // COLUMNS

    def h_copy(k):
        return remote(
            own_out.at[k], peer_out.at[k], h_send.at[k], h_recv.at[k], c_dev
        )

    for k in range(COLUMNS):
        own_out[k] = lax.dot_general(
            e_all[x].reshape(nz * rows, cols),
            grads[:, :, k * width : (k + 1) * width].reshape(nz * rows, width),
            (((0,), (0,)), ((), ())),
            preferred_element_type=jnp.float32,
        ).astype(jnp.bfloat16)
        h_copy(k).start()

    embed_out[...] = lax.dot_general(
        grads[z], w_all[x].reshape(cols, feats), (((1,), (1,)), ((), ())),
        preferred_element_type=jnp.float32,
    ).astype(jnp.bfloat16)

    w_first().wait_send()
    for kind, device in ((1, g_dev), (2, c_dev), (3, c_dev)):
        w_copy(c, g, kind, device).wait_send()
    for b in range(nz):
        f_copy(b, c).wait_send()
        n_copy(b, c).wait_send()
    for h in range(PIECES):
        for kind in (0, 1, 2, 4, 5, 6):
            e_copy(x, z, h, kind, x_dev).wait_send()

        @pl.when(is_mid)
        def _():
            for kind in (3, 7):
                e_copy(x, z, h, kind, x_dev).wait_send()

    for k in range(COLUMNS):
        h_copy(k).wait()


def line_finish(embed_ref, own_ref, peer_ref, embed_out, head_out):
    parts, _, width = own_ref.shape
    embed_out[...] = embed_ref[...]
    for k in range(parts):
        head_out[:, k * width : (k + 1) * width] = own_ref[k].astype(
            jnp.float32
        ) + peer_ref[k].astype(jnp.float32)


def line_body(embeddings, head_weight, gp_weights, counts):
    nz, nc, nx, ng = LINE, 2, 2, 2
    rows, cols = embeddings.shape
    feats = head_weight.shape[1]
    quarter, width = cols // (nc * ng), feats // COLUMNS
    lanes = 128
    gp_rows = gp_weights.reshape(-1, lanes)
    vmem = pl.BlockSpec(memory_space=pltpu.VMEM)
    hbm = pl.BlockSpec(memory_space=pltpu.HBM)
    dma = pltpu.SemaphoreType.DMA
    part = jax.ShapeDtypeStruct((COLUMNS, cols, width), jnp.bfloat16)
    embed_grad, own, peer = pl.pallas_call(
        line_kernel,
        out_shape=(jax.ShapeDtypeStruct((rows, cols), jnp.bfloat16), part, part),
        in_specs=[hbm, hbm, hbm, hbm],
        out_specs=(vmem, vmem, vmem),
        scratch_shapes=[
            pltpu.VMEM(gp_rows.shape, jnp.float32),
            pltpu.SMEM(counts.shape, jnp.int32),
            pltpu.VMEM((nx, nz, rows, cols), jnp.bfloat16),
            pltpu.VMEM((nx, nc, ng, quarter, feats), jnp.bfloat16),
            pltpu.VMEM((nz, nc, rows, feats), jnp.bfloat16),
            pltpu.VMEM((nz, nc, 1, rows), jnp.float32),
            pltpu.VMEM((nz, rows, lanes), jnp.float32),
            pltpu.VMEM((nz, 1, nc * rows), jnp.float32),
            pltpu.VMEM((nz, nz // 2, rows, feats), jnp.float32),
            pltpu.VMEM((nz, nz // 2, rows, lanes), jnp.float32),
            pltpu.VMEM((nz, rows, feats), jnp.bfloat16),
            dma((3 + nc * ng,)),
            dma((8, PIECES)),
            dma((nx, nz, PIECES)),
            dma((4,)),
            dma((nc, ng)),
            dma((nz,)),
            dma((nz,)),
            dma((nz,)),
            dma((nz,)),
            dma((COLUMNS,)),
            dma((COLUMNS,)),
        ],
        compiler_params=pltpu.CompilerParams(
            collective_id=0, has_side_effects=True, vmem_limit_bytes=VMEM_BYTES
        ),
    )(embeddings, head_weight, gp_rows, counts)
    return pl.pallas_call(
        line_finish,
        out_shape=(
            jax.ShapeDtypeStruct((rows, cols), jnp.bfloat16),
            jax.ShapeDtypeStruct((cols, feats), jnp.float32),
        ),
        in_specs=[vmem, vmem, vmem],
        out_specs=(vmem, vmem),
        compiler_params=pltpu.CompilerParams(vmem_limit_bytes=VMEM_BYTES),
    )(embed_grad, own, peer)


def body(*args):
    sizes = tuple(lax.axis_size(name) for name in ("loop", "enc", "rep", "groups"))
    return line_body(*args) if sizes == (LINE, 2, 2, 2) else ring_body(*args)


def solution(mesh):
    placed = (P(("groups", "loop", "rep"), "enc"), P("enc", None), P("groups"), P("groups"))
    return jax.shard_map(
        body,
        mesh=mesh,
        in_specs=placed,
        out_specs=(P(("groups", "loop", "rep"), "enc"), P(("groups", "enc"), None)),
        check_vma=False,
    )
```

```python
import functools

import jax
import jax.numpy as jnp
from jax import lax
from jax.experimental import pallas as pl
from jax.experimental.pallas import tpu as pltpu
from jax.sharding import PartitionSpec as P

EPSILON = 1e-06
PARTS = 6
CHUNKS = 2
VMEM_BYTES = 60 * 1024 * 1024
MESH_ID = pl.DeviceIdType.MESH


def kernel(
    sizes,
    emb_ref,
    head_ref,
    gp_hbm,
    counts_hbm,
    embed_out,
    head_out,
    gp_ref,
    counts_ref,
    e_all,
    w_all,
    f_own,
    n_own,
    accum,
    quot,
    h_own,
    h_core,
    h_recv,
    h_send,
    h_side,
    h_full,
    e_recv,
    z_send,
    x_send,
    c_send,
    w_send,
    w_recv,
    wy_send,
    wc_send,
    wc_recv,
    in_sem,
    hc_send,
    hc_recv,
    hi_send,
    hi_recv,
    ho_send,
    hf_send,
    hf_recv,
):
    nz, nx, nc, ng = sizes
    z = lax.axis_index("loop")
    x = lax.axis_index("enc")
    c = lax.axis_index("rep")
    g = lax.axis_index("groups")
    other = 1 - c
    rows, cols = e_all.shape[3:]
    piece = rows // CHUNKS
    quarter, feats = w_all.shape[3:]
    half = quarter * ng
    width = feats // PARTS
    has_left = z > 0
    has_right = z < nz - 1

    def x_peer(j):
        return lax.rem(x + 1 + j, nx)

    def remote(src, dst, send, recv, device):
        return pltpu.make_async_remote_copy(
            src_ref=src, dst_ref=dst, send_sem=send, recv_sem=recv,
            device_id=device, device_id_type=MESH_ID,
        )

    def g_peer(i):
        return lax.rem(g + 1 + i, ng)

    def e_copy(b, cc, xx, h, send, device):
        start = h * piece if isinstance(h, int) else pl.multiple_of(h * piece, piece)
        slot = e_all.at[b, cc, xx, pl.ds(start, piece)]
        return remote(slot, slot, send, e_recv.at[b, cc, xx, h], device)

    def z_copy(b, d, h):
        return e_copy(b, c, x, h, z_send.at[d, b, h], {"loop": z + (1 if d == 0 else -1)})

    def x_copy(b, j, h):
        return e_copy(b, c, x, h, x_send.at[j, b, h], {"enc": x_peer(j)})

    def c_copy(b, xx, h):
        return e_copy(b, c, xx, h, c_send.at[b, xx, h], {"rep": other})

    def e_wait(b, cc, xx, h):
        e_copy(b, cc, xx, h, c_send.at[b, xx, h], {"rep": other}).wait_recv()

    def w_copy(xx, gg, send, device):
        slot = w_all.at[xx, c, gg]
        return remote(slot, slot, send, w_recv.at[xx, gg], device)

    def wx_copy(j):
        return w_copy(x, g, w_send.at[j], {"enc": x_peer(j)})

    def wy_copy(j, i):
        return w_copy(x_peer(j), g, wy_send.at[j, i], {"groups": g_peer(i)})

    def w_wait(xx, gg):
        w_copy(xx, gg, w_send.at[0], {"rep": other}).wait_recv()

    def wc_copy(xx, cc, gg):
        slot = w_all.at[xx, cc, gg]
        return remote(slot, slot, wc_send.at[xx, gg], wc_recv.at[xx, gg], {"rep": other})

    own_emb = pltpu.make_async_copy(emb_ref, e_all.at[z, c, x], in_sem.at[0])
    own_emb.start()
    own_head = [
        pltpu.make_async_copy(gp_hbm, gp_ref, in_sem.at[1]),
        pltpu.make_async_copy(counts_hbm, counts_ref, in_sem.at[2]),
    ]
    for copy in own_head:
        copy.start()
    for cc in range(nc):
        for gg in range(ng):
            start = (cc * ng + gg) * quarter
            own_head.append(
                pltpu.make_async_copy(
                    head_ref.at[pl.ds(start, quarter)],
                    w_all.at[x, cc, gg],
                    in_sem.at[3 + cc * ng + gg],
                )
            )
            own_head[-1].start()

    barrier = pltpu.get_barrier_semaphore()

    @pl.when(has_left)
    def _():
        pl.semaphore_signal(barrier, 1, device_id={"loop": z - 1}, device_id_type=MESH_ID)

    @pl.when(has_right)
    def _():
        pl.semaphore_signal(barrier, 1, device_id={"loop": z + 1}, device_id_type=MESH_ID)

    for j in range(nx - 1):
        pl.semaphore_signal(barrier, 1, device_id={"enc": x_peer(j)}, device_id_type=MESH_ID)
    pl.semaphore_signal(barrier, 1, device_id={"rep": other}, device_id_type=MESH_ID)

    for i in range(ng - 1):
        pl.semaphore_signal(barrier, 1, device_id={"groups": g_peer(i)}, device_id_type=MESH_ID)
    accum[...] = jnp.zeros_like(accum)
    quot[...] = jnp.zeros_like(quot)

    pl.semaphore_wait(
        barrier, nx + ng - 1 + has_left.astype(jnp.int32) + has_right.astype(jnp.int32)
    )
    own_emb.wait()
    for copy in own_head:
        copy.wait()
    for j in range(nx - 1):
        wx_copy(j).start()

    def features(b, cc):
        total = jnp.dot(
            e_all[b, cc, 0], w_all[0].reshape(cols, feats),
            preferred_element_type=jnp.float32,
        )
        for xx in range(1, nx):
            total = total + jnp.dot(
                e_all[b, cc, xx], w_all[xx].reshape(cols, feats),
                preferred_element_type=jnp.float32,
            )
        total = total.astype(jnp.bfloat16)
        wide = total.astype(jnp.float32)
        return total, jnp.sum(wide * wide, axis=1, keepdims=True)

    def eye():
        return lax.broadcasted_iota(jnp.int32, (rows, rows), 0) == lax.broadcasted_iota(
            jnp.int32, (rows, rows), 1
        )

    def weight_row(b, cc):
        place = cc * rows + lax.broadcasted_iota(jnp.int32, (1, rows), 1)
        lanes = gp_ref.shape[1]
        split = rows // lanes
        first = (b * nc + cc) * split
        held = [gp_ref[pl.ds(first + i, 1), :] for i in range(split)]
        return jnp.where(place < counts_ref[b], jnp.concatenate(held, axis=1), 0.0)

    def tile(b, cc, feat, norm):
        norm_row = jnp.sum(jnp.where(eye(), norm, 0.0), axis=0, keepdims=True)
        scores = lax.dot_general(
            f_own[...], feat, (((1,), (1,)), ((), ())), preferred_element_type=jnp.float32
        )
        both = n_own[...] + norm_row
        denom = both - scores + EPSILON
        scaled = weight_row(b, cc) * (1.0 / (denom * denom))
        quot[...] += jnp.sum(scaled * scores, axis=1, keepdims=True)
        accum[...] += jnp.dot(
            (both * scaled).astype(jnp.bfloat16), feat, preferred_element_type=jnp.float32
        )

    def at_step(s, d):
        b = z - s if d == 0 else z + s
        return b, jnp.logical_and(jnp.logical_and(b >= 0, b < nz), s >= (1 if d else 0))

    def stage_z(u, d):
        s, h = u // CHUNKS, lax.rem(u, CHUNKS)
        b, valid = at_step(s, d)

        @pl.when(valid)
        def _():
            @pl.when(s > 0)
            def _():
                e_wait(b, c, x, h)

            @pl.when(has_right if d == 0 else has_left)
            def _():
                z_copy(b, d, h).start()

            if d == 0:
                @pl.when(jnp.logical_and(s == 0, has_left))
                def _():
                    z_copy(b, 1, h).start()

            for j in range(nx - 1):
                x_copy(b, j, h).start()
            c_copy(b, x, h).start()

    def stage_x(u, d):
        s, h = u // CHUNKS, lax.rem(u, CHUNKS)
        b, valid = at_step(s, d)

        @pl.when(valid)
        def _():
            for j in range(nx - 1):
                e_wait(b, c, x_peer(j), h)
                c_copy(b, x_peer(j), h).start()

    def stage_w():
        for j in range(nx - 1):
            w_wait(x_peer(j), g)
            for i in range(ng - 1):
                wy_copy(j, i).start()
            wc_copy(x_peer(j), c, g).start()

    def stage_first():
        for j in range(nx - 1):
            for i in range(ng - 1):
                w_wait(x_peer(j), g_peer(i))
                wc_copy(x_peer(j), c, g_peer(i)).start()
        for j in range(nx - 1):
            for gg in range(ng):
                wc_copy(x_peer(j), other, gg).wait_recv()
        feat, norm = features(z, c)
        f_own[...] = feat
        n_own[...] = norm

    def stage_c(s, d):
        b, valid = at_step(s, d)

        @pl.when(valid)
        def _():
            for h in range(CHUNKS):
                for xx in range(nx):
                    e_wait(b, other, xx, h)

            @pl.loop(0, nc)
            def _(cc):
                feat, norm = features(b, cc)
                tile(b, cc, feat, norm)

    steps = nz * CHUNKS
    x_lag = 3
    c_lag = 3 + CHUNKS

    @pl.loop(0, steps + c_lag - 1)
    def _(t):
        @pl.when(t < steps)
        def _():
            stage_z(t, 0)
            stage_z(t, 1)

        @pl.when(t == 2)
        def _():
            stage_w()

        @pl.when(t == c_lag)
        def _():
            stage_first()

        @pl.when(jnp.logical_and(t >= c_lag, lax.rem(t - c_lag + CHUNKS, CHUNKS) == 0))
        def _():
            stage_c((t - c_lag) // CHUNKS, 0)
            stage_c((t - c_lag) // CHUNKS, 1)

        @pl.when(jnp.logical_and(t >= x_lag, t < steps + x_lag))
        def _():
            stage_x(t - x_lag, 0)
            stage_x(t - x_lag, 1)

    own_weight = jnp.sum(jnp.where(eye(), weight_row(z, c), 0.0), axis=1, keepdims=True)
    grad = (
        own_weight * (accum[...] - f_own[...].astype(jnp.float32) * (2.0 * quot[...]))
    ).astype(jnp.bfloat16)
    f_own[...] = grad

    middle = nz // 2
    left_side = z < middle
    inward = jnp.where(left_side, z + 1, z - 1)
    outward = jnp.where(left_side, z - 1, z + 1)
    is_middle = jnp.logical_or(z == middle - 1, z == middle)
    is_outer = jnp.logical_or(z == 0, z == nz - 1)
    spot = is_middle.astype(jnp.int32)

    def hc_copy(k):
        return remote(
            h_core.at[k], h_recv.at[k], hc_send.at[k], hc_recv.at[k], {"rep": other}
        )

    def hi_copy(k):
        return remote(
            h_send.at[k], h_side.at[spot, k], hi_send.at[k], hi_recv.at[spot, k],
            {"loop": inward},
        )

    def hi_wait(place, k):
        remote(
            h_send.at[k], h_side.at[place, k], hi_send.at[k], hi_recv.at[place, k],
            {"loop": inward},
        ).wait_recv()

    def ho_copy(k):
        slot = h_full.at[c, k]
        return remote(slot, slot, ho_send.at[k], hf_recv.at[c, k], {"loop": outward})

    def hf_copy(k):
        slot = h_full.at[c, k]
        return remote(slot, slot, hf_send.at[k], hf_recv.at[c, k], {"rep": other})

    for k in range(PARTS):
        part = lax.dot_general(
            e_all[z, c, x], f_own[:, k * width : (k + 1) * width], (((0,), (0,)), ((), ())),
            preferred_element_type=jnp.float32,
        )
        h_full_part = part.reshape(nc, half, width)

        @pl.when(c == 0)
        def _():
            h_own[k] = h_full_part[0]
            h_core[k] = h_full_part[1].astype(jnp.bfloat16)

        @pl.when(c == 1)
        def _():
            h_own[k] = h_full_part[1]
            h_core[k] = h_full_part[0].astype(jnp.bfloat16)

        hc_copy(k).start()

    for k in range(PARTS):
        hc_copy(k).wait_recv()
        h_own[k] = h_own[k] + h_recv[k].astype(jnp.float32)

        @pl.when(is_outer)
        def _():
            h_send[k] = h_own[k].astype(jnp.bfloat16)
            hi_copy(k).start()

    for k in range(PARTS):
        @pl.when(jnp.logical_not(is_outer))
        def _():
            hi_wait(0, k)
            h_send[k] = (h_own[k] + h_side[0, k].astype(jnp.float32)).astype(jnp.bfloat16)
            hi_copy(k).start()

    embed_out[...] = lax.dot_general(
        f_own[...], w_all[x].reshape(cols, feats), (((1,), (1,)), ((), ())), preferred_element_type=jnp.float32
    ).astype(jnp.bfloat16)

    for k in range(PARTS):
        @pl.when(is_middle)
        def _():
            hi_wait(1, k)
            h_full[c, k] = (
                h_send[k].astype(jnp.float32) + h_side[1, k].astype(jnp.float32)
            ).astype(jnp.bfloat16)

        @pl.when(jnp.logical_not(is_middle))
        def _():
            ho_copy(k).wait_recv()

        @pl.when(jnp.logical_not(is_outer))
        def _():
            ho_copy(k).start()

        hf_copy(k).start()

    for k in range(PARTS):
        slot = h_full.at[other, k]
        remote(slot, slot, hf_send.at[k], hf_recv.at[other, k], {"rep": other}).wait_recv()
    head_out[...] = h_full[...]

    @pl.loop(0, nz)
    def _(b):
        for h in range(CHUNKS):
            @pl.when(jnp.logical_and(b <= z, has_right))
            def _():
                z_copy(b, 0, h).wait_send()

            @pl.when(jnp.logical_and(b >= z, has_left))
            def _():
                z_copy(b, 1, h).wait_send()

            for j in range(nx - 1):
                x_copy(b, j, h).wait_send()
            for xx in range(nx):
                c_copy(b, xx, h).wait_send()

    for j in range(nx - 1):
        wx_copy(j).wait_send()
        for i in range(ng - 1):
            wy_copy(j, i).wait_send()
        for gg in range(ng):
            wc_copy(x_peer(j), c, gg).wait_send()
    for k in range(PARTS):
        hc_copy(k).wait_send()
        hi_copy(k).wait_send()
        hf_copy(k).wait_send()

        @pl.when(jnp.logical_not(is_outer))
        def _():
            ho_copy(k).wait_send()


def finish(embed_ref, head_ref, embed_out, head_out):
    cores, parts, half, width = head_ref.shape
    embed_out[...] = embed_ref[...]
    for cc in range(cores):
        for k in range(parts):
            head_out[cc * half : (cc + 1) * half, k * width : (k + 1) * width] = head_ref[
                cc, k
            ].astype(jnp.float32)


def ring_body(embeddings, head_weight, gp_weights, counts):
    nz, nx, nc, ng = (lax.axis_size(name) for name in ("loop", "enc", "rep", "groups"))
    rows, cols = embeddings.shape
    feats = head_weight.shape[1]
    half, width = cols // nc, feats // PARTS
    if half % (16 * ng):
        raise ValueError("head rows")
    gp_rows = gp_weights.reshape(-1, 128)
    vmem = pl.BlockSpec(memory_space=pltpu.VMEM)
    hbm = pl.BlockSpec(memory_space=pltpu.HBM)
    dma = pltpu.SemaphoreType.DMA
    embed_grad, head_sum = pl.pallas_call(
        functools.partial(kernel, (nz, nx, nc, ng)),
        out_shape=(
            jax.ShapeDtypeStruct((rows, cols), jnp.bfloat16),
            jax.ShapeDtypeStruct((nc, PARTS, half, width), jnp.bfloat16),
        ),
        in_specs=[hbm, hbm, hbm, hbm],
        out_specs=(vmem, vmem),
        scratch_shapes=[
            pltpu.VMEM(gp_rows.shape, jnp.float32),
            pltpu.SMEM(counts.shape, jnp.int32),
            pltpu.VMEM((nz, nc, nx, rows, cols), jnp.bfloat16),
            pltpu.VMEM((nx, nc, ng, half // ng, feats), jnp.bfloat16),
            pltpu.VMEM((rows, feats), jnp.bfloat16),
            pltpu.VMEM((rows, 1), jnp.float32),
            pltpu.VMEM((rows, feats), jnp.float32),
            pltpu.VMEM((rows, 1), jnp.float32),
            pltpu.VMEM((PARTS, half, width), jnp.float32),
            pltpu.VMEM((PARTS, half, width), jnp.bfloat16),
            pltpu.VMEM((PARTS, half, width), jnp.bfloat16),
            pltpu.VMEM((PARTS, half, width), jnp.bfloat16),
            pltpu.VMEM((2, PARTS, half, width), jnp.bfloat16),
            pltpu.VMEM((nc, PARTS, half, width), jnp.bfloat16),
            dma((nz, nc, nx, CHUNKS)),
            dma((2, nz, CHUNKS)),
            dma((nx - 1, nz, CHUNKS)),
            dma((nz, nx, CHUNKS)),
            dma((nx - 1,)),
            dma((nx, ng)),
            dma((nx - 1, max(ng - 1, 1))),
            dma((nx, ng)),
            dma((nx, ng)),
            dma((3 + nc * ng,)),
            dma((PARTS,)),
            dma((PARTS,)),
            dma((PARTS,)),
            dma((2, PARTS)),
            dma((PARTS,)),
            dma((PARTS,)),
            dma((nc, PARTS)),
        ],
        compiler_params=pltpu.CompilerParams(
            collective_id=0, has_side_effects=True, vmem_limit_bytes=VMEM_BYTES
        ),
    )(embeddings, head_weight, gp_rows, counts)
    return pl.pallas_call(
        finish,
        out_shape=(
            jax.ShapeDtypeStruct((rows, cols), jnp.bfloat16),
            jax.ShapeDtypeStruct((cols, feats), jnp.float32),
        ),
        in_specs=[vmem, vmem],
        out_specs=(vmem, vmem),
        compiler_params=pltpu.CompilerParams(vmem_limit_bytes=VMEM_BYTES),
    )(embed_grad, head_sum)


LINE = 4
PIECES = 4
COLUMNS = 3


def line_kernel(
    emb_ref,
    head_ref,
    gp_hbm,
    counts_hbm,
    embed_out,
    own_out,
    peer_out,
    gp_ref,
    counts_ref,
    e_all,
    w_all,
    f_all,
    n_row,
    n_col,
    w_row,
    accum,
    quot,
    grads,
    in_sem,
    e_send,
    e_recv,
    w_send,
    w_recv,
    f_send,
    f_recv,
    n_send,
    n_recv,
    h_send,
    h_recv,
):
    nz, nc = LINE, 2
    z = lax.axis_index("loop")
    x = lax.axis_index("enc")
    c = lax.axis_index("rep")
    g = lax.axis_index("groups")
    rows, cols = e_all.shape[2:]
    piece = rows // PIECES
    quarter, feats = w_all.shape[3:]
    block = nc * rows
    lanes = gp_ref.shape[1]
    inward = jnp.where(z < nz // 2, 1, -1)
    is_end = jnp.logical_or(z == 0, z == nz - 1)
    is_mid = jnp.logical_not(is_end)
    near = z + inward
    outer = z - inward
    second = z + 2 * inward
    third = z + 3 * inward
    x_dev, c_dev, g_dev = {"enc": 1 - x}, {"rep": 1 - c}, {"groups": 1 - g}

    def remote(src, dst, send, recv, device):
        return pltpu.make_async_remote_copy(
            src_ref=src, dst_ref=dst, send_sem=send, recv_sem=recv,
            device_id=device, device_id_type=MESH_ID,
        )

    def e_copy(side, b, h, kind, device):
        slot = e_all.at[side, b, pl.ds(h * piece, piece)]
        return remote(slot, slot, e_send.at[kind, h], e_recv.at[side, b, h], device)

    def e_wait(side, b, h):
        e_copy(side, b, h, 0, x_dev).wait_recv()

    def w_copy(cc, gg, kind, device):
        slot = w_all.at[1 - x, cc, gg]
        return remote(slot, slot, w_send.at[kind], w_recv.at[cc, gg], device)

    def w_first():
        slot = w_all.at[x, c, g]
        return remote(slot, slot, w_send.at[0], w_recv.at[c, g], x_dev)

    def f_copy(b, cc):
        slot = f_all.at[b, cc]
        return remote(slot, slot, f_send.at[b], f_recv.at[b], c_dev)

    def n_copy(b, cc):
        slot = n_row.at[b, cc]
        return remote(slot, slot, n_send.at[b], n_recv.at[b], c_dev)

    own_emb = pltpu.make_async_copy(emb_ref, e_all.at[x, z], in_sem.at[0])
    own_emb.start()
    loads = []
    for cc in range(nc):
        for gg in range(2):
            loads.append(
                pltpu.make_async_copy(
                    head_ref.at[pl.ds((cc * 2 + gg) * quarter, quarter)],
                    w_all.at[x, cc, gg],
                    in_sem.at[3 + cc * 2 + gg],
                )
            )
    loads.append(pltpu.make_async_copy(gp_hbm, gp_ref, in_sem.at[1]))
    loads.append(pltpu.make_async_copy(counts_hbm, counts_ref, in_sem.at[2]))
    for copy in loads:
        copy.start()

    barrier = pltpu.get_barrier_semaphore()

    def greet(device):
        pl.semaphore_signal(barrier, 1, device_id=device, device_id_type=MESH_ID)

    greet(x_dev)
    greet(c_dev)
    greet(g_dev)
    greet({"loop": near})

    @pl.when(is_mid)
    def _():
        greet({"loop": outer})

    for copy in loads:
        copy.wait()
    own_emb.wait()
    pl.semaphore_wait(barrier, 4 + is_mid.astype(jnp.int32))

    w_first().start()
    for h in range(PIECES):
        e_copy(x, z, h, 0, {"loop": near}).start()

        @pl.when(is_mid)
        def _():
            e_copy(x, z, h, 1, {"loop": outer}).start()

        e_copy(x, z, h, 2, x_dev).start()

    fourth = jnp.where(is_end, second, outer)
    last = jnp.where(is_end, third, second)
    half = rows // 2
    parts = [
        [(z, 0), (z, 1)],
        [(fourth, 0), (fourth, 1)],
        [(near, 0), (last, 0)],
        [(near, 1), (last, 1)],
    ]

    accum[...] = jnp.zeros_like(accum)
    quot[...] = jnp.zeros_like(quot)
    inside = lax.broadcasted_iota(jnp.int32, (1, lanes), 1)
    for v in range(nz):
        for cc in range(nc):
            for k, (b, h) in enumerate(parts[v]):
                place = cc * rows + h * half
                held = gp_ref[pl.ds(b * (block // lanes) + place // lanes, 1), :]
                w_row[v, cc, :, k * half : (k + 1) * half] = jnp.where(
                    inside + place < counts_ref[b], held, 0.0
                )

    def head_pass():
        w_copy(c, g, 0, x_dev).wait_recv()
        w_copy(c, g, 1, g_dev).start()
        w_copy(c, g, 2, c_dev).start()

    @pl.when(is_mid)
    def _():
        for h in range(PIECES):
            e_wait(x, outer, h)
            e_copy(x, outer, h, 3, {"loop": near}).start()
            e_wait(x, near, h)
            e_copy(x, near, h, 4, {"loop": outer}).start()
            if h == PIECES // 2 - 1:
                head_pass()
        for h in range(PIECES):
            e_wait(x, second, h)
            e_copy(x, second, h, 5, {"loop": outer}).start()
            e_copy(x, second, h, 6, x_dev).start()
        for h in range(PIECES):
            e_wait(1 - x, z, h)
            e_copy(1 - x, z, h, 7, {"loop": outer}).start()
            e_copy(1 - x, z, h, 8, {"loop": near}).start()

    @pl.when(is_end)
    def _():
        head_pass()
        for h in range(PIECES):
            e_wait(1 - x, z, h)
            e_copy(1 - x, z, h, 3, {"loop": near}).start()
        for h in range(PIECES):
            e_wait(x, second, h)
            e_copy(x, second, h, 4, x_dev).start()

    w_copy(c, 1 - g, 1, g_dev).wait_recv()
    w_copy(c, 1 - g, 3, c_dev).start()
    w_copy(1 - c, g, 2, c_dev).wait_recv()
    w_copy(1 - c, 1 - g, 3, c_dev).wait_recv()

    def eye():
        return lax.broadcasted_iota(jnp.int32, (rows, rows), 0) == lax.broadcasted_iota(
            jnp.int32, (rows, rows), 1
        )

    def taken(side, v):
        return jnp.concatenate(
            [e_all[side, b, h * half : (h + 1) * half] for b, h in parts[v]], axis=0
        )

    def features(v):
        total = jnp.dot(
            taken(0, v), w_all[0].reshape(cols, feats), preferred_element_type=jnp.float32
        ) + jnp.dot(
            taken(1, v), w_all[1].reshape(cols, feats), preferred_element_type=jnp.float32
        )
        held = total.astype(jnp.bfloat16)
        f_all[v, c] = held
        f_copy(v, c).start()
        wide = held.astype(jnp.float32)
        norm = jnp.sum(wide * wide, axis=1, keepdims=True)
        n_col[v] = jnp.broadcast_to(norm, (rows, lanes))
        n_row[v, c] = jnp.sum(jnp.where(eye(), norm, 0.0), axis=0, keepdims=True)
        n_copy(v, c).start()

    def scores_of(i, j):
        return lax.dot_general(
            f_all[i, c], f_all[j].reshape(block, feats), (((1,), (1,)), ((), ())),
            preferred_element_type=jnp.float32,
        )

    def wide_row(ref, j):
        return jnp.concatenate([ref[j, cc] for cc in range(nc)], axis=1)

    def pairs(i, j, scores):
        spread = block // lanes
        left = jnp.concatenate([n_col[i]] * spread, axis=1)
        both = left + wide_row(n_row, j)
        denom = (both - scores) + EPSILON
        scaled = wide_row(w_row, j) * (1.0 / (denom * denom))
        part = scaled * scores
        total = part[:, :lanes]
        for k in range(1, spread):
            total = total + part[:, k * lanes : (k + 1) * lanes]
        quot[i] += total
        return (both * scaled).astype(jnp.bfloat16)

    def finalize(i, carried):
        quotient = 2.0 * jnp.sum(quot[i], axis=1, keepdims=True)
        own_weight = jnp.sum(jnp.where(eye(), w_row[i, c], 0.0), axis=1, keepdims=True)
        grads[i] = (
            own_weight * (carried - f_all[i, c].astype(jnp.float32) * quotient)
        ).astype(jnp.bfloat16)

    def tiles(todo, final=False):
        scores = scores_of(*todo[0])
        for k, (i, j) in enumerate(todo):
            following = scores_of(*todo[k + 1]) if k + 1 < len(todo) else None
            weight = pairs(i, j, scores)
            carried = accum[i] + jnp.dot(
                weight, f_all[j].reshape(block, feats), preferred_element_type=jnp.float32
            )
            if final:
                finalize(i, carried)
            else:
                accum[i] = carried
            scores = following

    def third_pass(some):
        @pl.when(is_end)
        def _():
            for h in some:
                e_wait(x, third, h)
                e_copy(x, third, h, 5, x_dev).start()

    def meet(v):
        f_copy(v, 1 - c).wait_recv()
        n_copy(v, 1 - c).wait_recv()

    features(0)
    meet(0)
    tiles([(0, 0)])
    third_pass(range(PIECES // 2))
    for h in range(PIECES):
        e_wait(1 - x, fourth, h)
    features(1)
    third_pass(range(PIECES // 2, PIECES))
    tiles([(1, 0)])
    meet(1)
    tiles([(0, 1), (1, 1)])
    for v in (2, 3):
        start = (v - 2) * (PIECES // 2)
        for h in range(start, start + PIECES // 2):
            @pl.when(is_end)
            def _():
                e_wait(x, near, h)

            e_wait(1 - x, near, h)
            e_wait(1 - x, last, h)
        features(v)
        tiles([(v, j) for j in range(v)])
        meet(v)
        tiles([(i, v) for i in range(v + 1)], v == 3)

    width = feats // COLUMNS

    def h_copy(k):
        return remote(
            own_out.at[k], peer_out.at[k], h_send.at[k], h_recv.at[k], c_dev
        )

    for k in range(COLUMNS):
        own_out[k] = lax.dot_general(
            jnp.concatenate([taken(x, v) for v in range(nz)], axis=0),
            grads[:, :, k * width : (k + 1) * width].reshape(nz * rows, width),
            (((0,), (0,)), ((), ())),
            preferred_element_type=jnp.float32,
        ).astype(jnp.bfloat16)
        h_copy(k).start()

    embed_out[...] = lax.dot_general(
        grads[0], w_all[x].reshape(cols, feats), (((1,), (1,)), ((), ())),
        preferred_element_type=jnp.float32,
    ).astype(jnp.bfloat16)

    w_first().wait_send()
    for kind, device in ((1, g_dev), (2, c_dev), (3, c_dev)):
        w_copy(c, g, kind, device).wait_send()
    for b in range(nz):
        f_copy(b, c).wait_send()
        n_copy(b, c).wait_send()
    for h in range(PIECES):
        for kind in (0, 2, 3, 4, 5):
            e_copy(x, z, h, kind, x_dev).wait_send()

        @pl.when(is_mid)
        def _():
            for kind in (1, 6, 7, 8):
                e_copy(x, z, h, kind, x_dev).wait_send()

    for k in range(COLUMNS):
        h_copy(k).wait()


def line_finish(embed_ref, own_ref, peer_ref, embed_out, head_out):
    parts, _, width = own_ref.shape
    embed_out[...] = embed_ref[...]
    for k in range(parts):
        head_out[:, k * width : (k + 1) * width] = own_ref[k].astype(
            jnp.float32
        ) + peer_ref[k].astype(jnp.float32)


def line_body(embeddings, head_weight, gp_weights, counts):
    nz, nc, nx, ng = LINE, 2, 2, 2
    rows, cols = embeddings.shape
    feats = head_weight.shape[1]
    quarter, width = cols // (nc * ng), feats // COLUMNS
    lanes = 128
    gp_rows = gp_weights.reshape(-1, lanes)
    vmem = pl.BlockSpec(memory_space=pltpu.VMEM)
    hbm = pl.BlockSpec(memory_space=pltpu.HBM)
    dma = pltpu.SemaphoreType.DMA
    part = pltpu.VMEM((COLUMNS, cols, width), jnp.bfloat16)
    embed_grad, own, peer = pl.pallas_call(
        line_kernel,
        out_shape=(pltpu.VMEM((rows, cols), jnp.bfloat16), part, part),
        in_specs=[hbm, hbm, hbm, hbm],
        out_specs=(vmem, vmem, vmem),
        scratch_shapes=[
            pltpu.VMEM(gp_rows.shape, jnp.float32),
            pltpu.SMEM(counts.shape, jnp.int32),
            pltpu.VMEM((nx, nz, rows, cols), jnp.bfloat16),
            pltpu.VMEM((nx, nc, ng, quarter, feats), jnp.bfloat16),
            pltpu.VMEM((nz, nc, rows, feats), jnp.bfloat16),
            pltpu.VMEM((nz, nc, 1, rows), jnp.float32),
            pltpu.VMEM((nz, rows, lanes), jnp.float32),
            pltpu.VMEM((nz, nc, 1, rows), jnp.float32),
            pltpu.VMEM((nz, rows, feats), jnp.float32),
            pltpu.VMEM((nz, rows, lanes), jnp.float32),
            pltpu.VMEM((nz, rows, feats), jnp.bfloat16),
            dma((3 + nc * ng,)),
            dma((9, PIECES)),
            dma((nx, nz, PIECES)),
            dma((4,)),
            dma((nc, ng)),
            dma((nz,)),
            dma((nz,)),
            dma((nz,)),
            dma((nz,)),
            dma((COLUMNS,)),
            dma((COLUMNS,)),
        ],
        compiler_params=pltpu.CompilerParams(
            collective_id=0, has_side_effects=True, vmem_limit_bytes=VMEM_BYTES
        ),
    )(embeddings, head_weight, gp_rows, counts)
    embed_grad, own, peer = (
        pltpu.with_memory_space_constraint(held, pltpu.VMEM)
        for held in (embed_grad, own, peer)
    )
    return pl.pallas_call(
        line_finish,
        out_shape=(
            jax.ShapeDtypeStruct((rows, cols), jnp.bfloat16),
            jax.ShapeDtypeStruct((cols, feats), jnp.float32),
        ),
        in_specs=[vmem, vmem, vmem],
        out_specs=(vmem, vmem),
        compiler_params=pltpu.CompilerParams(vmem_limit_bytes=VMEM_BYTES),
    )(embed_grad, own, peer)


def body(*args):
    sizes = tuple(lax.axis_size(name) for name in ("loop", "enc", "rep", "groups"))
    return line_body(*args) if sizes == (LINE, 2, 2, 2) else ring_body(*args)


def solution(mesh):
    placed = (P(("groups", "loop", "rep"), "enc"), P("enc", None), P("groups"), P("groups"))
    return jax.shard_map(
        body,
        mesh=mesh,
        in_specs=placed,
        out_specs=(P(("groups", "loop", "rep"), "enc"), P(("groups", "enc"), None)),
        check_vma=False,
    )
```

```python
import functools

import jax
import jax.numpy as jnp
from jax import lax
from jax.experimental import pallas as pl
from jax.experimental.pallas import tpu as pltpu
from jax.sharding import PartitionSpec as P

EPSILON = 1e-06
PARTS = 6
CHUNKS = 2
VMEM_BYTES = 60 * 1024 * 1024
MESH_ID = pl.DeviceIdType.MESH


def kernel(
    sizes,
    emb_ref,
    head_ref,
    gp_hbm,
    counts_hbm,
    embed_out,
    head_out,
    gp_ref,
    counts_ref,
    e_all,
    w_all,
    f_own,
    n_own,
    accum,
    quot,
    h_own,
    h_core,
    h_recv,
    h_send,
    h_side,
    h_full,
    e_recv,
    z_send,
    x_send,
    c_send,
    w_send,
    w_recv,
    wy_send,
    wc_send,
    wc_recv,
    in_sem,
    hc_send,
    hc_recv,
    hi_send,
    hi_recv,
    ho_send,
    hf_send,
    hf_recv,
):
    nz, nx, nc, ng = sizes
    z = lax.axis_index("loop")
    x = lax.axis_index("enc")
    c = lax.axis_index("rep")
    g = lax.axis_index("groups")
    other = 1 - c
    rows, cols = e_all.shape[3:]
    piece = rows // CHUNKS
    quarter, feats = w_all.shape[3:]
    half = quarter * ng
    width = feats // PARTS
    has_left = z > 0
    has_right = z < nz - 1

    def x_peer(j):
        return lax.rem(x + 1 + j, nx)

    def remote(src, dst, send, recv, device):
        return pltpu.make_async_remote_copy(
            src_ref=src, dst_ref=dst, send_sem=send, recv_sem=recv,
            device_id=device, device_id_type=MESH_ID,
        )

    def g_peer(i):
        return lax.rem(g + 1 + i, ng)

    def e_copy(b, cc, xx, h, send, device):
        start = h * piece if isinstance(h, int) else pl.multiple_of(h * piece, piece)
        slot = e_all.at[b, cc, xx, pl.ds(start, piece)]
        return remote(slot, slot, send, e_recv.at[b, cc, xx, h], device)

    def z_copy(b, d, h):
        return e_copy(b, c, x, h, z_send.at[d, b, h], {"loop": z + (1 if d == 0 else -1)})

    def x_copy(b, j, h):
        return e_copy(b, c, x, h, x_send.at[j, b, h], {"enc": x_peer(j)})

    def c_copy(b, xx, h):
        return e_copy(b, c, xx, h, c_send.at[b, xx, h], {"rep": other})

    def e_wait(b, cc, xx, h):
        e_copy(b, cc, xx, h, c_send.at[b, xx, h], {"rep": other}).wait_recv()

    def w_copy(xx, gg, send, device):
        slot = w_all.at[xx, c, gg]
        return remote(slot, slot, send, w_recv.at[xx, gg], device)

    def wx_copy(j):
        return w_copy(x, g, w_send.at[j], {"enc": x_peer(j)})

    def wy_copy(j, i):
        return w_copy(x_peer(j), g, wy_send.at[j, i], {"groups": g_peer(i)})

    def w_wait(xx, gg):
        w_copy(xx, gg, w_send.at[0], {"rep": other}).wait_recv()

    def wc_copy(xx, cc, gg):
        slot = w_all.at[xx, cc, gg]
        return remote(slot, slot, wc_send.at[xx, gg], wc_recv.at[xx, gg], {"rep": other})

    own_emb = pltpu.make_async_copy(emb_ref, e_all.at[z, c, x], in_sem.at[0])
    own_emb.start()
    own_head = [
        pltpu.make_async_copy(gp_hbm, gp_ref, in_sem.at[1]),
        pltpu.make_async_copy(counts_hbm, counts_ref, in_sem.at[2]),
    ]
    for copy in own_head:
        copy.start()
    for cc in range(nc):
        for gg in range(ng):
            start = (cc * ng + gg) * quarter
            own_head.append(
                pltpu.make_async_copy(
                    head_ref.at[pl.ds(start, quarter)],
                    w_all.at[x, cc, gg],
                    in_sem.at[3 + cc * ng + gg],
                )
            )
            own_head[-1].start()

    barrier = pltpu.get_barrier_semaphore()

    @pl.when(has_left)
    def _():
        pl.semaphore_signal(barrier, 1, device_id={"loop": z - 1}, device_id_type=MESH_ID)

    @pl.when(has_right)
    def _():
        pl.semaphore_signal(barrier, 1, device_id={"loop": z + 1}, device_id_type=MESH_ID)

    for j in range(nx - 1):
        pl.semaphore_signal(barrier, 1, device_id={"enc": x_peer(j)}, device_id_type=MESH_ID)
    pl.semaphore_signal(barrier, 1, device_id={"rep": other}, device_id_type=MESH_ID)

    for i in range(ng - 1):
        pl.semaphore_signal(barrier, 1, device_id={"groups": g_peer(i)}, device_id_type=MESH_ID)
    accum[...] = jnp.zeros_like(accum)
    quot[...] = jnp.zeros_like(quot)

    pl.semaphore_wait(
        barrier, nx + ng - 1 + has_left.astype(jnp.int32) + has_right.astype(jnp.int32)
    )
    own_emb.wait()
    for copy in own_head:
        copy.wait()
    for j in range(nx - 1):
        wx_copy(j).start()

    def features(b, cc):
        total = jnp.dot(
            e_all[b, cc, 0], w_all[0].reshape(cols, feats),
            preferred_element_type=jnp.float32,
        )
        for xx in range(1, nx):
            total = total + jnp.dot(
                e_all[b, cc, xx], w_all[xx].reshape(cols, feats),
                preferred_element_type=jnp.float32,
            )
        total = total.astype(jnp.bfloat16)
        wide = total.astype(jnp.float32)
        return total, jnp.sum(wide * wide, axis=1, keepdims=True)

    def eye():
        return lax.broadcasted_iota(jnp.int32, (rows, rows), 0) == lax.broadcasted_iota(
            jnp.int32, (rows, rows), 1
        )

    def weight_row(b, cc):
        place = cc * rows + lax.broadcasted_iota(jnp.int32, (1, rows), 1)
        lanes = gp_ref.shape[1]
        split = rows // lanes
        first = (b * nc + cc) * split
        held = [gp_ref[pl.ds(first + i, 1), :] for i in range(split)]
        return jnp.where(place < counts_ref[b], jnp.concatenate(held, axis=1), 0.0)

    def tile(b, cc, feat, norm):
        norm_row = jnp.sum(jnp.where(eye(), norm, 0.0), axis=0, keepdims=True)
        scores = lax.dot_general(
            f_own[...], feat, (((1,), (1,)), ((), ())), preferred_element_type=jnp.float32
        )
        both = n_own[...] + norm_row
        denom = both - scores + EPSILON
        scaled = weight_row(b, cc) * (1.0 / (denom * denom))
        quot[...] += jnp.sum(scaled * scores, axis=1, keepdims=True)
        accum[...] += jnp.dot(
            (both * scaled).astype(jnp.bfloat16), feat, preferred_element_type=jnp.float32
        )

    def at_step(s, d):
        b = z - s if d == 0 else z + s
        return b, jnp.logical_and(jnp.logical_and(b >= 0, b < nz), s >= (1 if d else 0))

    def stage_z(u, d):
        s, h = u // CHUNKS, lax.rem(u, CHUNKS)
        b, valid = at_step(s, d)

        @pl.when(valid)
        def _():
            @pl.when(s > 0)
            def _():
                e_wait(b, c, x, h)

            @pl.when(has_right if d == 0 else has_left)
            def _():
                z_copy(b, d, h).start()

            if d == 0:
                @pl.when(jnp.logical_and(s == 0, has_left))
                def _():
                    z_copy(b, 1, h).start()

            for j in range(nx - 1):
                x_copy(b, j, h).start()
            c_copy(b, x, h).start()

    def stage_x(u, d):
        s, h = u // CHUNKS, lax.rem(u, CHUNKS)
        b, valid = at_step(s, d)

        @pl.when(valid)
        def _():
            for j in range(nx - 1):
                e_wait(b, c, x_peer(j), h)
                c_copy(b, x_peer(j), h).start()

    def stage_w():
        for j in range(nx - 1):
            w_wait(x_peer(j), g)
            for i in range(ng - 1):
                wy_copy(j, i).start()
            wc_copy(x_peer(j), c, g).start()

    def stage_first():
        for j in range(nx - 1):
            for i in range(ng - 1):
                w_wait(x_peer(j), g_peer(i))
                wc_copy(x_peer(j), c, g_peer(i)).start()
        for j in range(nx - 1):
            for gg in range(ng):
                wc_copy(x_peer(j), other, gg).wait_recv()
        feat, norm = features(z, c)
        f_own[...] = feat
        n_own[...] = norm

    def stage_c(s, d):
        b, valid = at_step(s, d)

        @pl.when(valid)
        def _():
            for h in range(CHUNKS):
                for xx in range(nx):
                    e_wait(b, other, xx, h)

            @pl.loop(0, nc)
            def _(cc):
                feat, norm = features(b, cc)
                tile(b, cc, feat, norm)

    steps = nz * CHUNKS
    x_lag = 3
    c_lag = 3 + CHUNKS

    @pl.loop(0, steps + c_lag - 1)
    def _(t):
        @pl.when(t < steps)
        def _():
            stage_z(t, 0)
            stage_z(t, 1)

        @pl.when(t == 2)
        def _():
            stage_w()

        @pl.when(t == c_lag)
        def _():
            stage_first()

        @pl.when(jnp.logical_and(t >= c_lag, lax.rem(t - c_lag + CHUNKS, CHUNKS) == 0))
        def _():
            stage_c((t - c_lag) // CHUNKS, 0)
            stage_c((t - c_lag) // CHUNKS, 1)

        @pl.when(jnp.logical_and(t >= x_lag, t < steps + x_lag))
        def _():
            stage_x(t - x_lag, 0)
            stage_x(t - x_lag, 1)

    own_weight = jnp.sum(jnp.where(eye(), weight_row(z, c), 0.0), axis=1, keepdims=True)
    grad = (
        own_weight * (accum[...] - f_own[...].astype(jnp.float32) * (2.0 * quot[...]))
    ).astype(jnp.bfloat16)
    f_own[...] = grad

    middle = nz // 2
    left_side = z < middle
    inward = jnp.where(left_side, z + 1, z - 1)
    outward = jnp.where(left_side, z - 1, z + 1)
    is_middle = jnp.logical_or(z == middle - 1, z == middle)
    is_outer = jnp.logical_or(z == 0, z == nz - 1)
    spot = is_middle.astype(jnp.int32)

    def hc_copy(k):
        return remote(
            h_core.at[k], h_recv.at[k], hc_send.at[k], hc_recv.at[k], {"rep": other}
        )

    def hi_copy(k):
        return remote(
            h_send.at[k], h_side.at[spot, k], hi_send.at[k], hi_recv.at[spot, k],
            {"loop": inward},
        )

    def hi_wait(place, k):
        remote(
            h_send.at[k], h_side.at[place, k], hi_send.at[k], hi_recv.at[place, k],
            {"loop": inward},
        ).wait_recv()

    def ho_copy(k):
        slot = h_full.at[c, k]
        return remote(slot, slot, ho_send.at[k], hf_recv.at[c, k], {"loop": outward})

    def hf_copy(k):
        slot = h_full.at[c, k]
        return remote(slot, slot, hf_send.at[k], hf_recv.at[c, k], {"rep": other})

    for k in range(PARTS):
        part = lax.dot_general(
            e_all[z, c, x], f_own[:, k * width : (k + 1) * width], (((0,), (0,)), ((), ())),
            preferred_element_type=jnp.float32,
        )
        h_full_part = part.reshape(nc, half, width)

        @pl.when(c == 0)
        def _():
            h_own[k] = h_full_part[0]
            h_core[k] = h_full_part[1].astype(jnp.bfloat16)

        @pl.when(c == 1)
        def _():
            h_own[k] = h_full_part[1]
            h_core[k] = h_full_part[0].astype(jnp.bfloat16)

        hc_copy(k).start()

    for k in range(PARTS):
        hc_copy(k).wait_recv()
        h_own[k] = h_own[k] + h_recv[k].astype(jnp.float32)

        @pl.when(is_outer)
        def _():
            h_send[k] = h_own[k].astype(jnp.bfloat16)
            hi_copy(k).start()

    for k in range(PARTS):
        @pl.when(jnp.logical_not(is_outer))
        def _():
            hi_wait(0, k)
            h_send[k] = (h_own[k] + h_side[0, k].astype(jnp.float32)).astype(jnp.bfloat16)
            hi_copy(k).start()

    embed_out[...] = lax.dot_general(
        f_own[...], w_all[x].reshape(cols, feats), (((1,), (1,)), ((), ())), preferred_element_type=jnp.float32
    ).astype(jnp.bfloat16)

    for k in range(PARTS):
        @pl.when(is_middle)
        def _():
            hi_wait(1, k)
            h_full[c, k] = (
                h_send[k].astype(jnp.float32) + h_side[1, k].astype(jnp.float32)
            ).astype(jnp.bfloat16)

        @pl.when(jnp.logical_not(is_middle))
        def _():
            ho_copy(k).wait_recv()

        @pl.when(jnp.logical_not(is_outer))
        def _():
            ho_copy(k).start()

        hf_copy(k).start()

    for k in range(PARTS):
        slot = h_full.at[other, k]
        remote(slot, slot, hf_send.at[k], hf_recv.at[other, k], {"rep": other}).wait_recv()
    head_out[...] = h_full[...]

    @pl.loop(0, nz)
    def _(b):
        for h in range(CHUNKS):
            @pl.when(jnp.logical_and(b <= z, has_right))
            def _():
                z_copy(b, 0, h).wait_send()

            @pl.when(jnp.logical_and(b >= z, has_left))
            def _():
                z_copy(b, 1, h).wait_send()

            for j in range(nx - 1):
                x_copy(b, j, h).wait_send()
            for xx in range(nx):
                c_copy(b, xx, h).wait_send()

    for j in range(nx - 1):
        wx_copy(j).wait_send()
        for i in range(ng - 1):
            wy_copy(j, i).wait_send()
        for gg in range(ng):
            wc_copy(x_peer(j), c, gg).wait_send()
    for k in range(PARTS):
        hc_copy(k).wait_send()
        hi_copy(k).wait_send()
        hf_copy(k).wait_send()

        @pl.when(jnp.logical_not(is_outer))
        def _():
            ho_copy(k).wait_send()


def finish(embed_ref, head_ref, embed_out, head_out):
    cores, parts, half, width = head_ref.shape
    embed_out[...] = embed_ref[...]
    for cc in range(cores):
        for k in range(parts):
            head_out[cc * half : (cc + 1) * half, k * width : (k + 1) * width] = head_ref[
                cc, k
            ].astype(jnp.float32)


def ring_body(embeddings, head_weight, gp_weights, counts):
    nz, nx, nc, ng = (lax.axis_size(name) for name in ("loop", "enc", "rep", "groups"))
    rows, cols = embeddings.shape
    feats = head_weight.shape[1]
    half, width = cols // nc, feats // PARTS
    if half % (16 * ng):
        raise ValueError("head rows")
    gp_rows = gp_weights.reshape(-1, 128)
    vmem = pl.BlockSpec(memory_space=pltpu.VMEM)
    hbm = pl.BlockSpec(memory_space=pltpu.HBM)
    dma = pltpu.SemaphoreType.DMA
    embed_grad, head_sum = pl.pallas_call(
        functools.partial(kernel, (nz, nx, nc, ng)),
        out_shape=(
            jax.ShapeDtypeStruct((rows, cols), jnp.bfloat16),
            jax.ShapeDtypeStruct((nc, PARTS, half, width), jnp.bfloat16),
        ),
        in_specs=[hbm, hbm, hbm, hbm],
        out_specs=(vmem, vmem),
        scratch_shapes=[
            pltpu.VMEM(gp_rows.shape, jnp.float32),
            pltpu.SMEM(counts.shape, jnp.int32),
            pltpu.VMEM((nz, nc, nx, rows, cols), jnp.bfloat16),
            pltpu.VMEM((nx, nc, ng, half // ng, feats), jnp.bfloat16),
            pltpu.VMEM((rows, feats), jnp.bfloat16),
            pltpu.VMEM((rows, 1), jnp.float32),
            pltpu.VMEM((rows, feats), jnp.float32),
            pltpu.VMEM((rows, 1), jnp.float32),
            pltpu.VMEM((PARTS, half, width), jnp.float32),
            pltpu.VMEM((PARTS, half, width), jnp.bfloat16),
            pltpu.VMEM((PARTS, half, width), jnp.bfloat16),
            pltpu.VMEM((PARTS, half, width), jnp.bfloat16),
            pltpu.VMEM((2, PARTS, half, width), jnp.bfloat16),
            pltpu.VMEM((nc, PARTS, half, width), jnp.bfloat16),
            dma((nz, nc, nx, CHUNKS)),
            dma((2, nz, CHUNKS)),
            dma((nx - 1, nz, CHUNKS)),
            dma((nz, nx, CHUNKS)),
            dma((nx - 1,)),
            dma((nx, ng)),
            dma((nx - 1, max(ng - 1, 1))),
            dma((nx, ng)),
            dma((nx, ng)),
            dma((3 + nc * ng,)),
            dma((PARTS,)),
            dma((PARTS,)),
            dma((PARTS,)),
            dma((2, PARTS)),
            dma((PARTS,)),
            dma((PARTS,)),
            dma((nc, PARTS)),
        ],
        compiler_params=pltpu.CompilerParams(
            collective_id=0, has_side_effects=True, vmem_limit_bytes=VMEM_BYTES
        ),
    )(embeddings, head_weight, gp_rows, counts)
    return pl.pallas_call(
        finish,
        out_shape=(
            jax.ShapeDtypeStruct((rows, cols), jnp.bfloat16),
            jax.ShapeDtypeStruct((cols, feats), jnp.float32),
        ),
        in_specs=[vmem, vmem],
        out_specs=(vmem, vmem),
        compiler_params=pltpu.CompilerParams(vmem_limit_bytes=VMEM_BYTES),
    )(embed_grad, head_sum)


LINE = 4
PIECES = 4
STRIPS = 3
COLUMNS = 3


def line_kernel(
    emb_ref,
    head_ref,
    gp_hbm,
    counts_hbm,
    embed_out,
    own_out,
    peer_out,
    gp_ref,
    counts_ref,
    e_all,
    w_all,
    f_all,
    n_row,
    n_col,
    w_row,
    accum,
    quot,
    grads,
    early_sum,
    w_col,
    e_turned,
    in_sem,
    e_send,
    e_recv,
    w_send,
    w_recv,
    f_send,
    f_recv,
    n_send,
    n_recv,
    h_send,
    h_recv,
):
    nz, nc = LINE, 2
    z = lax.axis_index("loop")
    x = lax.axis_index("enc")
    c = lax.axis_index("rep")
    g = lax.axis_index("groups")
    rows, cols = e_all.shape[2:]
    piece = rows // PIECES
    quarter, feats = w_all.shape[3:]
    block = nc * rows
    lanes = gp_ref.shape[1]
    inward = jnp.where(z < nz // 2, 1, -1)
    is_end = jnp.logical_or(z == 0, z == nz - 1)
    is_mid = jnp.logical_not(is_end)
    near = z + inward
    outer = z - inward
    second = z + 2 * inward
    third = z + 3 * inward
    x_dev, c_dev, g_dev = {"enc": 1 - x}, {"rep": 1 - c}, {"groups": 1 - g}

    def remote(src, dst, send, recv, device):
        return pltpu.make_async_remote_copy(
            src_ref=src, dst_ref=dst, send_sem=send, recv_sem=recv,
            device_id=device, device_id_type=MESH_ID,
        )

    def e_copy(side, b, h, kind, device):
        slot = e_all.at[side, b, pl.ds(h * piece, piece)]
        return remote(slot, slot, e_send.at[kind, h], e_recv.at[side, b, h], device)

    def e_wait(side, b, h):
        e_copy(side, b, h, 0, x_dev).wait_recv()

    def w_copy(cc, gg, p, kind, device, side=1 - x):
        strip = quarter // STRIPS
        slot = w_all.at[side, cc, gg, pl.ds(p * strip, strip)]
        return remote(slot, slot, w_send.at[kind, p], w_recv.at[cc, gg, p], device)

    def f_copy(b, cc):
        slot = f_all.at[b, cc]
        return remote(slot, slot, f_send.at[b], f_recv.at[b], c_dev)

    def n_copy(b, cc):
        slot = n_row.at[b, cc]
        return remote(slot, slot, n_send.at[b], n_recv.at[b], c_dev)

    own_emb = pltpu.make_async_copy(emb_ref, e_all.at[x, z], in_sem.at[0])
    own_emb.start()
    loads = []
    for cc in range(nc):
        for gg in range(2):
            loads.append(
                pltpu.make_async_copy(
                    head_ref.at[pl.ds((cc * 2 + gg) * quarter, quarter)],
                    w_all.at[x, cc, gg],
                    in_sem.at[3 + cc * 2 + gg],
                )
            )
    loads.append(pltpu.make_async_copy(gp_hbm, gp_ref, in_sem.at[1]))
    loads.append(pltpu.make_async_copy(counts_hbm, counts_ref, in_sem.at[2]))
    for copy in loads:
        copy.start()

    barrier = pltpu.get_barrier_semaphore()

    def greet(device):
        pl.semaphore_signal(barrier, 1, device_id=device, device_id_type=MESH_ID)

    greet(x_dev)
    greet(c_dev)
    greet(g_dev)
    greet({"loop": near})

    @pl.when(is_mid)
    def _():
        greet({"loop": outer})

    for copy in loads:
        copy.wait()
    own_emb.wait()
    pl.semaphore_wait(barrier, 4 + is_mid.astype(jnp.int32))

    for p in range(STRIPS):
        w_copy(c, g, p, 0, x_dev, x).start()
    for h in range(PIECES):
        e_copy(x, z, h, 0, {"loop": near}).start()

        @pl.when(is_mid)
        def _():
            e_copy(x, z, h, 1, {"loop": outer}).start()

        e_copy(x, z, h, 2, x_dev).start()

    fourth = jnp.where(is_end, second, outer)
    last = jnp.where(is_end, third, second)
    half = rows // 2
    parts = [
        [(z, 0), (z, 1)],
        [(fourth, 0), (fourth, 1)],
        [(near, 0), (last, 0)],
        [(near, 1), (last, 1)],
    ]

    accum[...] = jnp.zeros_like(accum)
    quot[...] = jnp.zeros_like(quot)
    inside = lax.broadcasted_iota(jnp.int32, (1, lanes), 1)
    for v in range(nz):
        for cc in range(nc):
            for k, (b, h) in enumerate(parts[v]):
                place = cc * rows + h * half
                held = gp_ref[pl.ds(b * (block // lanes) + place // lanes, 1), :]
                w_row[v, cc, :, k * half : (k + 1) * half] = jnp.where(
                    inside + place < counts_ref[b], held, 0.0
                )

    def eye():
        return lax.broadcasted_iota(jnp.int32, (rows, rows), 0) == lax.broadcasted_iota(
            jnp.int32, (rows, rows), 1
        )

    def taken(side, v):
        return jnp.concatenate(
            [e_all[side, b, h * half : (h + 1) * half] for b, h in parts[v]], axis=0
        )

    def early(v):
        own = taken(x, v)
        early_sum[...] = jnp.dot(
            own, w_all[x].reshape(cols, feats), preferred_element_type=jnp.float32
        )
        e_turned[:, v * rows : (v + 1) * rows] = own.T

    early(0)
    for v in range(nz):
        column = jnp.sum(jnp.where(eye(), w_row[v, c], 0.0), axis=1, keepdims=True)
        w_col[v] = jnp.broadcast_to(column, (rows, lanes))

    def x_strip(p):
        w_copy(c, g, p, 0, x_dev).wait_recv()
        w_copy(c, g, p, 1, g_dev).start()
        w_copy(c, g, p, 2, c_dev).start()

    def g_strip(p):
        w_copy(c, 1 - g, p, 1, g_dev).wait_recv()
        w_copy(c, 1 - g, p, 3, c_dev).start()

    @pl.when(is_mid)
    def _():
        for h in range(max(PIECES, STRIPS)):
            if h < STRIPS:
                x_strip(h)
            if h < PIECES:
                e_wait(x, outer, h)
                e_copy(x, outer, h, 3, {"loop": near}).start()
                e_wait(x, near, h)
                e_copy(x, near, h, 4, {"loop": outer}).start()
        for p in range(STRIPS):
            g_strip(p)
        for h in range(PIECES):
            e_wait(x, second, h)
            e_copy(x, second, h, 5, {"loop": outer}).start()
            e_copy(x, second, h, 6, x_dev).start()
        for h in range(PIECES):
            e_wait(1 - x, z, h)
            e_copy(1 - x, z, h, 7, {"loop": outer}).start()
            e_copy(1 - x, z, h, 8, {"loop": near}).start()

    @pl.when(is_end)
    def _():
        for p in range(STRIPS):
            x_strip(p)
        for h in range(PIECES + 1):
            if h < PIECES:
                e_wait(1 - x, z, h)
                e_copy(1 - x, z, h, 3, {"loop": near}).start()
            if h < STRIPS:
                g_strip(h)
            if h > 0:
                e_wait(x, second, h - 1)
                e_copy(x, second, h - 1, 4, x_dev).start()

    for p in range(STRIPS):
        w_copy(1 - c, g, p, 2, c_dev).wait_recv()
        w_copy(1 - c, 1 - g, p, 3, c_dev).wait_recv()

    def features(v):
        total = early_sum[...] + jnp.dot(
            taken(1 - x, v), w_all[1 - x].reshape(cols, feats),
            preferred_element_type=jnp.float32,
        )
        held = total.astype(jnp.bfloat16)
        f_all[v, c] = held
        f_copy(v, c).start()
        return held

    def norms(v, held):
        wide = held.astype(jnp.float32)
        norm = jnp.sum(wide * wide, axis=1, keepdims=True)
        n_col[v] = jnp.broadcast_to(norm, (rows, lanes))
        n_row[v, c] = jnp.sum(jnp.where(eye(), norm, 0.0), axis=0, keepdims=True)
        n_copy(v, c).start()

    def scores_of(i, j):
        return lax.dot_general(
            f_all[i, c], f_all[j].reshape(block, feats), (((1,), (1,)), ((), ())),
            preferred_element_type=jnp.float32,
        )

    def wide_row(ref, j):
        return jnp.concatenate([ref[j, cc] for cc in range(nc)], axis=1)

    def pairs(i, j, scores):
        spread = block // lanes
        left = jnp.concatenate([n_col[i]] * spread, axis=1)
        both = left + wide_row(n_row, j)
        denom = (both - scores) + EPSILON
        scaled = wide_row(w_row, j) * (1.0 / (denom * denom))
        part = scaled * scores
        total = part[:, :lanes]
        for k in range(1, spread):
            total = total + part[:, k * lanes : (k + 1) * lanes]
        quot[i] += total
        return (both * scaled).astype(jnp.bfloat16)

    def finalize(i, carried):
        quotient = 2.0 * jnp.sum(quot[i], axis=1, keepdims=True)
        own_weight = jnp.concatenate([w_col[i]] * (feats // lanes), axis=1)
        grads[i] = (
            own_weight * (carried - f_all[i, c].astype(jnp.float32) * quotient)
        ).astype(jnp.bfloat16)

    def tiles(todo, final=False, between=None):
        scores = scores_of(*todo[0])
        if between is not None:
            norms(*between)
        for k, (i, j) in enumerate(todo):
            following = scores_of(*todo[k + 1]) if k + 1 < len(todo) else None
            weight = pairs(i, j, scores)
            carried = accum[i] + jnp.dot(
                weight, f_all[j].reshape(block, feats), preferred_element_type=jnp.float32
            )
            if final:
                finalize(i, carried)
            else:
                accum[i] = carried
            scores = following

    def third_pass(some):
        @pl.when(is_end)
        def _():
            for h in some:
                e_wait(x, third, h)
                e_copy(x, third, h, 5, x_dev).start()

    def quarter_of(k):
        return range(k * PIECES // 4, (k + 1) * PIECES // 4)

    def meet(v):
        f_copy(v, 1 - c).wait_recv()
        n_copy(v, 1 - c).wait_recv()

    def near_own(some):
        @pl.when(is_end)
        def _():
            for h in some:
                e_wait(x, near, h)

    norms(0, features(0))
    third_pass(quarter_of(0))
    meet(0)
    tiles([(0, 0)])
    third_pass(quarter_of(1))
    early(1)
    for h in range(PIECES):
        e_wait(1 - x, fourth, h)
    held = features(1)
    third_pass(quarter_of(2))
    tiles([(1, 0)], between=(1, held))
    third_pass(quarter_of(3))
    near_own(range(PIECES // 2))
    early(2)
    meet(1)
    tiles([(0, 1), (1, 1)])
    for v in (2, 3):
        start = (v - 2) * (PIECES // 2)
        for h in range(start, start + PIECES // 2):
            e_wait(1 - x, near, h)
            e_wait(1 - x, last, h)
        held = features(v)
        tiles([(v, j) for j in range(v)], between=(v, held))
        if v == 2:
            near_own(range(PIECES // 2, PIECES))
            early(3)
        meet(v)
        tiles([(i, v) for i in range(v + 1)], v == 3)

    width = feats // COLUMNS

    def h_copy(k):
        return remote(
            own_out.at[k], peer_out.at[k], h_send.at[k], h_recv.at[k], c_dev
        )

    for k in range(COLUMNS):
        own_out[k] = jnp.dot(
            e_turned[...],
            grads[:, :, k * width : (k + 1) * width].reshape(nz * rows, width),
            preferred_element_type=jnp.float32,
        ).astype(jnp.bfloat16)
        h_copy(k).start()

    embed_out[...] = lax.dot_general(
        grads[0], w_all[x].reshape(cols, feats), (((1,), (1,)), ((), ())),
        preferred_element_type=jnp.float32,
    ).astype(jnp.bfloat16)

    for p in range(STRIPS):
        for kind, device in ((0, x_dev), (1, g_dev), (2, c_dev), (3, c_dev)):
            w_copy(c, g, p, kind, device).wait_send()
    for b in range(nz):
        f_copy(b, c).wait_send()
        n_copy(b, c).wait_send()
    for h in range(PIECES):
        for kind in (0, 2, 3, 4, 5):
            e_copy(x, z, h, kind, x_dev).wait_send()

        @pl.when(is_mid)
        def _():
            for kind in (1, 6, 7, 8):
                e_copy(x, z, h, kind, x_dev).wait_send()

    for k in range(COLUMNS):
        h_copy(k).wait()


def line_finish(embed_ref, own_ref, peer_ref, embed_out, head_out):
    parts, _, width = own_ref.shape
    embed_out[...] = embed_ref[...]
    for k in range(parts):
        head_out[:, k * width : (k + 1) * width] = own_ref[k].astype(
            jnp.float32
        ) + peer_ref[k].astype(jnp.float32)


def line_body(embeddings, head_weight, gp_weights, counts):
    nz, nc, nx, ng = LINE, 2, 2, 2
    rows, cols = embeddings.shape
    feats = head_weight.shape[1]
    quarter, width = cols // (nc * ng), feats // COLUMNS
    lanes = 128
    gp_rows = gp_weights.reshape(-1, lanes)
    vmem = pl.BlockSpec(memory_space=pltpu.VMEM)
    hbm = pl.BlockSpec(memory_space=pltpu.HBM)
    dma = pltpu.SemaphoreType.DMA
    part = pltpu.VMEM((COLUMNS, cols, width), jnp.bfloat16)
    embed_grad, own, peer = pl.pallas_call(
        line_kernel,
        out_shape=(pltpu.VMEM((rows, cols), jnp.bfloat16), part, part),
        in_specs=[hbm, hbm, hbm, hbm],
        out_specs=(vmem, vmem, vmem),
        scratch_shapes=[
            pltpu.VMEM(gp_rows.shape, jnp.float32),
            pltpu.SMEM(counts.shape, jnp.int32),
            pltpu.VMEM((nx, nz, rows, cols), jnp.bfloat16),
            pltpu.VMEM((nx, nc, ng, quarter, feats), jnp.bfloat16),
            pltpu.VMEM((nz, nc, rows, feats), jnp.bfloat16),
            pltpu.VMEM((nz, nc, 1, rows), jnp.float32),
            pltpu.VMEM((nz, rows, lanes), jnp.float32),
            pltpu.VMEM((nz, nc, 1, rows), jnp.float32),
            pltpu.VMEM((nz, rows, feats), jnp.float32),
            pltpu.VMEM((nz, rows, lanes), jnp.float32),
            pltpu.VMEM((nz, rows, feats), jnp.bfloat16),
            pltpu.VMEM((rows, feats), jnp.float32),
            pltpu.VMEM((nz, rows, lanes), jnp.float32),
            pltpu.VMEM((cols, nz * rows), jnp.bfloat16),
            dma((3 + nc * ng,)),
            dma((9, PIECES)),
            dma((nx, nz, PIECES)),
            dma((4, STRIPS)),
            dma((nc, ng, STRIPS)),
            dma((nz,)),
            dma((nz,)),
            dma((nz,)),
            dma((nz,)),
            dma((COLUMNS,)),
            dma((COLUMNS,)),
        ],
        compiler_params=pltpu.CompilerParams(
            collective_id=0, has_side_effects=True, vmem_limit_bytes=VMEM_BYTES
        ),
    )(embeddings, head_weight, gp_rows, counts)
    embed_grad, own, peer = (
        pltpu.with_memory_space_constraint(held, pltpu.VMEM)
        for held in (embed_grad, own, peer)
    )
    return pl.pallas_call(
        line_finish,
        out_shape=(
            jax.ShapeDtypeStruct((rows, cols), jnp.bfloat16),
            jax.ShapeDtypeStruct((cols, feats), jnp.float32),
        ),
        in_specs=[vmem, vmem, vmem],
        out_specs=(vmem, vmem),
        compiler_params=pltpu.CompilerParams(vmem_limit_bytes=VMEM_BYTES),
    )(embed_grad, own, peer)


def body(*args):
    sizes = tuple(lax.axis_size(name) for name in ("loop", "enc", "rep", "groups"))
    return line_body(*args) if sizes == (LINE, 2, 2, 2) else ring_body(*args)


def solution(mesh):
    placed = (P(("groups", "loop", "rep"), "enc"), P("enc", None), P("groups"), P("groups"))
    return jax.shard_map(
        body,
        mesh=mesh,
        in_specs=placed,
        out_specs=(P(("groups", "loop", "rep"), "enc"), P(("groups", "enc"), None)),
        check_vma=False,
    )
```

```python
import functools

import jax
import jax.numpy as jnp
from jax import lax
from jax.experimental import pallas as pl
from jax.experimental.pallas import tpu as pltpu
from jax.sharding import PartitionSpec as P

EPSILON = 1e-06
PARTS = 6
CHUNKS = 2
VMEM_BYTES = 60 * 1024 * 1024
MESH_ID = pl.DeviceIdType.MESH


def kernel(
    sizes,
    emb_ref,
    head_ref,
    gp_hbm,
    counts_hbm,
    embed_out,
    head_out,
    gp_ref,
    counts_ref,
    e_all,
    w_all,
    f_own,
    n_own,
    accum,
    quot,
    h_own,
    h_core,
    h_recv,
    h_send,
    h_side,
    h_full,
    e_recv,
    z_send,
    x_send,
    c_send,
    w_send,
    w_recv,
    wy_send,
    wc_send,
    wc_recv,
    in_sem,
    hc_send,
    hc_recv,
    hi_send,
    hi_recv,
    ho_send,
    hf_send,
    hf_recv,
):
    nz, nx, nc, ng = sizes
    z = lax.axis_index("loop")
    x = lax.axis_index("enc")
    c = lax.axis_index("rep")
    g = lax.axis_index("groups")
    other = 1 - c
    rows, cols = e_all.shape[3:]
    piece = rows // CHUNKS
    quarter, feats = w_all.shape[3:]
    half = quarter * ng
    width = feats // PARTS
    has_left = z > 0
    has_right = z < nz - 1

    def x_peer(j):
        return lax.rem(x + 1 + j, nx)

    def remote(src, dst, send, recv, device):
        return pltpu.make_async_remote_copy(
            src_ref=src, dst_ref=dst, send_sem=send, recv_sem=recv,
            device_id=device, device_id_type=MESH_ID,
        )

    def g_peer(i):
        return lax.rem(g + 1 + i, ng)

    def e_copy(b, cc, xx, h, send, device):
        start = h * piece if isinstance(h, int) else pl.multiple_of(h * piece, piece)
        slot = e_all.at[b, cc, xx, pl.ds(start, piece)]
        return remote(slot, slot, send, e_recv.at[b, cc, xx, h], device)

    def z_copy(b, d, h):
        return e_copy(b, c, x, h, z_send.at[d, b, h], {"loop": z + (1 if d == 0 else -1)})

    def x_copy(b, j, h):
        return e_copy(b, c, x, h, x_send.at[j, b, h], {"enc": x_peer(j)})

    def c_copy(b, xx, h):
        return e_copy(b, c, xx, h, c_send.at[b, xx, h], {"rep": other})

    def e_wait(b, cc, xx, h):
        e_copy(b, cc, xx, h, c_send.at[b, xx, h], {"rep": other}).wait_recv()

    def w_copy(xx, gg, send, device):
        slot = w_all.at[xx, c, gg]
        return remote(slot, slot, send, w_recv.at[xx, gg], device)

    def wx_copy(j):
        return w_copy(x, g, w_send.at[j], {"enc": x_peer(j)})

    def wy_copy(j, i):
        return w_copy(x_peer(j), g, wy_send.at[j, i], {"groups": g_peer(i)})

    def w_wait(xx, gg):
        w_copy(xx, gg, w_send.at[0], {"rep": other}).wait_recv()

    def wc_copy(xx, cc, gg):
        slot = w_all.at[xx, cc, gg]
        return remote(slot, slot, wc_send.at[xx, gg], wc_recv.at[xx, gg], {"rep": other})

    own_emb = pltpu.make_async_copy(emb_ref, e_all.at[z, c, x], in_sem.at[0])
    own_emb.start()
    own_head = [
        pltpu.make_async_copy(gp_hbm, gp_ref, in_sem.at[1]),
        pltpu.make_async_copy(counts_hbm, counts_ref, in_sem.at[2]),
    ]
    for copy in own_head:
        copy.start()
    for cc in range(nc):
        for gg in range(ng):
            start = (cc * ng + gg) * quarter
            own_head.append(
                pltpu.make_async_copy(
                    head_ref.at[pl.ds(start, quarter)],
                    w_all.at[x, cc, gg],
                    in_sem.at[3 + cc * ng + gg],
                )
            )
            own_head[-1].start()

    barrier = pltpu.get_barrier_semaphore()

    @pl.when(has_left)
    def _():
        pl.semaphore_signal(barrier, 1, device_id={"loop": z - 1}, device_id_type=MESH_ID)

    @pl.when(has_right)
    def _():
        pl.semaphore_signal(barrier, 1, device_id={"loop": z + 1}, device_id_type=MESH_ID)

    for j in range(nx - 1):
        pl.semaphore_signal(barrier, 1, device_id={"enc": x_peer(j)}, device_id_type=MESH_ID)
    pl.semaphore_signal(barrier, 1, device_id={"rep": other}, device_id_type=MESH_ID)

    for i in range(ng - 1):
        pl.semaphore_signal(barrier, 1, device_id={"groups": g_peer(i)}, device_id_type=MESH_ID)
    accum[...] = jnp.zeros_like(accum)
    quot[...] = jnp.zeros_like(quot)

    pl.semaphore_wait(
        barrier, nx + ng - 1 + has_left.astype(jnp.int32) + has_right.astype(jnp.int32)
    )
    own_emb.wait()
    for copy in own_head:
        copy.wait()
    for j in range(nx - 1):
        wx_copy(j).start()

    def features(b, cc):
        total = jnp.dot(
            e_all[b, cc, 0], w_all[0].reshape(cols, feats),
            preferred_element_type=jnp.float32,
        )
        for xx in range(1, nx):
            total = total + jnp.dot(
                e_all[b, cc, xx], w_all[xx].reshape(cols, feats),
                preferred_element_type=jnp.float32,
            )
        total = total.astype(jnp.bfloat16)
        wide = total.astype(jnp.float32)
        return total, jnp.sum(wide * wide, axis=1, keepdims=True)

    def eye():
        return lax.broadcasted_iota(jnp.int32, (rows, rows), 0) == lax.broadcasted_iota(
            jnp.int32, (rows, rows), 1
        )

    def weight_row(b, cc):
        place = cc * rows + lax.broadcasted_iota(jnp.int32, (1, rows), 1)
        lanes = gp_ref.shape[1]
        split = rows // lanes
        first = (b * nc + cc) * split
        held = [gp_ref[pl.ds(first + i, 1), :] for i in range(split)]
        return jnp.where(place < counts_ref[b], jnp.concatenate(held, axis=1), 0.0)

    def tile(b, cc, feat, norm):
        norm_row = jnp.sum(jnp.where(eye(), norm, 0.0), axis=0, keepdims=True)
        scores = lax.dot_general(
            f_own[...], feat, (((1,), (1,)), ((), ())), preferred_element_type=jnp.float32
        )
        both = n_own[...] + norm_row
        denom = both - scores + EPSILON
        scaled = weight_row(b, cc) * (1.0 / (denom * denom))
        quot[...] += jnp.sum(scaled * scores, axis=1, keepdims=True)
        accum[...] += jnp.dot(
            (both * scaled).astype(jnp.bfloat16), feat, preferred_element_type=jnp.float32
        )

    def at_step(s, d):
        b = z - s if d == 0 else z + s
        return b, jnp.logical_and(jnp.logical_and(b >= 0, b < nz), s >= (1 if d else 0))

    def stage_z(u, d):
        s, h = u // CHUNKS, lax.rem(u, CHUNKS)
        b, valid = at_step(s, d)

        @pl.when(valid)
        def _():
            @pl.when(s > 0)
            def _():
                e_wait(b, c, x, h)

            @pl.when(has_right if d == 0 else has_left)
            def _():
                z_copy(b, d, h).start()

            if d == 0:
                @pl.when(jnp.logical_and(s == 0, has_left))
                def _():
                    z_copy(b, 1, h).start()

            for j in range(nx - 1):
                x_copy(b, j, h).start()
            c_copy(b, x, h).start()

    def stage_x(u, d):
        s, h = u // CHUNKS, lax.rem(u, CHUNKS)
        b, valid = at_step(s, d)

        @pl.when(valid)
        def _():
            for j in range(nx - 1):
                e_wait(b, c, x_peer(j), h)
                c_copy(b, x_peer(j), h).start()

    def stage_w():
        for j in range(nx - 1):
            w_wait(x_peer(j), g)
            for i in range(ng - 1):
                wy_copy(j, i).start()
            wc_copy(x_peer(j), c, g).start()

    def stage_first():
        for j in range(nx - 1):
            for i in range(ng - 1):
                w_wait(x_peer(j), g_peer(i))
                wc_copy(x_peer(j), c, g_peer(i)).start()
        for j in range(nx - 1):
            for gg in range(ng):
                wc_copy(x_peer(j), other, gg).wait_recv()
        feat, norm = features(z, c)
        f_own[...] = feat
        n_own[...] = norm

    def stage_c(s, d):
        b, valid = at_step(s, d)

        @pl.when(valid)
        def _():
            for h in range(CHUNKS):
                for xx in range(nx):
                    e_wait(b, other, xx, h)

            @pl.loop(0, nc)
            def _(cc):
                feat, norm = features(b, cc)
                tile(b, cc, feat, norm)

    steps = nz * CHUNKS
    x_lag = 3
    c_lag = 3 + CHUNKS

    @pl.loop(0, steps + c_lag - 1)
    def _(t):
        @pl.when(t < steps)
        def _():
            stage_z(t, 0)
            stage_z(t, 1)

        @pl.when(t == 2)
        def _():
            stage_w()

        @pl.when(t == c_lag)
        def _():
            stage_first()

        @pl.when(jnp.logical_and(t >= c_lag, lax.rem(t - c_lag + CHUNKS, CHUNKS) == 0))
        def _():
            stage_c((t - c_lag) // CHUNKS, 0)
            stage_c((t - c_lag) // CHUNKS, 1)

        @pl.when(jnp.logical_and(t >= x_lag, t < steps + x_lag))
        def _():
            stage_x(t - x_lag, 0)
            stage_x(t - x_lag, 1)

    own_weight = jnp.sum(jnp.where(eye(), weight_row(z, c), 0.0), axis=1, keepdims=True)
    grad = (
        own_weight * (accum[...] - f_own[...].astype(jnp.float32) * (2.0 * quot[...]))
    ).astype(jnp.bfloat16)
    f_own[...] = grad

    middle = nz // 2
    left_side = z < middle
    inward = jnp.where(left_side, z + 1, z - 1)
    outward = jnp.where(left_side, z - 1, z + 1)
    is_middle = jnp.logical_or(z == middle - 1, z == middle)
    is_outer = jnp.logical_or(z == 0, z == nz - 1)
    spot = is_middle.astype(jnp.int32)

    def hc_copy(k):
        return remote(
            h_core.at[k], h_recv.at[k], hc_send.at[k], hc_recv.at[k], {"rep": other}
        )

    def hi_copy(k):
        return remote(
            h_send.at[k], h_side.at[spot, k], hi_send.at[k], hi_recv.at[spot, k],
            {"loop": inward},
        )

    def hi_wait(place, k):
        remote(
            h_send.at[k], h_side.at[place, k], hi_send.at[k], hi_recv.at[place, k],
            {"loop": inward},
        ).wait_recv()

    def ho_copy(k):
        slot = h_full.at[c, k]
        return remote(slot, slot, ho_send.at[k], hf_recv.at[c, k], {"loop": outward})

    def hf_copy(k):
        slot = h_full.at[c, k]
        return remote(slot, slot, hf_send.at[k], hf_recv.at[c, k], {"rep": other})

    for k in range(PARTS):
        part = lax.dot_general(
            e_all[z, c, x], f_own[:, k * width : (k + 1) * width], (((0,), (0,)), ((), ())),
            preferred_element_type=jnp.float32,
        )
        h_full_part = part.reshape(nc, half, width)

        @pl.when(c == 0)
        def _():
            h_own[k] = h_full_part[0]
            h_core[k] = h_full_part[1].astype(jnp.bfloat16)

        @pl.when(c == 1)
        def _():
            h_own[k] = h_full_part[1]
            h_core[k] = h_full_part[0].astype(jnp.bfloat16)

        hc_copy(k).start()

    for k in range(PARTS):
        hc_copy(k).wait_recv()
        h_own[k] = h_own[k] + h_recv[k].astype(jnp.float32)

        @pl.when(is_outer)
        def _():
            h_send[k] = h_own[k].astype(jnp.bfloat16)
            hi_copy(k).start()

    for k in range(PARTS):
        @pl.when(jnp.logical_not(is_outer))
        def _():
            hi_wait(0, k)
            h_send[k] = (h_own[k] + h_side[0, k].astype(jnp.float32)).astype(jnp.bfloat16)
            hi_copy(k).start()

    embed_out[...] = lax.dot_general(
        f_own[...], w_all[x].reshape(cols, feats), (((1,), (1,)), ((), ())), preferred_element_type=jnp.float32
    ).astype(jnp.bfloat16)

    for k in range(PARTS):
        @pl.when(is_middle)
        def _():
            hi_wait(1, k)
            h_full[c, k] = (
                h_send[k].astype(jnp.float32) + h_side[1, k].astype(jnp.float32)
            ).astype(jnp.bfloat16)

        @pl.when(jnp.logical_not(is_middle))
        def _():
            ho_copy(k).wait_recv()

        @pl.when(jnp.logical_not(is_outer))
        def _():
            ho_copy(k).start()

        hf_copy(k).start()

    for k in range(PARTS):
        slot = h_full.at[other, k]
        remote(slot, slot, hf_send.at[k], hf_recv.at[other, k], {"rep": other}).wait_recv()
    head_out[...] = h_full[...]

    @pl.loop(0, nz)
    def _(b):
        for h in range(CHUNKS):
            @pl.when(jnp.logical_and(b <= z, has_right))
            def _():
                z_copy(b, 0, h).wait_send()

            @pl.when(jnp.logical_and(b >= z, has_left))
            def _():
                z_copy(b, 1, h).wait_send()

            for j in range(nx - 1):
                x_copy(b, j, h).wait_send()
            for xx in range(nx):
                c_copy(b, xx, h).wait_send()

    for j in range(nx - 1):
        wx_copy(j).wait_send()
        for i in range(ng - 1):
            wy_copy(j, i).wait_send()
        for gg in range(ng):
            wc_copy(x_peer(j), c, gg).wait_send()
    for k in range(PARTS):
        hc_copy(k).wait_send()
        hi_copy(k).wait_send()
        hf_copy(k).wait_send()

        @pl.when(jnp.logical_not(is_outer))
        def _():
            ho_copy(k).wait_send()


def finish(embed_ref, head_ref, embed_out, head_out):
    cores, parts, half, width = head_ref.shape
    embed_out[...] = embed_ref[...]
    for cc in range(cores):
        for k in range(parts):
            head_out[cc * half : (cc + 1) * half, k * width : (k + 1) * width] = head_ref[
                cc, k
            ].astype(jnp.float32)


def ring_body(embeddings, head_weight, gp_weights, counts):
    nz, nx, nc, ng = (lax.axis_size(name) for name in ("loop", "enc", "rep", "groups"))
    rows, cols = embeddings.shape
    feats = head_weight.shape[1]
    half, width = cols // nc, feats // PARTS
    if half % (16 * ng):
        raise ValueError("head rows")
    gp_rows = gp_weights.reshape(-1, 128)
    vmem = pl.BlockSpec(memory_space=pltpu.VMEM)
    hbm = pl.BlockSpec(memory_space=pltpu.HBM)
    dma = pltpu.SemaphoreType.DMA
    embed_grad, head_sum = pl.pallas_call(
        functools.partial(kernel, (nz, nx, nc, ng)),
        out_shape=(
            jax.ShapeDtypeStruct((rows, cols), jnp.bfloat16),
            jax.ShapeDtypeStruct((nc, PARTS, half, width), jnp.bfloat16),
        ),
        in_specs=[hbm, hbm, hbm, hbm],
        out_specs=(vmem, vmem),
        scratch_shapes=[
            pltpu.VMEM(gp_rows.shape, jnp.float32),
            pltpu.SMEM(counts.shape, jnp.int32),
            pltpu.VMEM((nz, nc, nx, rows, cols), jnp.bfloat16),
            pltpu.VMEM((nx, nc, ng, half // ng, feats), jnp.bfloat16),
            pltpu.VMEM((rows, feats), jnp.bfloat16),
            pltpu.VMEM((rows, 1), jnp.float32),
            pltpu.VMEM((rows, feats), jnp.float32),
            pltpu.VMEM((rows, 1), jnp.float32),
            pltpu.VMEM((PARTS, half, width), jnp.float32),
            pltpu.VMEM((PARTS, half, width), jnp.bfloat16),
            pltpu.VMEM((PARTS, half, width), jnp.bfloat16),
            pltpu.VMEM((PARTS, half, width), jnp.bfloat16),
            pltpu.VMEM((2, PARTS, half, width), jnp.bfloat16),
            pltpu.VMEM((nc, PARTS, half, width), jnp.bfloat16),
            dma((nz, nc, nx, CHUNKS)),
            dma((2, nz, CHUNKS)),
            dma((nx - 1, nz, CHUNKS)),
            dma((nz, nx, CHUNKS)),
            dma((nx - 1,)),
            dma((nx, ng)),
            dma((nx - 1, max(ng - 1, 1))),
            dma((nx, ng)),
            dma((nx, ng)),
            dma((3 + nc * ng,)),
            dma((PARTS,)),
            dma((PARTS,)),
            dma((PARTS,)),
            dma((2, PARTS)),
            dma((PARTS,)),
            dma((PARTS,)),
            dma((nc, PARTS)),
        ],
        compiler_params=pltpu.CompilerParams(
            collective_id=0, has_side_effects=True, vmem_limit_bytes=VMEM_BYTES
        ),
    )(embeddings, head_weight, gp_rows, counts)
    return pl.pallas_call(
        finish,
        out_shape=(
            jax.ShapeDtypeStruct((rows, cols), jnp.bfloat16),
            jax.ShapeDtypeStruct((cols, feats), jnp.float32),
        ),
        in_specs=[vmem, vmem],
        out_specs=(vmem, vmem),
        compiler_params=pltpu.CompilerParams(vmem_limit_bytes=VMEM_BYTES),
    )(embed_grad, head_sum)


LINE = 4
PIECES = 4
STRIPS = 3
COLUMNS = 2


def line_kernel(
    emb_ref,
    head_ref,
    gp_hbm,
    counts_hbm,
    embed_out,
    own_out,
    peer_out,
    gp_ref,
    counts_ref,
    e_all,
    w_all,
    f_all,
    n_row,
    n_col,
    w_row,
    accum,
    quot,
    grads,
    early_sum,
    w_col,
    e_turned,
    in_sem,
    e_send,
    e_recv,
    w_send,
    w_recv,
    f_send,
    f_recv,
    n_send,
    n_recv,
    h_send,
    h_recv,
):
    nz, nc = LINE, 2
    z = lax.axis_index("loop")
    x = lax.axis_index("enc")
    c = lax.axis_index("rep")
    g = lax.axis_index("groups")
    rows, cols = e_all.shape[2:]
    piece = rows // PIECES
    quarter, feats = w_all.shape[3:]
    block = nc * rows
    lanes = gp_ref.shape[1]
    inward = jnp.where(z < nz // 2, 1, -1)
    is_end = jnp.logical_or(z == 0, z == nz - 1)
    is_mid = jnp.logical_not(is_end)
    near = z + inward
    outer = z - inward
    second = z + 2 * inward
    third = z + 3 * inward
    x_dev, c_dev, g_dev = {"enc": 1 - x}, {"rep": 1 - c}, {"groups": 1 - g}

    def remote(src, dst, send, recv, device):
        return pltpu.make_async_remote_copy(
            src_ref=src, dst_ref=dst, send_sem=send, recv_sem=recv,
            device_id=device, device_id_type=MESH_ID,
        )

    def e_copy(side, b, h, kind, device):
        slot = e_all.at[side, b, pl.ds(h * piece, piece)]
        return remote(slot, slot, e_send.at[kind, h], e_recv.at[side, b, h], device)

    def e_wait(side, b, h):
        e_copy(side, b, h, 0, x_dev).wait_recv()

    def w_copy(cc, gg, p, kind, device, side=1 - x):
        strip = quarter // STRIPS
        slot = w_all.at[side, cc, gg, pl.ds(p * strip, strip)]
        return remote(slot, slot, w_send.at[kind, p], w_recv.at[cc, gg, p], device)

    def f_copy(b, cc):
        slot = f_all.at[b, cc]
        return remote(slot, slot, f_send.at[b], f_recv.at[b], c_dev)

    def n_copy(b, cc):
        slot = n_row.at[b, cc]
        return remote(slot, slot, n_send.at[b], n_recv.at[b], c_dev)

    own_emb = pltpu.make_async_copy(emb_ref, e_all.at[x, z], in_sem.at[0])
    own_emb.start()
    loads = []
    for cc in range(nc):
        for gg in range(2):
            loads.append(
                pltpu.make_async_copy(
                    head_ref.at[pl.ds((cc * 2 + gg) * quarter, quarter)],
                    w_all.at[x, cc, gg],
                    in_sem.at[3 + cc * 2 + gg],
                )
            )
    loads.append(pltpu.make_async_copy(gp_hbm, gp_ref, in_sem.at[1]))
    loads.append(pltpu.make_async_copy(counts_hbm, counts_ref, in_sem.at[2]))
    for copy in loads:
        copy.start()

    barrier = pltpu.get_barrier_semaphore()

    def greet(device):
        pl.semaphore_signal(barrier, 1, device_id=device, device_id_type=MESH_ID)

    greet(x_dev)
    greet(c_dev)
    greet(g_dev)
    greet({"loop": near})

    @pl.when(is_mid)
    def _():
        greet({"loop": outer})

    for copy in loads:
        copy.wait()
    own_emb.wait()
    pl.semaphore_wait(barrier, 4 + is_mid.astype(jnp.int32))

    for p in range(STRIPS):
        w_copy(c, g, p, 0, x_dev, x).start()
    for h in range(PIECES):
        e_copy(x, z, h, 0, {"loop": near}).start()

    @pl.when(is_mid)
    def _():
        for h in range(4):
            e_copy(x, z, h, 1, {"loop": outer}).start()


    fourth = jnp.where(is_end, second, outer)
    last = jnp.where(is_end, third, second)
    half = rows // 2
    parts = [
        [(z, 0), (z, 1)],
        [(fourth, 0), (fourth, 1)],
        [(near, 0), (last, 0)],
        [(near, 1), (last, 1)],
    ]

    accum[...] = jnp.zeros_like(accum)
    quot[...] = jnp.zeros_like(quot)
    inside = lax.broadcasted_iota(jnp.int32, (1, lanes), 1)
    for v in range(nz):
        for cc in range(nc):
            for k, (b, h) in enumerate(parts[v]):
                place = cc * rows + h * half
                held = gp_ref[pl.ds(b * (block // lanes) + place // lanes, 1), :]
                w_row[v, cc, :, k * half : (k + 1) * half] = jnp.where(
                    inside + place < counts_ref[b], held, 0.0
                )

    def eye():
        return lax.broadcasted_iota(jnp.int32, (rows, rows), 0) == lax.broadcasted_iota(
            jnp.int32, (rows, rows), 1
        )

    def taken(side, v):
        return jnp.concatenate(
            [e_all[side, b, h * half : (h + 1) * half] for b, h in parts[v]], axis=0
        )

    def early(b, places):
        made = jnp.dot(
            e_all[x, b], w_all[x].reshape(cols, feats), preferred_element_type=jnp.float32
        )
        for h, (v, k) in enumerate(places):
            own = slice(h * half, (h + 1) * half)
            early_sum[v, k * half : (k + 1) * half] = made[own]
            spot = v * rows + k * half
            e_turned[:, spot : spot + half] = e_all[x, b, own].T

    early(z, [(0, 0), (0, 1)])
    for v in range(nz):
        column = jnp.sum(jnp.where(eye(), w_row[v, c], 0.0), axis=1, keepdims=True)
        w_col[v] = jnp.broadcast_to(column, (rows, lanes))

    for p in range(STRIPS):
        w_copy(c, g, p, 0, x_dev, x).wait_send()
        if p == STRIPS - 1:
            for h in range(PIECES):
                e_copy(x, z, h, 2, x_dev).start()

    def x_strip(p):
        w_copy(c, g, p, 0, x_dev).wait_recv()
        w_copy(c, g, p, 1, g_dev).start()
        w_copy(c, g, p, 2, c_dev).start()

    def g_strip(p):
        w_copy(c, 1 - g, p, 1, g_dev).wait_recv()
        w_copy(c, 1 - g, p, 3, c_dev).start()

    @pl.when(is_mid)
    def _():
        for h in range(max(PIECES, STRIPS)):
            if h < STRIPS:
                x_strip(h)
            if h < PIECES:
                e_wait(x, outer, h)
                e_copy(x, outer, h, 3, {"loop": near}).start()
                e_wait(x, near, h)
                e_copy(x, near, h, 4, {"loop": outer}).start()
        early(near, [(2, 0), (3, 0)])
        for p in range(STRIPS):
            g_strip(p)
        for h in range(PIECES):
            e_wait(x, second, h)
            e_copy(x, second, h, 5, {"loop": outer}).start()
            e_copy(x, second, h, 6, x_dev).start()
        for h in range(PIECES):
            e_wait(1 - x, z, h)
            e_copy(1 - x, z, h, 7, {"loop": outer}).start()
            e_copy(1 - x, z, h, 8, {"loop": near}).start()

    @pl.when(is_end)
    def _():
        for p in range(STRIPS):
            x_strip(p)
        for h in range(PIECES):
            e_wait(x, near, h)
        early(near, [(2, 0), (3, 0)])
        for h in range(PIECES + 1):
            if h < PIECES:
                e_wait(1 - x, z, h)
                e_copy(1 - x, z, h, 3, {"loop": near}).start()
            if h < STRIPS:
                g_strip(h)
            if h > 0:
                e_wait(x, second, h - 1)
                e_copy(x, second, h - 1, 4, x_dev).start()

    for p in range(STRIPS):
        w_copy(1 - c, g, p, 2, c_dev).wait_recv()
        w_copy(1 - c, 1 - g, p, 3, c_dev).wait_recv()

    def features(v):
        total = early_sum[v] + jnp.dot(
            taken(1 - x, v), w_all[1 - x].reshape(cols, feats),
            preferred_element_type=jnp.float32,
        )
        held = total.astype(jnp.bfloat16)
        f_all[v, c] = held
        f_copy(v, c).start()
        return held

    def norms(v, held):
        wide = held.astype(jnp.float32)
        norm = jnp.sum(wide * wide, axis=1, keepdims=True)
        n_col[v] = jnp.broadcast_to(norm, (rows, lanes))
        n_row[v, c] = jnp.sum(jnp.where(eye(), norm, 0.0), axis=0, keepdims=True)
        n_copy(v, c).start()

    def scores_of(i, j):
        return lax.dot_general(
            f_all[i, c], f_all[j].reshape(block, feats), (((1,), (1,)), ((), ())),
            preferred_element_type=jnp.float32,
        )

    def wide_row(ref, j):
        return jnp.concatenate([ref[j, cc] for cc in range(nc)], axis=1)

    def pairs(i, j, scores):
        spread = block // lanes
        left = jnp.concatenate([n_col[i]] * spread, axis=1)
        both = left + wide_row(n_row, j)
        denom = (both - scores) + EPSILON
        scaled = wide_row(w_row, j) * (1.0 / (denom * denom))
        part = scaled * scores
        total = part[:, :lanes]
        for k in range(1, spread):
            total = total + part[:, k * lanes : (k + 1) * lanes]
        quot[i] += total
        return (both * scaled).astype(jnp.bfloat16)

    def finalize(i, carried):
        quotient = 2.0 * jnp.sum(quot[i], axis=1, keepdims=True)
        own_weight = jnp.concatenate([w_col[i]] * (feats // lanes), axis=1)
        grads[i] = (
            own_weight * (carried - f_all[i, c].astype(jnp.float32) * quotient)
        ).astype(jnp.bfloat16)

    def tiles(todo, final=False, between=None):
        scores = scores_of(*todo[0])
        if between is not None:
            norms(*between)
        for k, (i, j) in enumerate(todo):
            following = scores_of(*todo[k + 1]) if k + 1 < len(todo) else None
            weight = pairs(i, j, scores)
            carried = accum[i] + jnp.dot(
                weight, f_all[j].reshape(block, feats), preferred_element_type=jnp.float32
            )
            if final and j == nz - 1:
                finalize(i, carried)
            else:
                accum[i] = carried
            scores = following

    def third_pass(some):
        @pl.when(is_end)
        def _():
            for h in some:
                e_wait(x, third, h)
                e_copy(x, third, h, 5, x_dev).start()

    def quarter_of(k):
        return range(k * PIECES // 4, (k + 1) * PIECES // 4)

    def meet(v):
        f_copy(v, 1 - c).wait_recv()
        n_copy(v, 1 - c).wait_recv()

    norms(0, features(0))
    third_pass(quarter_of(0))
    early(fourth, [(1, 0), (1, 1)])
    meet(0)
    tiles([(0, 0)])
    third_pass(quarter_of(1))
    for h in range(PIECES):
        e_wait(1 - x, fourth, h)
    held = features(1)
    third_pass(quarter_of(2))
    tiles([(1, 0)], between=(1, held))
    third_pass(quarter_of(3))
    early(last, [(2, 1), (3, 1)])
    meet(1)
    tiles([(0, 1), (1, 1)])
    for v in (2, 3):
        start = (v - 2) * (PIECES // 2)
        for h in range(start, start + PIECES // 2):
            e_wait(1 - x, near, h)
            e_wait(1 - x, last, h)
        held = features(v)
        tiles([(v, j) for j in range(v)], between=(v, held))
        meet(v)
        tiles([(i, v) for i in range(v + 1)], v == 3)

    width = feats // COLUMNS

    def h_copy(k):
        return remote(
            own_out.at[k], peer_out.at[k], h_send.at[k], h_recv.at[k], c_dev
        )

    for k in range(COLUMNS):
        own_out[k] = jnp.dot(
            e_turned[...],
            grads[:, :, k * width : (k + 1) * width].reshape(nz * rows, width),
            preferred_element_type=jnp.float32,
        ).astype(jnp.bfloat16)
        h_copy(k).start()

    embed_out[...] = lax.dot_general(
        grads[0], w_all[x].reshape(cols, feats), (((1,), (1,)), ((), ())),
        preferred_element_type=jnp.float32,
    ).astype(jnp.bfloat16)

    for p in range(STRIPS):
        for kind, device in ((1, g_dev), (2, c_dev), (3, c_dev)):
            w_copy(c, g, p, kind, device).wait_send()
    for b in range(nz):
        f_copy(b, c).wait_send()
        n_copy(b, c).wait_send()
    for h in range(PIECES):
        for kind in (0, 2, 3, 4, 5):
            e_copy(x, z, h, kind, x_dev).wait_send()

        @pl.when(is_mid)
        def _():
            for kind in (1, 6, 7, 8):
                e_copy(x, z, h, kind, x_dev).wait_send()

    for k in range(COLUMNS):
        h_copy(k).wait()


def line_finish(embed_ref, own_ref, peer_ref, embed_out, head_out):
    parts, _, width = own_ref.shape
    embed_out[...] = embed_ref[...]
    for k in range(parts):
        head_out[:, k * width : (k + 1) * width] = own_ref[k].astype(
            jnp.float32
        ) + peer_ref[k].astype(jnp.float32)


def line_body(embeddings, head_weight, gp_weights, counts):
    nz, nc, nx, ng = LINE, 2, 2, 2
    rows, cols = embeddings.shape
    feats = head_weight.shape[1]
    quarter, width = cols // (nc * ng), feats // COLUMNS
    lanes = 128
    gp_rows = gp_weights.reshape(-1, lanes)
    vmem = pl.BlockSpec(memory_space=pltpu.VMEM)
    hbm = pl.BlockSpec(memory_space=pltpu.HBM)
    dma = pltpu.SemaphoreType.DMA
    part = pltpu.VMEM((COLUMNS, cols, width), jnp.bfloat16)
    embed_grad, own, peer = pl.pallas_call(
        line_kernel,
        out_shape=(pltpu.VMEM((rows, cols), jnp.bfloat16), part, part),
        in_specs=[hbm, hbm, hbm, hbm],
        out_specs=(vmem, vmem, vmem),
        scratch_shapes=[
            pltpu.VMEM(gp_rows.shape, jnp.float32),
            pltpu.SMEM(counts.shape, jnp.int32),
            pltpu.VMEM((nx, nz, rows, cols), jnp.bfloat16),
            pltpu.VMEM((nx, nc, ng, quarter, feats), jnp.bfloat16),
            pltpu.VMEM((nz, nc, rows, feats), jnp.bfloat16),
            pltpu.VMEM((nz, nc, 1, rows), jnp.float32),
            pltpu.VMEM((nz, rows, lanes), jnp.float32),
            pltpu.VMEM((nz, nc, 1, rows), jnp.float32),
            pltpu.VMEM((nz, rows, feats), jnp.float32),
            pltpu.VMEM((nz, rows, lanes), jnp.float32),
            pltpu.VMEM((nz, rows, feats), jnp.bfloat16),
            pltpu.VMEM((nz, rows, feats), jnp.float32),
            pltpu.VMEM((nz, rows, lanes), jnp.float32),
            pltpu.VMEM((cols, nz * rows), jnp.bfloat16),
            dma((3 + nc * ng,)),
            dma((9, PIECES)),
            dma((nx, nz, PIECES)),
            dma((4, STRIPS)),
            dma((nc, ng, STRIPS)),
            dma((nz,)),
            dma((nz,)),
            dma((nz,)),
            dma((nz,)),
            dma((COLUMNS,)),
            dma((COLUMNS,)),
        ],
        compiler_params=pltpu.CompilerParams(
            collective_id=0, has_side_effects=True, vmem_limit_bytes=VMEM_BYTES
        ),
    )(embeddings, head_weight, gp_rows, counts)
    embed_grad, own, peer = (
        pltpu.with_memory_space_constraint(held, pltpu.VMEM)
        for held in (embed_grad, own, peer)
    )
    return pl.pallas_call(
        line_finish,
        out_shape=(
            jax.ShapeDtypeStruct((rows, cols), jnp.bfloat16),
            jax.ShapeDtypeStruct((cols, feats), jnp.float32),
        ),
        in_specs=[vmem, vmem, vmem],
        out_specs=(vmem, vmem),
        compiler_params=pltpu.CompilerParams(vmem_limit_bytes=VMEM_BYTES),
    )(embed_grad, own, peer)


def body(*args):
    sizes = tuple(lax.axis_size(name) for name in ("loop", "enc", "rep", "groups"))
    return line_body(*args) if sizes == (LINE, 2, 2, 2) else ring_body(*args)


def solution(mesh):
    placed = (P(("groups", "loop", "rep"), "enc"), P("enc", None), P("groups"), P("groups"))
    return jax.shard_map(
        body,
        mesh=mesh,
        in_specs=placed,
        out_specs=(P(("groups", "loop", "rep"), "enc"), P(("groups", "enc"), None)),
        check_vma=False,
    )
```

```python
import functools

import jax
import jax.numpy as jnp
from jax import lax
from jax.experimental import pallas as pl
from jax.experimental.pallas import tpu as pltpu
from jax.sharding import PartitionSpec as P

EPSILON = 1e-06
PARTS = 6
CHUNKS = 2
VMEM_BYTES = 60 * 1024 * 1024
MESH_ID = pl.DeviceIdType.MESH


def kernel(
    sizes,
    emb_ref,
    head_ref,
    gp_hbm,
    counts_hbm,
    embed_out,
    head_out,
    gp_ref,
    counts_ref,
    e_all,
    w_all,
    f_own,
    n_own,
    accum,
    quot,
    h_own,
    h_core,
    h_recv,
    h_send,
    h_side,
    h_full,
    e_recv,
    z_send,
    x_send,
    c_send,
    w_send,
    w_recv,
    wy_send,
    wc_send,
    wc_recv,
    in_sem,
    hc_send,
    hc_recv,
    hi_send,
    hi_recv,
    ho_send,
    hf_send,
    hf_recv,
):
    nz, nx, nc, ng = sizes
    z = lax.axis_index("loop")
    x = lax.axis_index("enc")
    c = lax.axis_index("rep")
    g = lax.axis_index("groups")
    other = 1 - c
    rows, cols = e_all.shape[3:]
    piece = rows // CHUNKS
    quarter, feats = w_all.shape[3:]
    half = quarter * ng
    width = feats // PARTS
    has_left = z > 0
    has_right = z < nz - 1

    def x_peer(j):
        return lax.rem(x + 1 + j, nx)

    def remote(src, dst, send, recv, device):
        return pltpu.make_async_remote_copy(
            src_ref=src, dst_ref=dst, send_sem=send, recv_sem=recv,
            device_id=device, device_id_type=MESH_ID,
        )

    def g_peer(i):
        return lax.rem(g + 1 + i, ng)

    def e_copy(b, cc, xx, h, send, device):
        start = h * piece if isinstance(h, int) else pl.multiple_of(h * piece, piece)
        slot = e_all.at[b, cc, xx, pl.ds(start, piece)]
        return remote(slot, slot, send, e_recv.at[b, cc, xx, h], device)

    def z_copy(b, d, h):
        return e_copy(b, c, x, h, z_send.at[d, b, h], {"loop": z + (1 if d == 0 else -1)})

    def x_copy(b, j, h):
        return e_copy(b, c, x, h, x_send.at[j, b, h], {"enc": x_peer(j)})

    def c_copy(b, xx, h):
        return e_copy(b, c, xx, h, c_send.at[b, xx, h], {"rep": other})

    def e_wait(b, cc, xx, h):
        e_copy(b, cc, xx, h, c_send.at[b, xx, h], {"rep": other}).wait_recv()

    def w_copy(xx, gg, send, device):
        slot = w_all.at[xx, c, gg]
        return remote(slot, slot, send, w_recv.at[xx, gg], device)

    def wx_copy(j):
        return w_copy(x, g, w_send.at[j], {"enc": x_peer(j)})

    def wy_copy(j, i):
        return w_copy(x_peer(j), g, wy_send.at[j, i], {"groups": g_peer(i)})

    def w_wait(xx, gg):
        w_copy(xx, gg, w_send.at[0], {"rep": other}).wait_recv()

    def wc_copy(xx, cc, gg):
        slot = w_all.at[xx, cc, gg]
        return remote(slot, slot, wc_send.at[xx, gg], wc_recv.at[xx, gg], {"rep": other})

    own_emb = pltpu.make_async_copy(emb_ref, e_all.at[z, c, x], in_sem.at[0])
    own_emb.start()
    own_head = [
        pltpu.make_async_copy(gp_hbm, gp_ref, in_sem.at[1]),
        pltpu.make_async_copy(counts_hbm, counts_ref, in_sem.at[2]),
    ]
    for copy in own_head:
        copy.start()
    for cc in range(nc):
        for gg in range(ng):
            start = (cc * ng + gg) * quarter
            own_head.append(
                pltpu.make_async_copy(
                    head_ref.at[pl.ds(start, quarter)],
                    w_all.at[x, cc, gg],
                    in_sem.at[3 + cc * ng + gg],
                )
            )
            own_head[-1].start()

    barrier = pltpu.get_barrier_semaphore()

    @pl.when(has_left)
    def _():
        pl.semaphore_signal(barrier, 1, device_id={"loop": z - 1}, device_id_type=MESH_ID)

    @pl.when(has_right)
    def _():
        pl.semaphore_signal(barrier, 1, device_id={"loop": z + 1}, device_id_type=MESH_ID)

    for j in range(nx - 1):
        pl.semaphore_signal(barrier, 1, device_id={"enc": x_peer(j)}, device_id_type=MESH_ID)
    pl.semaphore_signal(barrier, 1, device_id={"rep": other}, device_id_type=MESH_ID)

    for i in range(ng - 1):
        pl.semaphore_signal(barrier, 1, device_id={"groups": g_peer(i)}, device_id_type=MESH_ID)
    accum[...] = jnp.zeros_like(accum)
    quot[...] = jnp.zeros_like(quot)

    pl.semaphore_wait(
        barrier, nx + ng - 1 + has_left.astype(jnp.int32) + has_right.astype(jnp.int32)
    )
    own_emb.wait()
    for copy in own_head:
        copy.wait()
    for j in range(nx - 1):
        wx_copy(j).start()

    def features(b, cc):
        total = jnp.dot(
            e_all[b, cc, 0], w_all[0].reshape(cols, feats),
            preferred_element_type=jnp.float32,
        )
        for xx in range(1, nx):
            total = total + jnp.dot(
                e_all[b, cc, xx], w_all[xx].reshape(cols, feats),
                preferred_element_type=jnp.float32,
            )
        total = total.astype(jnp.bfloat16)
        wide = total.astype(jnp.float32)
        return total, jnp.sum(wide * wide, axis=1, keepdims=True)

    def eye():
        return lax.broadcasted_iota(jnp.int32, (rows, rows), 0) == lax.broadcasted_iota(
            jnp.int32, (rows, rows), 1
        )

    def weight_row(b, cc):
        place = cc * rows + lax.broadcasted_iota(jnp.int32, (1, rows), 1)
        lanes = gp_ref.shape[1]
        split = rows // lanes
        first = (b * nc + cc) * split
        held = [gp_ref[pl.ds(first + i, 1), :] for i in range(split)]
        return jnp.where(place < counts_ref[b], jnp.concatenate(held, axis=1), 0.0)

    def tile(b, cc, feat, norm):
        norm_row = jnp.sum(jnp.where(eye(), norm, 0.0), axis=0, keepdims=True)
        scores = lax.dot_general(
            f_own[...], feat, (((1,), (1,)), ((), ())), preferred_element_type=jnp.float32
        )
        both = n_own[...] + norm_row
        denom = both - scores + EPSILON
        scaled = weight_row(b, cc) * (1.0 / (denom * denom))
        quot[...] += jnp.sum(scaled * scores, axis=1, keepdims=True)
        accum[...] += jnp.dot(
            (both * scaled).astype(jnp.bfloat16), feat, preferred_element_type=jnp.float32
        )

    def at_step(s, d):
        b = z - s if d == 0 else z + s
        return b, jnp.logical_and(jnp.logical_and(b >= 0, b < nz), s >= (1 if d else 0))

    def stage_z(u, d):
        s, h = u // CHUNKS, lax.rem(u, CHUNKS)
        b, valid = at_step(s, d)

        @pl.when(valid)
        def _():
            @pl.when(s > 0)
            def _():
                e_wait(b, c, x, h)

            @pl.when(has_right if d == 0 else has_left)
            def _():
                z_copy(b, d, h).start()

            if d == 0:
                @pl.when(jnp.logical_and(s == 0, has_left))
                def _():
                    z_copy(b, 1, h).start()

            for j in range(nx - 1):
                x_copy(b, j, h).start()
            c_copy(b, x, h).start()

    def stage_x(u, d):
        s, h = u // CHUNKS, lax.rem(u, CHUNKS)
        b, valid = at_step(s, d)

        @pl.when(valid)
        def _():
            for j in range(nx - 1):
                e_wait(b, c, x_peer(j), h)
                c_copy(b, x_peer(j), h).start()

    def stage_w():
        for j in range(nx - 1):
            w_wait(x_peer(j), g)
            for i in range(ng - 1):
                wy_copy(j, i).start()
            wc_copy(x_peer(j), c, g).start()

    def stage_first():
        for j in range(nx - 1):
            for i in range(ng - 1):
                w_wait(x_peer(j), g_peer(i))
                wc_copy(x_peer(j), c, g_peer(i)).start()
        for j in range(nx - 1):
            for gg in range(ng):
                wc_copy(x_peer(j), other, gg).wait_recv()
        feat, norm = features(z, c)
        f_own[...] = feat
        n_own[...] = norm

    def stage_c(s, d):
        b, valid = at_step(s, d)

        @pl.when(valid)
        def _():
            for h in range(CHUNKS):
                for xx in range(nx):
                    e_wait(b, other, xx, h)

            @pl.loop(0, nc)
            def _(cc):
                feat, norm = features(b, cc)
                tile(b, cc, feat, norm)

    steps = nz * CHUNKS
    x_lag = 3
    c_lag = 3 + CHUNKS

    @pl.loop(0, steps + c_lag - 1)
    def _(t):
        @pl.when(t < steps)
        def _():
            stage_z(t, 0)
            stage_z(t, 1)

        @pl.when(t == 2)
        def _():
            stage_w()

        @pl.when(t == c_lag)
        def _():
            stage_first()

        @pl.when(jnp.logical_and(t >= c_lag, lax.rem(t - c_lag + CHUNKS, CHUNKS) == 0))
        def _():
            stage_c((t - c_lag) // CHUNKS, 0)
            stage_c((t - c_lag) // CHUNKS, 1)

        @pl.when(jnp.logical_and(t >= x_lag, t < steps + x_lag))
        def _():
            stage_x(t - x_lag, 0)
            stage_x(t - x_lag, 1)

    own_weight = jnp.sum(jnp.where(eye(), weight_row(z, c), 0.0), axis=1, keepdims=True)
    grad = (
        own_weight * (accum[...] - f_own[...].astype(jnp.float32) * (2.0 * quot[...]))
    ).astype(jnp.bfloat16)
    f_own[...] = grad

    middle = nz // 2
    left_side = z < middle
    inward = jnp.where(left_side, z + 1, z - 1)
    outward = jnp.where(left_side, z - 1, z + 1)
    is_middle = jnp.logical_or(z == middle - 1, z == middle)
    is_outer = jnp.logical_or(z == 0, z == nz - 1)
    spot = is_middle.astype(jnp.int32)

    def hc_copy(k):
        return remote(
            h_core.at[k], h_recv.at[k], hc_send.at[k], hc_recv.at[k], {"rep": other}
        )

    def hi_copy(k):
        return remote(
            h_send.at[k], h_side.at[spot, k], hi_send.at[k], hi_recv.at[spot, k],
            {"loop": inward},
        )

    def hi_wait(place, k):
        remote(
            h_send.at[k], h_side.at[place, k], hi_send.at[k], hi_recv.at[place, k],
            {"loop": inward},
        ).wait_recv()

    def ho_copy(k):
        slot = h_full.at[c, k]
        return remote(slot, slot, ho_send.at[k], hf_recv.at[c, k], {"loop": outward})

    def hf_copy(k):
        slot = h_full.at[c, k]
        return remote(slot, slot, hf_send.at[k], hf_recv.at[c, k], {"rep": other})

    for k in range(PARTS):
        part = lax.dot_general(
            e_all[z, c, x], f_own[:, k * width : (k + 1) * width], (((0,), (0,)), ((), ())),
            preferred_element_type=jnp.float32,
        )
        h_full_part = part.reshape(nc, half, width)

        @pl.when(c == 0)
        def _():
            h_own[k] = h_full_part[0]
            h_core[k] = h_full_part[1].astype(jnp.bfloat16)

        @pl.when(c == 1)
        def _():
            h_own[k] = h_full_part[1]
            h_core[k] = h_full_part[0].astype(jnp.bfloat16)

        hc_copy(k).start()

    for k in range(PARTS):
        hc_copy(k).wait_recv()
        h_own[k] = h_own[k] + h_recv[k].astype(jnp.float32)

        @pl.when(is_outer)
        def _():
            h_send[k] = h_own[k].astype(jnp.bfloat16)
            hi_copy(k).start()

    for k in range(PARTS):
        @pl.when(jnp.logical_not(is_outer))
        def _():
            hi_wait(0, k)
            h_send[k] = (h_own[k] + h_side[0, k].astype(jnp.float32)).astype(jnp.bfloat16)
            hi_copy(k).start()

    embed_out[...] = lax.dot_general(
        f_own[...], w_all[x].reshape(cols, feats), (((1,), (1,)), ((), ())), preferred_element_type=jnp.float32
    ).astype(jnp.bfloat16)

    for k in range(PARTS):
        @pl.when(is_middle)
        def _():
            hi_wait(1, k)
            h_full[c, k] = (
                h_send[k].astype(jnp.float32) + h_side[1, k].astype(jnp.float32)
            ).astype(jnp.bfloat16)

        @pl.when(jnp.logical_not(is_middle))
        def _():
            ho_copy(k).wait_recv()

        @pl.when(jnp.logical_not(is_outer))
        def _():
            ho_copy(k).start()

        hf_copy(k).start()

    for k in range(PARTS):
        slot = h_full.at[other, k]
        remote(slot, slot, hf_send.at[k], hf_recv.at[other, k], {"rep": other}).wait_recv()
    head_out[...] = h_full[...]

    @pl.loop(0, nz)
    def _(b):
        for h in range(CHUNKS):
            @pl.when(jnp.logical_and(b <= z, has_right))
            def _():
                z_copy(b, 0, h).wait_send()

            @pl.when(jnp.logical_and(b >= z, has_left))
            def _():
                z_copy(b, 1, h).wait_send()

            for j in range(nx - 1):
                x_copy(b, j, h).wait_send()
            for xx in range(nx):
                c_copy(b, xx, h).wait_send()

    for j in range(nx - 1):
        wx_copy(j).wait_send()
        for i in range(ng - 1):
            wy_copy(j, i).wait_send()
        for gg in range(ng):
            wc_copy(x_peer(j), c, gg).wait_send()
    for k in range(PARTS):
        hc_copy(k).wait_send()
        hi_copy(k).wait_send()
        hf_copy(k).wait_send()

        @pl.when(jnp.logical_not(is_outer))
        def _():
            ho_copy(k).wait_send()


def finish(embed_ref, head_ref, embed_out, head_out):
    cores, parts, half, width = head_ref.shape
    embed_out[...] = embed_ref[...]
    for cc in range(cores):
        for k in range(parts):
            head_out[cc * half : (cc + 1) * half, k * width : (k + 1) * width] = head_ref[
                cc, k
            ].astype(jnp.float32)


def ring_body(embeddings, head_weight, gp_weights, counts):
    nz, nx, nc, ng = (lax.axis_size(name) for name in ("loop", "enc", "rep", "groups"))
    rows, cols = embeddings.shape
    feats = head_weight.shape[1]
    half, width = cols // nc, feats // PARTS
    if half % (16 * ng):
        raise ValueError("head rows")
    gp_rows = gp_weights.reshape(-1, 128)
    vmem = pl.BlockSpec(memory_space=pltpu.VMEM)
    hbm = pl.BlockSpec(memory_space=pltpu.HBM)
    dma = pltpu.SemaphoreType.DMA
    embed_grad, head_sum = pl.pallas_call(
        functools.partial(kernel, (nz, nx, nc, ng)),
        out_shape=(
            jax.ShapeDtypeStruct((rows, cols), jnp.bfloat16),
            jax.ShapeDtypeStruct((nc, PARTS, half, width), jnp.bfloat16),
        ),
        in_specs=[hbm, hbm, hbm, hbm],
        out_specs=(vmem, vmem),
        scratch_shapes=[
            pltpu.VMEM(gp_rows.shape, jnp.float32),
            pltpu.SMEM(counts.shape, jnp.int32),
            pltpu.VMEM((nz, nc, nx, rows, cols), jnp.bfloat16),
            pltpu.VMEM((nx, nc, ng, half // ng, feats), jnp.bfloat16),
            pltpu.VMEM((rows, feats), jnp.bfloat16),
            pltpu.VMEM((rows, 1), jnp.float32),
            pltpu.VMEM((rows, feats), jnp.float32),
            pltpu.VMEM((rows, 1), jnp.float32),
            pltpu.VMEM((PARTS, half, width), jnp.float32),
            pltpu.VMEM((PARTS, half, width), jnp.bfloat16),
            pltpu.VMEM((PARTS, half, width), jnp.bfloat16),
            pltpu.VMEM((PARTS, half, width), jnp.bfloat16),
            pltpu.VMEM((2, PARTS, half, width), jnp.bfloat16),
            pltpu.VMEM((nc, PARTS, half, width), jnp.bfloat16),
            dma((nz, nc, nx, CHUNKS)),
            dma((2, nz, CHUNKS)),
            dma((nx - 1, nz, CHUNKS)),
            dma((nz, nx, CHUNKS)),
            dma((nx - 1,)),
            dma((nx, ng)),
            dma((nx - 1, max(ng - 1, 1))),
            dma((nx, ng)),
            dma((nx, ng)),
            dma((3 + nc * ng,)),
            dma((PARTS,)),
            dma((PARTS,)),
            dma((PARTS,)),
            dma((2, PARTS)),
            dma((PARTS,)),
            dma((PARTS,)),
            dma((nc, PARTS)),
        ],
        compiler_params=pltpu.CompilerParams(
            collective_id=0, has_side_effects=True, vmem_limit_bytes=VMEM_BYTES
        ),
    )(embeddings, head_weight, gp_rows, counts)
    return pl.pallas_call(
        finish,
        out_shape=(
            jax.ShapeDtypeStruct((rows, cols), jnp.bfloat16),
            jax.ShapeDtypeStruct((cols, feats), jnp.float32),
        ),
        in_specs=[vmem, vmem],
        out_specs=(vmem, vmem),
        compiler_params=pltpu.CompilerParams(vmem_limit_bytes=VMEM_BYTES),
    )(embed_grad, head_sum)


LINE = 4
PIECES = 4
STRIPS = 3
COLUMNS = 2


def line_kernel(
    emb_ref,
    head_ref,
    gp_hbm,
    counts_hbm,
    embed_out,
    own_out,
    peer_out,
    gp_ref,
    counts_ref,
    e_all,
    w_all,
    f_all,
    n_row,
    n_col,
    w_row,
    accum,
    quot,
    grads,
    early_sum,
    w_col,
    e_turned,
    in_sem,
    e_send,
    e_recv,
    w_send,
    w_recv,
    f_send,
    f_recv,
    n_send,
    n_recv,
    h_send,
    h_recv,
):
    nz, nc = LINE, 2
    z = lax.axis_index("loop")
    x = lax.axis_index("enc")
    c = lax.axis_index("rep")
    g = lax.axis_index("groups")
    rows, cols = e_all.shape[2:]
    piece = rows // PIECES
    quarter, feats = w_all.shape[3:]
    block = nc * rows
    lanes = gp_ref.shape[1]
    inward = jnp.where(z < nz // 2, 1, -1)
    is_end = jnp.logical_or(z == 0, z == nz - 1)
    is_mid = jnp.logical_not(is_end)
    near = z + inward
    outer = z - inward
    second = z + 2 * inward
    third = z + 3 * inward
    x_dev, c_dev, g_dev = {"enc": 1 - x}, {"rep": 1 - c}, {"groups": 1 - g}

    def remote(src, dst, send, recv, device):
        return pltpu.make_async_remote_copy(
            src_ref=src, dst_ref=dst, send_sem=send, recv_sem=recv,
            device_id=device, device_id_type=MESH_ID,
        )

    def e_copy(side, b, h, kind, device):
        slot = e_all.at[side, b, pl.ds(h * piece, piece)]
        return remote(slot, slot, e_send.at[kind, h], e_recv.at[side, b, h], device)

    def e_wait(side, b, h):
        e_copy(side, b, h, 0, x_dev).wait_recv()

    def w_copy(cc, gg, p, kind, device, side=1 - x):
        strip = quarter // STRIPS
        slot = w_all.at[side, cc, gg, pl.ds(p * strip, strip)]
        return remote(slot, slot, w_send.at[kind, p], w_recv.at[cc, gg, p], device)

    def f_copy(b, cc):
        slot = f_all.at[b, cc]
        return remote(slot, slot, f_send.at[b], f_recv.at[b], c_dev)

    def n_copy(b, cc):
        slot = n_row.at[b, cc]
        return remote(slot, slot, n_send.at[b], n_recv.at[b], c_dev)

    barrier = pltpu.get_barrier_semaphore()

    def greet(device):
        pl.semaphore_signal(barrier, 1, device_id=device, device_id_type=MESH_ID)

    greet(x_dev)
    greet(c_dev)
    greet(g_dev)
    greet({"loop": near})

    @pl.when(is_mid)
    def _():
        greet({"loop": outer})

    own_emb = pltpu.make_async_copy(emb_ref, e_all.at[x, z], in_sem.at[0])
    own_emb.start()
    loads = []
    for cc in range(nc):
        for gg in range(2):
            loads.append(
                pltpu.make_async_copy(
                    head_ref.at[pl.ds((cc * 2 + gg) * quarter, quarter)],
                    w_all.at[x, cc, gg],
                    in_sem.at[3 + cc * 2 + gg],
                )
            )
    loads.append(pltpu.make_async_copy(gp_hbm, gp_ref, in_sem.at[1]))
    loads.append(pltpu.make_async_copy(counts_hbm, counts_ref, in_sem.at[2]))
    for copy in loads:
        copy.start()

    own_emb.wait()
    for copy in loads[:4]:
        copy.wait()
    pl.semaphore_wait(barrier, 4 + is_mid.astype(jnp.int32))

    for p in range(STRIPS):
        w_copy(c, g, p, 0, x_dev, x).start()
    for h in range(PIECES):
        e_copy(x, z, h, 0, {"loop": near}).start()

    @pl.when(is_mid)
    def _():
        for h in range(4):
            e_copy(x, z, h, 1, {"loop": outer}).start()


    fourth = jnp.where(is_end, second, outer)
    last = jnp.where(is_end, third, second)
    half = rows // 2
    parts = [
        [(z, 0), (z, 1)],
        [(fourth, 0), (fourth, 1)],
        [(near, 0), (last, 0)],
        [(near, 1), (last, 1)],
    ]

    for copy in loads[4:]:
        copy.wait()
    accum[...] = jnp.zeros_like(accum)
    quot[...] = jnp.zeros_like(quot)
    inside = lax.broadcasted_iota(jnp.int32, (1, lanes), 1)
    for v in range(nz):
        for cc in range(nc):
            for k, (b, h) in enumerate(parts[v]):
                place = cc * rows + h * half
                held = gp_ref[pl.ds(b * (block // lanes) + place // lanes, 1), :]
                w_row[v, cc, :, k * half : (k + 1) * half] = jnp.where(
                    inside + place < counts_ref[b], held, 0.0
                )

    def eye():
        return lax.broadcasted_iota(jnp.int32, (rows, rows), 0) == lax.broadcasted_iota(
            jnp.int32, (rows, rows), 1
        )

    def taken(side, v):
        return jnp.concatenate(
            [e_all[side, b, h * half : (h + 1) * half] for b, h in parts[v]], axis=0
        )

    def early(b, places):
        made = jnp.dot(
            e_all[x, b], w_all[x].reshape(cols, feats), preferred_element_type=jnp.float32
        )
        for h, (v, k) in enumerate(places):
            own = slice(h * half, (h + 1) * half)
            early_sum[v, k * half : (k + 1) * half] = made[own]
            spot = v * rows + k * half
            e_turned[:, spot : spot + half] = e_all[x, b, own].T

    early(z, [(0, 0), (0, 1)])
    for v in range(nz):
        column = jnp.sum(jnp.where(eye(), w_row[v, c], 0.0), axis=1, keepdims=True)
        w_col[v] = jnp.broadcast_to(column, (rows, lanes))

    for p in range(STRIPS):
        w_copy(c, g, p, 0, x_dev, x).wait_send()
        if p == STRIPS - 1:
            for h in range(PIECES):
                e_copy(x, z, h, 2, x_dev).start()

    def x_strip(p):
        w_copy(c, g, p, 0, x_dev).wait_recv()
        w_copy(c, g, p, 1, g_dev).start()
        w_copy(c, g, p, 2, c_dev).start()

    def g_strip(p):
        w_copy(c, 1 - g, p, 1, g_dev).wait_recv()
        w_copy(c, 1 - g, p, 3, c_dev).start()

    @pl.when(is_mid)
    def _():
        for h in range(max(PIECES, STRIPS)):
            if h < STRIPS:
                x_strip(h)
            if h < PIECES:
                e_wait(x, outer, h)
                e_copy(x, outer, h, 3, {"loop": near}).start()
                e_wait(x, near, h)
                e_copy(x, near, h, 4, {"loop": outer}).start()
        early(near, [(2, 0), (3, 0)])
        for p in range(STRIPS):
            g_strip(p)
        for h in range(PIECES):
            e_wait(x, second, h)
            e_copy(x, second, h, 5, {"loop": outer}).start()
            e_copy(x, second, h, 6, x_dev).start()
        for h in range(PIECES):
            e_wait(1 - x, z, h)
            e_copy(1 - x, z, h, 7, {"loop": outer}).start()
            e_copy(1 - x, z, h, 8, {"loop": near}).start()

    @pl.when(is_end)
    def _():
        for p in range(STRIPS):
            x_strip(p)
        for h in range(PIECES):
            e_wait(x, near, h)
        early(near, [(2, 0), (3, 0)])
        for h in range(PIECES + 1):
            if h < PIECES:
                e_wait(1 - x, z, h)
                e_copy(1 - x, z, h, 3, {"loop": near}).start()
            if h < STRIPS:
                g_strip(h)
            if h > 0:
                e_wait(x, second, h - 1)
                e_copy(x, second, h - 1, 4, x_dev).start()

    for p in range(STRIPS):
        w_copy(1 - c, g, p, 2, c_dev).wait_recv()
        w_copy(1 - c, 1 - g, p, 3, c_dev).wait_recv()

    def features(v):
        total = early_sum[v] + jnp.dot(
            taken(1 - x, v), w_all[1 - x].reshape(cols, feats),
            preferred_element_type=jnp.float32,
        )
        held = total.astype(jnp.bfloat16)
        f_all[v, c] = held
        f_copy(v, c).start()
        return held

    def norms(v, held):
        wide = held.astype(jnp.float32)
        norm = jnp.sum(wide * wide, axis=1, keepdims=True)
        n_col[v] = jnp.broadcast_to(norm, (rows, lanes))
        n_row[v, c] = jnp.sum(jnp.where(eye(), norm, 0.0), axis=0, keepdims=True)
        n_copy(v, c).start()

    def scores_of(i, j):
        return lax.dot_general(
            f_all[i, c], f_all[j].reshape(block, feats), (((1,), (1,)), ((), ())),
            preferred_element_type=jnp.float32,
        )

    def wide_row(ref, j):
        return jnp.concatenate([ref[j, cc] for cc in range(nc)], axis=1)

    def pairs(i, j, scores):
        spread = block // lanes
        left = jnp.concatenate([n_col[i]] * spread, axis=1)
        both = left + wide_row(n_row, j)
        denom = (both - scores) + EPSILON
        scaled = wide_row(w_row, j) * (1.0 / (denom * denom))
        part = scaled * scores
        total = part[:, :lanes]
        for k in range(1, spread):
            total = total + part[:, k * lanes : (k + 1) * lanes]
        quot[i] += total
        return (both * scaled).astype(jnp.bfloat16)

    def finalize(i, carried):
        quotient = 2.0 * jnp.sum(quot[i], axis=1, keepdims=True)
        own_weight = jnp.concatenate([w_col[i]] * (feats // lanes), axis=1)
        grads[i] = (
            own_weight * (carried - f_all[i, c].astype(jnp.float32) * quotient)
        ).astype(jnp.bfloat16)

    def tiles(todo, final=False, between=None):
        scores = scores_of(*todo[0])
        if between is not None:
            norms(*between)
        for k, (i, j) in enumerate(todo):
            following = scores_of(*todo[k + 1]) if k + 1 < len(todo) else None
            weight = pairs(i, j, scores)
            carried = accum[i] + jnp.dot(
                weight, f_all[j].reshape(block, feats), preferred_element_type=jnp.float32
            )
            if final and j == nz - 1:
                finalize(i, carried)
            else:
                accum[i] = carried
            scores = following

    def third_pass(some):
        @pl.when(is_end)
        def _():
            for h in some:
                e_wait(x, third, h)
                e_copy(x, third, h, 5, x_dev).start()

    def quarter_of(k):
        return range(k * PIECES // 4, (k + 1) * PIECES // 4)

    def meet(v):
        f_copy(v, 1 - c).wait_recv()
        n_copy(v, 1 - c).wait_recv()

    norms(0, features(0))
    third_pass(quarter_of(0))
    early(fourth, [(1, 0), (1, 1)])
    meet(0)
    tiles([(0, 0)])
    third_pass(quarter_of(1))
    for h in range(PIECES):
        e_wait(1 - x, fourth, h)
    held = features(1)
    third_pass(quarter_of(2))
    tiles([(1, 0)], between=(1, held))
    third_pass(quarter_of(3))
    early(last, [(2, 1), (3, 1)])
    meet(1)
    tiles([(0, 1), (1, 1)])
    for v in (2, 3):
        start = (v - 2) * (PIECES // 2)
        for h in range(start, start + PIECES // 2):
            e_wait(1 - x, near, h)
            e_wait(1 - x, last, h)
        held = features(v)
        tiles([(v, j) for j in range(v)], between=(v, held))
        meet(v)
        tiles([(i, v) for i in range(v + 1)], v == 3)

    width = feats // COLUMNS

    def h_copy(k):
        return remote(
            own_out.at[k], peer_out.at[k], h_send.at[k], h_recv.at[k], c_dev
        )

    for k in range(COLUMNS):
        own_out[k] = jnp.dot(
            e_turned[...],
            grads[:, :, k * width : (k + 1) * width].reshape(nz * rows, width),
            preferred_element_type=jnp.float32,
        ).astype(jnp.bfloat16)
        h_copy(k).start()

    embed_out[...] = lax.dot_general(
        grads[0], w_all[x].reshape(cols, feats), (((1,), (1,)), ((), ())),
        preferred_element_type=jnp.float32,
    ).astype(jnp.bfloat16)

    for p in range(STRIPS):
        for kind, device in ((1, g_dev), (2, c_dev), (3, c_dev)):
            w_copy(c, g, p, kind, device).wait_send()
    for b in range(nz):
        f_copy(b, c).wait_send()
        n_copy(b, c).wait_send()
    for h in range(PIECES):
        for kind in (0, 2, 3, 4, 5):
            e_copy(x, z, h, kind, x_dev).wait_send()

        @pl.when(is_mid)
        def _():
            for kind in (1, 6, 7, 8):
                e_copy(x, z, h, kind, x_dev).wait_send()

    for k in range(COLUMNS):
        h_copy(k).wait()


def line_finish(embed_ref, own_ref, peer_ref, embed_out, head_out):
    parts, _, width = own_ref.shape
    embed_out[...] = embed_ref[...]
    for k in range(parts):
        head_out[:, k * width : (k + 1) * width] = own_ref[k].astype(
            jnp.float32
        ) + peer_ref[k].astype(jnp.float32)


def line_body(embeddings, head_weight, gp_weights, counts):
    nz, nc, nx, ng = LINE, 2, 2, 2
    rows, cols = embeddings.shape
    feats = head_weight.shape[1]
    quarter, width = cols // (nc * ng), feats // COLUMNS
    lanes = 128
    gp_rows = gp_weights.reshape(-1, lanes)
    vmem = pl.BlockSpec(memory_space=pltpu.VMEM)
    hbm = pl.BlockSpec(memory_space=pltpu.HBM)
    dma = pltpu.SemaphoreType.DMA
    part = pltpu.VMEM((COLUMNS, cols, width), jnp.bfloat16)
    embed_grad, own, peer = pl.pallas_call(
        line_kernel,
        out_shape=(pltpu.VMEM((rows, cols), jnp.bfloat16), part, part),
        in_specs=[hbm, hbm, hbm, hbm],
        out_specs=(vmem, vmem, vmem),
        scratch_shapes=[
            pltpu.VMEM(gp_rows.shape, jnp.float32),
            pltpu.SMEM(counts.shape, jnp.int32),
            pltpu.VMEM((nx, nz, rows, cols), jnp.bfloat16),
            pltpu.VMEM((nx, nc, ng, quarter, feats), jnp.bfloat16),
            pltpu.VMEM((nz, nc, rows, feats), jnp.bfloat16),
            pltpu.VMEM((nz, nc, 1, rows), jnp.float32),
            pltpu.VMEM((nz, rows, lanes), jnp.float32),
            pltpu.VMEM((nz, nc, 1, rows), jnp.float32),
            pltpu.VMEM((nz, rows, feats), jnp.float32),
            pltpu.VMEM((nz, rows, lanes), jnp.float32),
            pltpu.VMEM((nz, rows, feats), jnp.bfloat16),
            pltpu.VMEM((nz, rows, feats), jnp.float32),
            pltpu.VMEM((nz, rows, lanes), jnp.float32),
            pltpu.VMEM((cols, nz * rows), jnp.bfloat16),
            dma((3 + nc * ng,)),
            dma((9, PIECES)),
            dma((nx, nz, PIECES)),
            dma((4, STRIPS)),
            dma((nc, ng, STRIPS)),
            dma((nz,)),
            dma((nz,)),
            dma((nz,)),
            dma((nz,)),
            dma((COLUMNS,)),
            dma((COLUMNS,)),
        ],
        compiler_params=pltpu.CompilerParams(
            collective_id=0, has_side_effects=True, vmem_limit_bytes=VMEM_BYTES
        ),
    )(embeddings, head_weight, gp_rows, counts)
    embed_grad, own, peer = (
        pltpu.with_memory_space_constraint(held, pltpu.VMEM)
        for held in (embed_grad, own, peer)
    )
    return pl.pallas_call(
        line_finish,
        out_shape=(
            jax.ShapeDtypeStruct((rows, cols), jnp.bfloat16),
            jax.ShapeDtypeStruct((cols, feats), jnp.float32),
        ),
        in_specs=[vmem, vmem, vmem],
        out_specs=(vmem, vmem),
        compiler_params=pltpu.CompilerParams(vmem_limit_bytes=VMEM_BYTES),
    )(embed_grad, own, peer)


def body(*args):
    sizes = tuple(lax.axis_size(name) for name in ("loop", "enc", "rep", "groups"))
    return line_body(*args) if sizes == (LINE, 2, 2, 2) else ring_body(*args)


def solution(mesh):
    placed = (P(("groups", "loop", "rep"), "enc"), P("enc", None), P("groups"), P("groups"))
    return jax.shard_map(
        body,
        mesh=mesh,
        in_specs=placed,
        out_specs=(P(("groups", "loop", "rep"), "enc"), P(("groups", "enc"), None)),
        check_vma=False,
    )
```

```python
import functools

import jax
import jax.numpy as jnp
from jax import lax
from jax.experimental import pallas as pl
from jax.experimental.pallas import tpu as pltpu
from jax.sharding import PartitionSpec as P

EPSILON = 1e-06
PARTS = 6
CHUNKS = 2
VMEM_BYTES = 60 * 1024 * 1024
MESH_ID = pl.DeviceIdType.MESH


def kernel(
    sizes,
    emb_ref,
    head_ref,
    gp_hbm,
    counts_hbm,
    embed_out,
    head_out,
    gp_ref,
    counts_ref,
    e_all,
    w_all,
    f_own,
    n_own,
    accum,
    quot,
    h_own,
    h_core,
    h_recv,
    h_send,
    h_side,
    h_full,
    e_recv,
    z_send,
    x_send,
    c_send,
    w_send,
    w_recv,
    wy_send,
    wc_send,
    wc_recv,
    in_sem,
    hc_send,
    hc_recv,
    hi_send,
    hi_recv,
    ho_send,
    hf_send,
    hf_recv,
):
    nz, nx, nc, ng = sizes
    z = lax.axis_index("loop")
    x = lax.axis_index("enc")
    c = lax.axis_index("rep")
    g = lax.axis_index("groups")
    other = 1 - c
    rows, cols = e_all.shape[3:]
    piece = rows // CHUNKS
    quarter, feats = w_all.shape[3:]
    half = quarter * ng
    width = feats // PARTS
    has_left = z > 0
    has_right = z < nz - 1

    def x_peer(j):
        return lax.rem(x + 1 + j, nx)

    def remote(src, dst, send, recv, device):
        return pltpu.make_async_remote_copy(
            src_ref=src, dst_ref=dst, send_sem=send, recv_sem=recv,
            device_id=device, device_id_type=MESH_ID,
        )

    def g_peer(i):
        return lax.rem(g + 1 + i, ng)

    def e_copy(b, cc, xx, h, send, device):
        start = h * piece if isinstance(h, int) else pl.multiple_of(h * piece, piece)
        slot = e_all.at[b, cc, xx, pl.ds(start, piece)]
        return remote(slot, slot, send, e_recv.at[b, cc, xx, h], device)

    def z_copy(b, d, h):
        return e_copy(b, c, x, h, z_send.at[d, b, h], {"loop": z + (1 if d == 0 else -1)})

    def x_copy(b, j, h):
        return e_copy(b, c, x, h, x_send.at[j, b, h], {"enc": x_peer(j)})

    def c_copy(b, xx, h):
        return e_copy(b, c, xx, h, c_send.at[b, xx, h], {"rep": other})

    def e_wait(b, cc, xx, h):
        e_copy(b, cc, xx, h, c_send.at[b, xx, h], {"rep": other}).wait_recv()

    def w_copy(xx, gg, send, device):
        slot = w_all.at[xx, c, gg]
        return remote(slot, slot, send, w_recv.at[xx, gg], device)

    def wx_copy(j):
        return w_copy(x, g, w_send.at[j], {"enc": x_peer(j)})

    def wy_copy(j, i):
        return w_copy(x_peer(j), g, wy_send.at[j, i], {"groups": g_peer(i)})

    def w_wait(xx, gg):
        w_copy(xx, gg, w_send.at[0], {"rep": other}).wait_recv()

    def wc_copy(xx, cc, gg):
        slot = w_all.at[xx, cc, gg]
        return remote(slot, slot, wc_send.at[xx, gg], wc_recv.at[xx, gg], {"rep": other})

    own_emb = pltpu.make_async_copy(emb_ref, e_all.at[z, c, x], in_sem.at[0])
    own_emb.start()
    own_head = [
        pltpu.make_async_copy(gp_hbm, gp_ref, in_sem.at[1]),
        pltpu.make_async_copy(counts_hbm, counts_ref, in_sem.at[2]),
    ]
    for copy in own_head:
        copy.start()
    for cc in range(nc):
        for gg in range(ng):
            start = (cc * ng + gg) * quarter
            own_head.append(
                pltpu.make_async_copy(
                    head_ref.at[pl.ds(start, quarter)],
                    w_all.at[x, cc, gg],
                    in_sem.at[3 + cc * ng + gg],
                )
            )
            own_head[-1].start()

    barrier = pltpu.get_barrier_semaphore()

    @pl.when(has_left)
    def _():
        pl.semaphore_signal(barrier, 1, device_id={"loop": z - 1}, device_id_type=MESH_ID)

    @pl.when(has_right)
    def _():
        pl.semaphore_signal(barrier, 1, device_id={"loop": z + 1}, device_id_type=MESH_ID)

    for j in range(nx - 1):
        pl.semaphore_signal(barrier, 1, device_id={"enc": x_peer(j)}, device_id_type=MESH_ID)
    pl.semaphore_signal(barrier, 1, device_id={"rep": other}, device_id_type=MESH_ID)

    for i in range(ng - 1):
        pl.semaphore_signal(barrier, 1, device_id={"groups": g_peer(i)}, device_id_type=MESH_ID)
    accum[...] = jnp.zeros_like(accum)
    quot[...] = jnp.zeros_like(quot)

    pl.semaphore_wait(
        barrier, nx + ng - 1 + has_left.astype(jnp.int32) + has_right.astype(jnp.int32)
    )
    own_emb.wait()
    for copy in own_head:
        copy.wait()
    for j in range(nx - 1):
        wx_copy(j).start()

    def features(b, cc):
        total = jnp.dot(
            e_all[b, cc, 0], w_all[0].reshape(cols, feats),
            preferred_element_type=jnp.float32,
        )
        for xx in range(1, nx):
            total = total + jnp.dot(
                e_all[b, cc, xx], w_all[xx].reshape(cols, feats),
                preferred_element_type=jnp.float32,
            )
        total = total.astype(jnp.bfloat16)
        wide = total.astype(jnp.float32)
        return total, jnp.sum(wide * wide, axis=1, keepdims=True)

    def eye():
        return lax.broadcasted_iota(jnp.int32, (rows, rows), 0) == lax.broadcasted_iota(
            jnp.int32, (rows, rows), 1
        )

    def weight_row(b, cc):
        place = cc * rows + lax.broadcasted_iota(jnp.int32, (1, rows), 1)
        lanes = gp_ref.shape[1]
        split = rows // lanes
        first = (b * nc + cc) * split
        held = [gp_ref[pl.ds(first + i, 1), :] for i in range(split)]
        return jnp.where(place < counts_ref[b], jnp.concatenate(held, axis=1), 0.0)

    def tile(b, cc, feat, norm):
        norm_row = jnp.sum(jnp.where(eye(), norm, 0.0), axis=0, keepdims=True)
        scores = lax.dot_general(
            f_own[...], feat, (((1,), (1,)), ((), ())), preferred_element_type=jnp.float32
        )
        both = n_own[...] + norm_row
        denom = both - scores + EPSILON
        scaled = weight_row(b, cc) * (1.0 / (denom * denom))
        quot[...] += jnp.sum(scaled * scores, axis=1, keepdims=True)
        accum[...] += jnp.dot(
            (both * scaled).astype(jnp.bfloat16), feat, preferred_element_type=jnp.float32
        )

    def at_step(s, d):
        b = z - s if d == 0 else z + s
        return b, jnp.logical_and(jnp.logical_and(b >= 0, b < nz), s >= (1 if d else 0))

    def stage_z(u, d):
        s, h = u // CHUNKS, lax.rem(u, CHUNKS)
        b, valid = at_step(s, d)

        @pl.when(valid)
        def _():
            @pl.when(s > 0)
            def _():
                e_wait(b, c, x, h)

            @pl.when(has_right if d == 0 else has_left)
            def _():
                z_copy(b, d, h).start()

            if d == 0:
                @pl.when(jnp.logical_and(s == 0, has_left))
                def _():
                    z_copy(b, 1, h).start()

            for j in range(nx - 1):
                x_copy(b, j, h).start()
            c_copy(b, x, h).start()

    def stage_x(u, d):
        s, h = u // CHUNKS, lax.rem(u, CHUNKS)
        b, valid = at_step(s, d)

        @pl.when(valid)
        def _():
            for j in range(nx - 1):
                e_wait(b, c, x_peer(j), h)
                c_copy(b, x_peer(j), h).start()

    def stage_w():
        for j in range(nx - 1):
            w_wait(x_peer(j), g)
            for i in range(ng - 1):
                wy_copy(j, i).start()
            wc_copy(x_peer(j), c, g).start()

    def stage_first():
        for j in range(nx - 1):
            for i in range(ng - 1):
                w_wait(x_peer(j), g_peer(i))
                wc_copy(x_peer(j), c, g_peer(i)).start()
        for j in range(nx - 1):
            for gg in range(ng):
                wc_copy(x_peer(j), other, gg).wait_recv()
        feat, norm = features(z, c)
        f_own[...] = feat
        n_own[...] = norm

    def stage_c(s, d):
        b, valid = at_step(s, d)

        @pl.when(valid)
        def _():
            for h in range(CHUNKS):
                for xx in range(nx):
                    e_wait(b, other, xx, h)

            @pl.loop(0, nc)
            def _(cc):
                feat, norm = features(b, cc)
                tile(b, cc, feat, norm)

    steps = nz * CHUNKS
    x_lag = 3
    c_lag = 3 + CHUNKS

    @pl.loop(0, steps + c_lag - 1)
    def _(t):
        @pl.when(t < steps)
        def _():
            stage_z(t, 0)
            stage_z(t, 1)

        @pl.when(t == 2)
        def _():
            stage_w()

        @pl.when(t == c_lag)
        def _():
            stage_first()

        @pl.when(jnp.logical_and(t >= c_lag, lax.rem(t - c_lag + CHUNKS, CHUNKS) == 0))
        def _():
            stage_c((t - c_lag) // CHUNKS, 0)
            stage_c((t - c_lag) // CHUNKS, 1)

        @pl.when(jnp.logical_and(t >= x_lag, t < steps + x_lag))
        def _():
            stage_x(t - x_lag, 0)
            stage_x(t - x_lag, 1)

    own_weight = jnp.sum(jnp.where(eye(), weight_row(z, c), 0.0), axis=1, keepdims=True)
    grad = (
        own_weight * (accum[...] - f_own[...].astype(jnp.float32) * (2.0 * quot[...]))
    ).astype(jnp.bfloat16)
    f_own[...] = grad

    middle = nz // 2
    left_side = z < middle
    inward = jnp.where(left_side, z + 1, z - 1)
    outward = jnp.where(left_side, z - 1, z + 1)
    is_middle = jnp.logical_or(z == middle - 1, z == middle)
    is_outer = jnp.logical_or(z == 0, z == nz - 1)
    spot = is_middle.astype(jnp.int32)

    def hc_copy(k):
        return remote(
            h_core.at[k], h_recv.at[k], hc_send.at[k], hc_recv.at[k], {"rep": other}
        )

    def hi_copy(k):
        return remote(
            h_send.at[k], h_side.at[spot, k], hi_send.at[k], hi_recv.at[spot, k],
            {"loop": inward},
        )

    def hi_wait(place, k):
        remote(
            h_send.at[k], h_side.at[place, k], hi_send.at[k], hi_recv.at[place, k],
            {"loop": inward},
        ).wait_recv()

    def ho_copy(k):
        slot = h_full.at[c, k]
        return remote(slot, slot, ho_send.at[k], hf_recv.at[c, k], {"loop": outward})

    def hf_copy(k):
        slot = h_full.at[c, k]
        return remote(slot, slot, hf_send.at[k], hf_recv.at[c, k], {"rep": other})

    for k in range(PARTS):
        part = lax.dot_general(
            e_all[z, c, x], f_own[:, k * width : (k + 1) * width], (((0,), (0,)), ((), ())),
            preferred_element_type=jnp.float32,
        )
        h_full_part = part.reshape(nc, half, width)

        @pl.when(c == 0)
        def _():
            h_own[k] = h_full_part[0]
            h_core[k] = h_full_part[1].astype(jnp.bfloat16)

        @pl.when(c == 1)
        def _():
            h_own[k] = h_full_part[1]
            h_core[k] = h_full_part[0].astype(jnp.bfloat16)

        hc_copy(k).start()

    for k in range(PARTS):
        hc_copy(k).wait_recv()
        h_own[k] = h_own[k] + h_recv[k].astype(jnp.float32)

        @pl.when(is_outer)
        def _():
            h_send[k] = h_own[k].astype(jnp.bfloat16)
            hi_copy(k).start()

    for k in range(PARTS):
        @pl.when(jnp.logical_not(is_outer))
        def _():
            hi_wait(0, k)
            h_send[k] = (h_own[k] + h_side[0, k].astype(jnp.float32)).astype(jnp.bfloat16)
            hi_copy(k).start()

    embed_out[...] = lax.dot_general(
        f_own[...], w_all[x].reshape(cols, feats), (((1,), (1,)), ((), ())), preferred_element_type=jnp.float32
    ).astype(jnp.bfloat16)

    for k in range(PARTS):
        @pl.when(is_middle)
        def _():
            hi_wait(1, k)
            h_full[c, k] = (
                h_send[k].astype(jnp.float32) + h_side[1, k].astype(jnp.float32)
            ).astype(jnp.bfloat16)

        @pl.when(jnp.logical_not(is_middle))
        def _():
            ho_copy(k).wait_recv()

        @pl.when(jnp.logical_not(is_outer))
        def _():
            ho_copy(k).start()

        hf_copy(k).start()

    for k in range(PARTS):
        slot = h_full.at[other, k]
        remote(slot, slot, hf_send.at[k], hf_recv.at[other, k], {"rep": other}).wait_recv()
    head_out[...] = h_full[...]

    @pl.loop(0, nz)
    def _(b):
        for h in range(CHUNKS):
            @pl.when(jnp.logical_and(b <= z, has_right))
            def _():
                z_copy(b, 0, h).wait_send()

            @pl.when(jnp.logical_and(b >= z, has_left))
            def _():
                z_copy(b, 1, h).wait_send()

            for j in range(nx - 1):
                x_copy(b, j, h).wait_send()
            for xx in range(nx):
                c_copy(b, xx, h).wait_send()

    for j in range(nx - 1):
        wx_copy(j).wait_send()
        for i in range(ng - 1):
            wy_copy(j, i).wait_send()
        for gg in range(ng):
            wc_copy(x_peer(j), c, gg).wait_send()
    for k in range(PARTS):
        hc_copy(k).wait_send()
        hi_copy(k).wait_send()
        hf_copy(k).wait_send()

        @pl.when(jnp.logical_not(is_outer))
        def _():
            ho_copy(k).wait_send()


def finish(embed_ref, head_ref, embed_out, head_out):
    cores, parts, half, width = head_ref.shape
    embed_out[...] = embed_ref[...]
    for cc in range(cores):
        for k in range(parts):
            head_out[cc * half : (cc + 1) * half, k * width : (k + 1) * width] = head_ref[
                cc, k
            ].astype(jnp.float32)


def ring_body(embeddings, head_weight, gp_weights, counts):
    nz, nx, nc, ng = (lax.axis_size(name) for name in ("loop", "enc", "rep", "groups"))
    rows, cols = embeddings.shape
    feats = head_weight.shape[1]
    half, width = cols // nc, feats // PARTS
    if half % (16 * ng):
        raise ValueError("head rows")
    gp_rows = gp_weights.reshape(-1, 128)
    vmem = pl.BlockSpec(memory_space=pltpu.VMEM)
    hbm = pl.BlockSpec(memory_space=pltpu.HBM)
    dma = pltpu.SemaphoreType.DMA
    embed_grad, head_sum = pl.pallas_call(
        functools.partial(kernel, (nz, nx, nc, ng)),
        out_shape=(
            jax.ShapeDtypeStruct((rows, cols), jnp.bfloat16),
            jax.ShapeDtypeStruct((nc, PARTS, half, width), jnp.bfloat16),
        ),
        in_specs=[hbm, hbm, hbm, hbm],
        out_specs=(vmem, vmem),
        scratch_shapes=[
            pltpu.VMEM(gp_rows.shape, jnp.float32),
            pltpu.SMEM(counts.shape, jnp.int32),
            pltpu.VMEM((nz, nc, nx, rows, cols), jnp.bfloat16),
            pltpu.VMEM((nx, nc, ng, half // ng, feats), jnp.bfloat16),
            pltpu.VMEM((rows, feats), jnp.bfloat16),
            pltpu.VMEM((rows, 1), jnp.float32),
            pltpu.VMEM((rows, feats), jnp.float32),
            pltpu.VMEM((rows, 1), jnp.float32),
            pltpu.VMEM((PARTS, half, width), jnp.float32),
            pltpu.VMEM((PARTS, half, width), jnp.bfloat16),
            pltpu.VMEM((PARTS, half, width), jnp.bfloat16),
            pltpu.VMEM((PARTS, half, width), jnp.bfloat16),
            pltpu.VMEM((2, PARTS, half, width), jnp.bfloat16),
            pltpu.VMEM((nc, PARTS, half, width), jnp.bfloat16),
            dma((nz, nc, nx, CHUNKS)),
            dma((2, nz, CHUNKS)),
            dma((nx - 1, nz, CHUNKS)),
            dma((nz, nx, CHUNKS)),
            dma((nx - 1,)),
            dma((nx, ng)),
            dma((nx - 1, max(ng - 1, 1))),
            dma((nx, ng)),
            dma((nx, ng)),
            dma((3 + nc * ng,)),
            dma((PARTS,)),
            dma((PARTS,)),
            dma((PARTS,)),
            dma((2, PARTS)),
            dma((PARTS,)),
            dma((PARTS,)),
            dma((nc, PARTS)),
        ],
        compiler_params=pltpu.CompilerParams(
            collective_id=0, has_side_effects=True, vmem_limit_bytes=VMEM_BYTES
        ),
    )(embeddings, head_weight, gp_rows, counts)
    return pl.pallas_call(
        finish,
        out_shape=(
            jax.ShapeDtypeStruct((rows, cols), jnp.bfloat16),
            jax.ShapeDtypeStruct((cols, feats), jnp.float32),
        ),
        in_specs=[vmem, vmem],
        out_specs=(vmem, vmem),
        compiler_params=pltpu.CompilerParams(vmem_limit_bytes=VMEM_BYTES),
    )(embed_grad, head_sum)


LINE = 4
PIECES = 4
STRIPS = 3
COLUMNS = 2


def line_kernel(
    emb_ref,
    head_ref,
    gp_hbm,
    counts_hbm,
    embed_out,
    own_out,
    peer_out,
    gp_ref,
    counts_ref,
    e_all,
    w_all,
    f_all,
    n_row,
    n_col,
    w_row,
    accum,
    quot,
    grads,
    early_sum,
    w_col,
    e_turned,
    in_sem,
    e_send,
    e_recv,
    w_send,
    w_recv,
    f_send,
    f_recv,
    n_send,
    n_recv,
    h_send,
    h_recv,
):
    nz, nc = LINE, 2
    z = lax.axis_index("loop")
    x = lax.axis_index("enc")
    c = lax.axis_index("rep")
    g = lax.axis_index("groups")
    rows, cols = e_all.shape[2:]
    piece = rows // PIECES
    quarter, feats = w_all.shape[3:]
    block = nc * rows
    lanes = gp_ref.shape[1]
    inward = jnp.where(z < nz // 2, 1, -1)
    is_end = jnp.logical_or(z == 0, z == nz - 1)
    is_mid = jnp.logical_not(is_end)
    near = z + inward
    outer = z - inward
    second = z + 2 * inward
    third = z + 3 * inward
    x_dev, c_dev, g_dev = {"enc": 1 - x}, {"rep": 1 - c}, {"groups": 1 - g}

    def remote(src, dst, send, recv, device):
        return pltpu.make_async_remote_copy(
            src_ref=src, dst_ref=dst, send_sem=send, recv_sem=recv,
            device_id=device, device_id_type=MESH_ID,
        )

    def e_copy(side, b, h, kind, device):
        slot = e_all.at[side, b, pl.ds(h * piece, piece)]
        return remote(slot, slot, e_send.at[kind, h], e_recv.at[side, b, h], device)

    def e_wait(side, b, h):
        e_copy(side, b, h, 0, x_dev).wait_recv()

    def w_copy(cc, gg, p, kind, device, side=1 - x):
        strip = quarter // STRIPS
        slot = w_all.at[side, cc, gg, pl.ds(p * strip, strip)]
        return remote(slot, slot, w_send.at[kind, p], w_recv.at[cc, gg, p], device)

    def f_copy(b, cc):
        slot = f_all.at[b, cc]
        return remote(slot, slot, f_send.at[b], f_recv.at[b], c_dev)

    def n_copy(b, cc):
        slot = n_row.at[b, cc]
        return remote(slot, slot, n_send.at[b], n_recv.at[b], c_dev)

    barrier = pltpu.get_barrier_semaphore()

    def greet(device):
        pl.semaphore_signal(barrier, 1, device_id=device, device_id_type=MESH_ID)

    greet(x_dev)
    greet(c_dev)
    greet(g_dev)
    greet({"loop": near})

    @pl.when(is_mid)
    def _():
        greet({"loop": outer})

    own_emb = pltpu.make_async_copy(emb_ref, e_all.at[x, z], in_sem.at[0])
    own_emb.start()
    loads = []
    for cc in range(nc):
        for gg in range(2):
            loads.append(
                pltpu.make_async_copy(
                    head_ref.at[pl.ds((cc * 2 + gg) * quarter, quarter)],
                    w_all.at[x, cc, gg],
                    in_sem.at[3 + cc * 2 + gg],
                )
            )
    loads.append(pltpu.make_async_copy(gp_hbm, gp_ref, in_sem.at[1]))
    loads.append(pltpu.make_async_copy(counts_hbm, counts_ref, in_sem.at[2]))
    for copy in loads:
        copy.start()

    own_emb.wait()
    for copy in loads[:4]:
        copy.wait()
    pl.semaphore_wait(barrier, 4 + is_mid.astype(jnp.int32))

    for p in range(STRIPS):
        w_copy(c, g, p, 0, x_dev, x).start()
    for h in range(PIECES):
        e_copy(x, z, h, 0, {"loop": near}).start()

    @pl.when(is_mid)
    def _():
        for h in range(4):
            e_copy(x, z, h, 1, {"loop": outer}).start()


    fourth = jnp.where(is_end, second, outer)
    last = jnp.where(is_end, third, second)
    half = rows // 2
    parts = [
        [(z, 0), (z, 1)],
        [(fourth, 0), (fourth, 1)],
        [(near, 0), (last, 0)],
        [(near, 1), (last, 1)],
    ]

    for copy in loads[4:]:
        copy.wait()
    accum[...] = jnp.zeros_like(accum)
    quot[...] = jnp.zeros_like(quot)
    inside = lax.broadcasted_iota(jnp.int32, (1, lanes), 1)
    for v in range(nz):
        for cc in range(nc):
            for k, (b, h) in enumerate(parts[v]):
                place = cc * rows + h * half
                held = gp_ref[pl.ds(b * (block // lanes) + place // lanes, 1), :]
                w_row[v, cc, :, k * half : (k + 1) * half] = jnp.where(
                    inside + place < counts_ref[b], held, 0.0
                )

    def eye():
        return lax.broadcasted_iota(jnp.int32, (rows, rows), 0) == lax.broadcasted_iota(
            jnp.int32, (rows, rows), 1
        )

    def taken(side, v):
        return jnp.concatenate(
            [e_all[side, b, h * half : (h + 1) * half] for b, h in parts[v]], axis=0
        )

    def early(b, places):
        made = jnp.dot(
            e_all[x, b], w_all[x].reshape(cols, feats), preferred_element_type=jnp.float32
        )
        for h, (v, k) in enumerate(places):
            own = slice(h * half, (h + 1) * half)
            early_sum[v, k * half : (k + 1) * half] = made[own]
            spot = v * rows + k * half
            e_turned[:, spot : spot + half] = e_all[x, b, own].T

    early(z, [(0, 0), (0, 1)])
    for v in range(nz):
        column = jnp.sum(jnp.where(eye(), w_row[v, c], 0.0), axis=1, keepdims=True)
        w_col[v] = jnp.broadcast_to(column, (rows, lanes))

    for p in range(STRIPS):
        w_copy(c, g, p, 0, x_dev, x).wait_send()
        if p == STRIPS - 1:
            for h in range(PIECES):
                e_copy(x, z, h, 2, x_dev).start()

    def x_strip(p):
        w_copy(c, g, p, 0, x_dev).wait_recv()
        w_copy(c, g, p, 1, g_dev).start()
        w_copy(c, g, p, 2, c_dev).start()

    def g_strip(p):
        w_copy(c, 1 - g, p, 1, g_dev).wait_recv()
        w_copy(c, 1 - g, p, 3, c_dev).start()

    @pl.when(is_mid)
    def _():
        for h in range(max(PIECES, STRIPS)):
            if h < STRIPS:
                x_strip(h)
            if h < PIECES:
                e_wait(x, outer, h)
                e_copy(x, outer, h, 3, {"loop": near}).start()
                e_wait(x, near, h)
                e_copy(x, near, h, 4, {"loop": outer}).start()
        early(near, [(2, 0), (3, 0)])
        for p in range(STRIPS):
            g_strip(p)
        for h in range(PIECES):
            e_wait(x, second, h)
            e_copy(x, second, h, 5, {"loop": outer}).start()
            e_copy(x, second, h, 6, x_dev).start()
        for h in range(PIECES):
            e_wait(1 - x, z, h)
            e_copy(1 - x, z, h, 7, {"loop": outer}).start()
            e_copy(1 - x, z, h, 8, {"loop": near}).start()

    @pl.when(is_end)
    def _():
        for p in range(STRIPS):
            x_strip(p)
        for h in range(PIECES):
            e_wait(x, near, h)
        early(near, [(2, 0), (3, 0)])
        for h in range(PIECES + 1):
            if h < PIECES:
                e_wait(1 - x, z, h)
                e_copy(1 - x, z, h, 3, {"loop": near}).start()
            if h < STRIPS:
                g_strip(h)
            if h > 0:
                e_wait(x, second, h - 1)
                e_copy(x, second, h - 1, 4, x_dev).start()

    for p in range(STRIPS):
        w_copy(1 - c, g, p, 2, c_dev).wait_recv()
        w_copy(1 - c, 1 - g, p, 3, c_dev).wait_recv()

    def features(v):
        total = early_sum[v] + jnp.dot(
            taken(1 - x, v), w_all[1 - x].reshape(cols, feats),
            preferred_element_type=jnp.float32,
        )
        held = total.astype(jnp.bfloat16)
        f_all[v, c] = held
        f_copy(v, c).start()
        return held

    def norms(v, held):
        wide = held.astype(jnp.float32)
        norm = jnp.sum(wide * wide, axis=1, keepdims=True)
        n_col[v] = jnp.broadcast_to(norm, (rows, lanes))
        n_row[v, c] = jnp.sum(jnp.where(eye(), norm, 0.0), axis=0, keepdims=True)
        n_copy(v, c).start()

    def scores_of(i, j):
        return lax.dot_general(
            f_all[i, c], f_all[j].reshape(block, feats), (((1,), (1,)), ((), ())),
            preferred_element_type=jnp.float32,
        )

    def wide_row(ref, j):
        return jnp.concatenate([ref[j, cc] for cc in range(nc)], axis=1)

    def pairs(i, j, scores):
        spread = block // lanes
        left = jnp.concatenate([n_col[i]] * spread, axis=1)
        both = left + wide_row(n_row, j)
        denom = (both - scores) + EPSILON
        scaled = wide_row(w_row, j) * (1.0 / (denom * denom))
        part = scaled * scores
        total = part[:, :lanes]
        for k in range(1, spread):
            total = total + part[:, k * lanes : (k + 1) * lanes]
        quot[i] += total
        return (both * scaled).astype(jnp.bfloat16)

    def finalize(i, carried):
        quotient = 2.0 * jnp.sum(quot[i], axis=1, keepdims=True)
        own_weight = jnp.concatenate([w_col[i]] * (feats // lanes), axis=1)
        grads[i] = (
            own_weight * (carried - f_all[i, c].astype(jnp.float32) * quotient)
        ).astype(jnp.bfloat16)

    def tiles(todo, final=False, between=None):
        scores = scores_of(*todo[0])
        if between is not None:
            norms(*between)
        for k, (i, j) in enumerate(todo):
            following = scores_of(*todo[k + 1]) if k + 1 < len(todo) else None
            weight = pairs(i, j, scores)
            carried = accum[i] + jnp.dot(
                weight, f_all[j].reshape(block, feats), preferred_element_type=jnp.float32
            )
            if final and j == nz - 1:
                finalize(i, carried)
            else:
                accum[i] = carried
            scores = following

    def third_pass(some):
        @pl.when(is_end)
        def _():
            for h in some:
                e_wait(x, third, h)
                e_copy(x, third, h, 5, x_dev).start()

    def quarter_of(k):
        return range(k * PIECES // 4, (k + 1) * PIECES // 4)

    def meet(v):
        f_copy(v, 1 - c).wait_recv()
        n_copy(v, 1 - c).wait_recv()

    norms(0, features(0))
    third_pass(quarter_of(0))
    early(fourth, [(1, 0), (1, 1)])
    meet(0)
    third_pass(quarter_of(1))
    tiles([(0, 0)])
    for h in range(PIECES):
        e_wait(1 - x, fourth, h)
    held = features(1)
    third_pass(quarter_of(2))
    tiles([(1, 0)], between=(1, held))
    third_pass(quarter_of(3))
    early(last, [(2, 1), (3, 1)])
    meet(1)
    tiles([(0, 1), (1, 1)])
    for v in (2, 3):
        start = (v - 2) * (PIECES // 2)
        for h in range(start, start + PIECES // 2):
            e_wait(1 - x, near, h)
            e_wait(1 - x, last, h)
        held = features(v)
        tiles([(v, j) for j in range(v)], between=(v, held))
        meet(v)
        tiles([(i, v) for i in range(v + 1)], v == 3)

    width = feats // COLUMNS

    def h_copy(k):
        return remote(
            own_out.at[k], peer_out.at[k], h_send.at[k], h_recv.at[k], c_dev
        )

    for k in range(COLUMNS):
        own_out[k] = jnp.dot(
            e_turned[...],
            grads[:, :, k * width : (k + 1) * width].reshape(nz * rows, width),
            preferred_element_type=jnp.float32,
        ).astype(jnp.bfloat16)
        h_copy(k).start()

    embed_out[...] = lax.dot_general(
        grads[0], w_all[x].reshape(cols, feats), (((1,), (1,)), ((), ())),
        preferred_element_type=jnp.float32,
    ).astype(jnp.bfloat16)

    for p in range(STRIPS):
        for kind, device in ((1, g_dev), (2, c_dev), (3, c_dev)):
            w_copy(c, g, p, kind, device).wait_send()
    for b in range(nz):
        f_copy(b, c).wait_send()
        n_copy(b, c).wait_send()
    for h in range(PIECES):
        for kind in (0, 2, 3, 4, 5):
            e_copy(x, z, h, kind, x_dev).wait_send()

        @pl.when(is_mid)
        def _():
            for kind in (1, 6, 7, 8):
                e_copy(x, z, h, kind, x_dev).wait_send()

    for k in range(COLUMNS):
        h_copy(k).wait()


def line_finish(embed_ref, own_ref, peer_ref, embed_out, head_out):
    parts, _, width = own_ref.shape
    embed_out[...] = embed_ref[...]
    for k in range(parts):
        head_out[:, k * width : (k + 1) * width] = own_ref[k].astype(
            jnp.float32
        ) + peer_ref[k].astype(jnp.float32)


def line_body(embeddings, head_weight, gp_weights, counts):
    nz, nc, nx, ng = LINE, 2, 2, 2
    rows, cols = embeddings.shape
    feats = head_weight.shape[1]
    quarter, width = cols // (nc * ng), feats // COLUMNS
    lanes = 128
    gp_rows = gp_weights.reshape(-1, lanes)
    vmem = pl.BlockSpec(memory_space=pltpu.VMEM)
    hbm = pl.BlockSpec(memory_space=pltpu.HBM)
    dma = pltpu.SemaphoreType.DMA
    part = pltpu.VMEM((COLUMNS, cols, width), jnp.bfloat16)
    embed_grad, own, peer = pl.pallas_call(
        line_kernel,
        out_shape=(pltpu.VMEM((rows, cols), jnp.bfloat16), part, part),
        in_specs=[hbm, hbm, hbm, hbm],
        out_specs=(vmem, vmem, vmem),
        scratch_shapes=[
            pltpu.VMEM(gp_rows.shape, jnp.float32),
            pltpu.SMEM(counts.shape, jnp.int32),
            pltpu.VMEM((nx, nz, rows, cols), jnp.bfloat16),
            pltpu.VMEM((nx, nc, ng, quarter, feats), jnp.bfloat16),
            pltpu.VMEM((nz, nc, rows, feats), jnp.bfloat16),
            pltpu.VMEM((nz, nc, 1, rows), jnp.float32),
            pltpu.VMEM((nz, rows, lanes), jnp.float32),
            pltpu.VMEM((nz, nc, 1, rows), jnp.float32),
            pltpu.VMEM((nz, rows, feats), jnp.float32),
            pltpu.VMEM((nz, rows, lanes), jnp.float32),
            pltpu.VMEM((nz, rows, feats), jnp.bfloat16),
            pltpu.VMEM((nz, rows, feats), jnp.float32),
            pltpu.VMEM((nz, rows, lanes), jnp.float32),
            pltpu.VMEM((cols, nz * rows), jnp.bfloat16),
            dma((3 + nc * ng,)),
            dma((9, PIECES)),
            dma((nx, nz, PIECES)),
            dma((4, STRIPS)),
            dma((nc, ng, STRIPS)),
            dma((nz,)),
            dma((nz,)),
            dma((nz,)),
            dma((nz,)),
            dma((COLUMNS,)),
            dma((COLUMNS,)),
        ],
        compiler_params=pltpu.CompilerParams(
            collective_id=0, has_side_effects=True, vmem_limit_bytes=VMEM_BYTES
        ),
    )(embeddings, head_weight, gp_rows, counts)
    embed_grad, own, peer = (
        pltpu.with_memory_space_constraint(held, pltpu.VMEM)
        for held in (embed_grad, own, peer)
    )
    return pl.pallas_call(
        line_finish,
        out_shape=(
            jax.ShapeDtypeStruct((rows, cols), jnp.bfloat16),
            jax.ShapeDtypeStruct((cols, feats), jnp.float32),
        ),
        in_specs=[vmem, vmem, vmem],
        out_specs=(vmem, vmem),
        compiler_params=pltpu.CompilerParams(vmem_limit_bytes=VMEM_BYTES),
    )(embed_grad, own, peer)


def body(*args):
    sizes = tuple(lax.axis_size(name) for name in ("loop", "enc", "rep", "groups"))
    return line_body(*args) if sizes == (LINE, 2, 2, 2) else ring_body(*args)


def solution(mesh):
    placed = (P(("groups", "loop", "rep"), "enc"), P("enc", None), P("groups"), P("groups"))
    return jax.shard_map(
        body,
        mesh=mesh,
        in_specs=placed,
        out_specs=(P(("groups", "loop", "rep"), "enc"), P(("groups", "enc"), None)),
        check_vma=False,
    )
```
